128 devices in a mesh: fsdp: 128 (over x, y, z, core).
Axes of the slice: x: 4, y: 4, z: 4, core: 2. Of those that a mesh axis runs over, the one named last changes fastest.
Arguments:
- tokens: bfloat16 [49152, 768], P('fsdp'), may hold values from -6 to 6
- cotangent: bfloat16 [49152, 768], P('fsdp'), may hold values from -6 to 6
- segments: int32 [49152], P('fsdp'), may hold values from 0 to 47, as said below
- counts: int32 [128], P('fsdp'), may hold values from 96 to 384, as said below
- norm_gain: bfloat16 [2, 768], P(None, 'fsdp'), may hold values from 0.5 to 1.5
- in_weight: bfloat16 [2, 768, 3352], P(None, 'fsdp'), may hold values from -0.21875 to 0.21875
- conv_weight: bfloat16 [2, 1792, 4], P(None, 'fsdp'), may hold values from -3 to 3
- conv_bias: bfloat16 [2, 1792], P(None, 'fsdp'), may hold values from -2 to 2
- a_log: float32 [2, 24], replicated, may hold values from 0 to 2.77
- dt_bias: float32 [2, 24], replicated, may hold values from -4 to -1
- skip: float32 [2, 24], replicated, may hold values from 0.5 to 2
- gate_gain: bfloat16 [2, 1536], P(None, 'fsdp'), may hold values from 0.5 to 1.5
- out_weight: bfloat16 [2, 1536, 768], P(None, None, 'fsdp'), may hold values from -0.15625 to 0.15625
Outputs:
- output: bfloat16 [49152, 768], P('fsdp')
- tokens_grad: bfloat16 [49152, 768], P('fsdp')
- norm_gain_grad: float32 [2, 768], P(None, 'fsdp')
- in_weight_grad: float32 [2, 768, 3352], P(None, 'fsdp')
- conv_weight_grad: float32 [2, 1792, 4], P(None, 'fsdp')
- conv_bias_grad: float32 [2, 1792], P(None, 'fsdp')
- a_log_grad: float32 [2, 24], replicated
- dt_bias_grad: float32 [2, 24], replicated
- skip_grad: float32 [2, 24], replicated
- gate_gain_grad: float32 [2, 1536], P(None, 'fsdp')
- out_weight_grad: float32 [2, 1536, 768], P(None, None, 'fsdp')
The draws below stay inside these ranges and needn't reach their ends.
Inputs may be any that keep to these rules, and one draw needn't show every extreme that they name: `segments`: within each pack of 384 slots the numbers start at 0 and never fall; in every draw some pack holds one single sequence over all its 384 slots, and that pack is wholly live. `counts`: between a quarter and three quarters of a pack's slots are live, except that one or more packs are wholly live in every draw.
All inputs are finite; a program needn't handle non-finite values.
Results may differ from the reference program's by a relative error of at most 0.011.
Values may be sent and summed in bfloat16 or wider, within the bound.
A program may use at most 192 MiB of HBM per device.

```python
import jax
import jax.numpy as jnp
from jax import lax

D = 768
HEADS = 24
HEAD_DIM = 64
STATE = 128
KERNEL = 4
LAYERS = 2
TOK_DEV = 384
INNER = 1536
CONV_DIM = 1792
PROJ = 3352
TOKENS = 49152
N_FSDP = 128


def chosen_pack(key):
    return jax.random.randint(jax.random.fold_in(key, 11), (), 0, N_FSDP)


def draw_segments(key, part):
    whole_pack = chosen_pack(key)
    even_pack = (whole_pack + N_FSDP // 2) % N_FSDP
    key = jax.random.fold_in(key, 1)
    starts = (jax.random.randint(key, (N_FSDP, TOK_DEV), 0, 48) == 0).astype(jnp.int32)
    starts = starts.at[:, 0].set(0)
    numbers = jnp.minimum(jnp.cumsum(starts, axis=1), TOK_DEV // 8 - 1).astype(jnp.int32)
    packs = jnp.arange(N_FSDP, dtype=jnp.int32)[:, None]
    slots = jnp.arange(TOK_DEV, dtype=jnp.int32)[None, :]
    numbers = jnp.where(packs == even_pack, slots // 8, numbers).astype(jnp.int32)
    numbers = jnp.where(packs == whole_pack, 0, numbers).astype(jnp.int32)
    return numbers.reshape(TOKENS)


def draw_counts(key, part):
    whole_pack = chosen_pack(key)
    even_pack = (whole_pack + N_FSDP // 2) % N_FSDP
    key = jax.random.fold_in(key, 2)
    amounts = jax.random.randint(key, (N_FSDP,), TOK_DEV // 4, 3 * TOK_DEV // 4 + 1)
    packs = jnp.arange(N_FSDP, dtype=jnp.int32)
    amounts = jnp.where(packs == even_pack, TOK_DEV // 4, amounts)
    return jnp.where(packs == whole_pack, TOK_DEV, amounts).astype(jnp.int32)


def steps_of(rng, extent, cuts, least, top_value):
    level = 1.0
    for dim, parts in cuts:
        heights = jax.random.uniform(jax.random.fold_in(jax.random.fold_in(rng, 6), dim), (parts,), jnp.float32, least / len(cuts), top_value / len(cuts))
        level = level * jnp.repeat(jnp.exp(heights), extent[dim] // parts).reshape((-1,) + (1,) * (len(extent) - 1 - dim))
    return level


def gaussian(key, extent, spread, most, shards=(), held_as=jnp.bfloat16):
    values = jax.random.normal(key, extent, jnp.float32) * spread
    if len(shards) > 0:
        values = steps_of(key, extent, shards, -0.22, 0.18) * values
    return jnp.clip(values, min=-most, max=most).astype(held_as)


def setup_inputs(seed: int = 0) -> dict:
    key_list = jax.random.split(jax.random.key(seed), 14)
    tokens = gaussian(key_list[0], (TOKENS, D), 1.0, 6.0, ((0, 128),))
    cotangent = gaussian(key_list[1], (TOKENS, D), 1.0, 6.0, ((0, 128),))
    segments = draw_segments(jax.random.fold_in(key_list[13], 71), 0)
    counts = draw_counts(jax.random.fold_in(key_list[13], 71), 0)
    norm_gain = jnp.clip(0.5 + 1.0 * jax.random.uniform(key_list[4], (LAYERS, D), jnp.float32) ** steps_of(key_list[4], (LAYERS, D), ((1, 128),), -0.2, 0.2), 0.5, 1.5).astype(jnp.bfloat16)
    in_weight = gaussian(key_list[5], (LAYERS, D, PROJ), D ** -0.5, 0.21875, ((1, 128),))
    conv_weight = gaussian(key_list[6], (LAYERS, CONV_DIM, KERNEL), KERNEL ** -0.5, 3.0, ((1, 128),))
    conv_bias = gaussian(key_list[7], (LAYERS, CONV_DIM), 0.3, 2.0, ((1, 128),))
    a_log = jnp.clip(jax.random.uniform(key_list[8], (LAYERS, HEADS), jnp.float32, 0.0, 2.77), 0.0, 2.77)
    dt_bias = jnp.clip(jax.random.uniform(key_list[9], (LAYERS, HEADS), jnp.float32, -4.0, -1.0), -4.0, -1.0)
    skip = jnp.clip(jax.random.uniform(key_list[10], (LAYERS, HEADS), jnp.float32, 0.5, 2.0), 0.5, 2.0)
    gate_gain = jnp.clip(0.5 + 1.0 * jax.random.uniform(key_list[11], (LAYERS, INNER), jnp.float32) ** steps_of(key_list[11], (LAYERS, INNER), ((1, 128),), -0.2, 0.2), 0.5, 1.5).astype(jnp.bfloat16)
    out_weight = gaussian(key_list[12], (LAYERS, INNER, D), INNER ** -0.5, 0.15625, ((2, 128),))
    return dict(tokens=tokens, cotangent=cotangent, segments=segments, counts=counts, norm_gain=norm_gain, in_weight=in_weight, conv_weight=conv_weight, conv_bias=conv_bias, a_log=a_log, dt_bias=dt_bias, skip=skip, gate_gain=gate_gain, out_weight=out_weight)


epsilon = 1e-05
highest = lax.Precision.HIGHEST
pack_group = 4

@jax.custom_vjp
def low(v):
    return lax.optimization_barrier(v.astype(jnp.bfloat16)).astype(jnp.float32)

@jax.custom_vjp
def low_back(v):
    return v

def low_keep(v):
    return (low(v), None)

def low_pass(kept, grad):
    return (grad,)

def back_keep(v):
    return (v, None)

def back_low(kept, grad):
    return (low(grad),)
low.defvjp(low_keep, low_pass)
low_back.defvjp(back_keep, back_low)

def rms_norm(values, gain):
    return values * lax.rsqrt(lax.optimization_barrier(jnp.mean(values * values, axis=-1, keepdims=True)) + epsilon) * gain

def mixer(segment_ids, projected, params):
    conv_taps, conv_offset, decay_log, step_bias, direct, gated_gain = params
    length = projected.shape[0]
    gate_part = projected[:, :INNER]
    conv_input = projected[:, INNER:INNER + CONV_DIM]
    step_raw = projected[:, INNER + CONV_DIM:]
    convolved = conv_offset + conv_input * conv_taps[:, KERNEL - 1]
    for offset in range(1, KERNEL):
        earlier = jnp.concatenate([jnp.zeros((offset, CONV_DIM), jnp.float32), conv_input[:length - offset]], axis=0)
        earlier_ids = jnp.concatenate([jnp.full((offset,), -1, jnp.int32), segment_ids[:length - offset]])
        convolved = convolved + jnp.where((earlier_ids == segment_ids)[:, None], earlier, 0.0) * conv_taps[:, KERNEL - 1 - offset]
    activated = jax.nn.silu(convolved)
    head_values = activated[:, :INNER].reshape(length, HEADS, HEAD_DIM)
    inputs_b = activated[:, INNER:INNER + STATE]
    outputs_c = activated[:, INNER + STATE:]
    step_size = jax.nn.softplus(step_raw + step_bias)
    log_decay = jnp.cumsum(step_size * -jnp.exp(decay_log), axis=0)
    positions = jnp.arange(length, dtype=jnp.int32)
    linked = (segment_ids[:, None] == segment_ids[None, :]) & (positions[:, None] >= positions[None, :])
    decay = jnp.exp(jnp.where(linked[:, :, None], log_decay[:, None, :] - log_decay[None, :, :], -10000.0))
    scores = jnp.dot(outputs_c, inputs_b.T, precision=highest)
    weighting = scores[:, :, None] * decay * step_size[None, :, :]
    mixed = jnp.einsum('tsh,shp->thp', weighting, head_values, precision=highest) + direct[None, :, None] * head_values
    gated = mixed.reshape(length, INNER) * jax.nn.silu(gate_part)
    return rms_norm(gated, gated_gain)

def block(stream, segment_ids, weights):
    first_gain, proj_in, conv_taps, conv_offset, decay_log, step_bias, direct, gated_gain, proj_out = weights
    normed = low(rms_norm(stream, first_gain))
    projected = low_back(jnp.dot(normed.reshape(-1, D), proj_in, precision=highest))
    projected = projected.reshape(stream.shape[0], stream.shape[1], PROJ)
    small = (conv_taps, conv_offset, decay_log, step_bias, direct, gated_gain)
    mixed = low(jax.vmap(mixer, in_axes=(0, 0, None))(segment_ids, projected, small))
    branch = low_back(jnp.dot(mixed.reshape(-1, INNER), proj_out, precision=highest))
    return stream + branch.reshape(stream.shape)

def network(stream, segment_ids, live_rows, params):
    for layer_index in range(LAYERS):
        stream = block(stream, segment_ids, tuple((weight[layer_index] for weight in params)))
    return stream * live_rows

def reference(tokens, cotangent, segments, counts, norm_gain, in_weight, conv_weight, conv_bias, a_log, dt_bias, skip, gate_gain, out_weight):
    params = tuple((weight.astype(jnp.float32) for weight in (norm_gain, in_weight, conv_weight, conv_bias, a_log, dt_bias, skip, gate_gain, out_weight)))
    groups = N_FSDP // pack_group
    inputs = tokens.astype(jnp.float32).reshape(groups, pack_group, TOK_DEV, D)
    cotan = cotangent.astype(jnp.float32).reshape(groups, pack_group, TOK_DEV, D)
    seg_ids = segments.reshape(groups, pack_group, TOK_DEV)
    positions = jnp.arange(TOK_DEV, dtype=jnp.int32)
    live_rows = (positions[None, :] < counts[:, None]).astype(jnp.float32).reshape(groups, pack_group, TOK_DEV, 1)

    def one_group(totals, pieces):
        stream, cot_piece, seg_piece, live_piece = pieces

        def forward(values, weights):
            return network(values, seg_piece, live_piece, weights)
        result, pullback = jax.vjp(forward, stream, params)
        input_grad, param_grads = pullback(cot_piece)
        totals = jax.tree.map(lambda left, right: left + right, totals, param_grads)
        return (totals, (result, input_grad))
    zeros = jax.tree.map(jnp.zeros_like, params)
    totals, (result, input_grad) = lax.scan(one_group, zeros, (inputs, cotan, seg_ids, live_rows))
    output = result.reshape(TOKENS, D).astype(jnp.bfloat16)
    tokens_grad = input_grad.reshape(TOKENS, D).astype(jnp.bfloat16)
    return (output, tokens_grad, totals[0], totals[1], totals[2], totals[3], totals[4], totals[5], totals[6], totals[7], totals[8])
```

```python
from functools import partial

import jax
import jax.numpy as jnp
from jax import lax
from jax.experimental import pallas as pl
from jax.experimental.pallas import tpu as pltpu
from jax.sharding import PartitionSpec as P

D = 768
HEADS = 24
STATE = 128
INNER = 1536
CONV = 1792
T = 384
GC = 3328
OUT0 = 3328
STEP0 = 4864
WIDE = 4992
PROJW = 3456
EPS = 1e-05
F32 = jnp.float32
BF = jnp.bfloat16


def nn(a, b):
    return lax.dot_general(a, b, (((1,), (0,)), ((), ())), preferred_element_type=F32)


def nt(a, b):
    return lax.dot_general(a, b, (((1,), (1,)), ((), ())), preferred_element_type=F32)


def tn(a, b):
    return lax.dot_general(a, b, (((0,), (0,)), ((), ())), preferred_element_type=F32)


def iota(shape, dim):
    return lax.broadcasted_iota(jnp.int32, shape, dim)


def ones_where(cond):
    return jnp.where(cond, 1.0, 0.0)


def cols_at(start, width):
    if isinstance(start, int):
        return pl.ds(start, width)
    return pl.ds(pl.multiple_of(start, 128), width)


def sigmoid(v):
    return 1.0 / (1.0 + jnp.exp(-v))


def pack3(v):
    hi = v.astype(BF).astype(F32)
    rest = v - hi
    mid = rest.astype(BF).astype(F32)
    low = rest - mid
    return (hi + pltpu.roll(mid, 32, 1) + pltpu.roll(low, 64, 1)).astype(BF)


def unpack3(v):
    return v + pltpu.roll(v, 96, 1) + pltpu.roll(v, 64, 1)


def head_mask(shape=(T, 128)):
    return iota(shape, 1) < HEADS


def spread_matrix(j, width, shift):
    return ones_where((iota((128, width), 0) & 31) == 4 * j + (iota((128, width), 1) >> shift)).astype(BF)


def rms_normed(stream, gain):
    r = lax.rsqrt(jnp.mean(stream * stream, axis=-1, keepdims=True) + EPS)
    return stream * r * gain


def step_terms(raw, heads_ref):
    mask = head_mask()
    rate = -jnp.exp(heads_ref[0:1, :])
    x = raw + heads_ref[1:2, :]
    x = jnp.where(mask, x, 0.0)
    step = jnp.where(mask, jnp.maximum(x, 0.0) + jnp.log1p(jnp.exp(-jnp.abs(x))), 0.0)
    return rate, x, step


def prepare_scan(raw, heads_ref, step3, log3, log_t):
    rate, x, step = step_terms(raw, heads_ref)
    lower = ones_where(iota((T, T), 0) >= iota((T, T), 1)).astype(BF)
    total = unpack3(nn(lower, pack3(jnp.where(head_mask(), step * rate, 0.0))))
    total = jnp.where(head_mask(), total, 0.0)
    step3[...] = pack3(step)
    log3[...] = pack3(total)
    flipped = jnp.transpose(total)
    for h in range(HEADS):
        log_t[h] = flipped[h : h + 1]
    return rate, x, step


def conv_pass(proj_ref, rows_ref, cols_ref, act_ref):
    masks = [ones_where(cols_ref[:, k : k + 1] == cols_ref[:, 0:1]) for k in range(1, 4)]

    def body(c, carry):
        ci = proj_ref[:, cols_at(INNER + c * 128, 128)]
        here = cols_at(c * 128, 128)
        total = rows_ref[0:1, here] + ci * rows_ref[4:5, here]
        for k in range(1, 4):
            total = total + pltpu.roll(ci, k, 0) * masks[k - 1] * rows_ref[4 - k : 5 - k, here]
        act_ref[:, here] = total * sigmoid(total)
        return carry

    lax.fori_loop(0, 14, body, 0)


def score_pass(act_ref, cols_ref, seg_row_ref, scores, scores_low):
    b = act_ref[:, INNER : INNER + STATE]
    c = act_ref[:, INNER + STATE :]
    s = lax.dot_general(c, b, (((1,), (1,)), ((), ())), precision=lax.Precision.HIGHEST, preferred_element_type=F32)
    linked = (cols_ref[:, 0:1] == seg_row_ref[0:1, :]) & (iota((T, T), 0) >= iota((T, T), 1))
    s = jnp.where(linked, s, 0.0)
    scores[...] = s
    scores_low[...] = s.astype(BF)


def lane_heads(q):
    return (iota((128, 256), 1) >> 6) == q


def block_rows(i):
    return slice(128 * i, 128 * (i + 1))


def scan_chunk_terms(j, act_ref, step3, log3, heads_skip, scores):
    here = cols_at(j * 256, 256)
    x = act_ref[:, here]
    spread = spread_matrix(j, 256, 6)
    step_e = nn(step3[...], spread)
    log_e = nn(log3[...], spread)
    wide = nn(log3[...], spread_matrix(j, 512, 7))
    xd = x * step_e
    return x, step_e, log_e, wide, xd


def decays(i, j, wide, log_t):
    out = []
    for q in range(4):
        row = log_t[4 * j + q, :, block_rows(i)]
        out.append(jnp.exp(jnp.minimum(wide[block_rows(i), 128 * q : 128 * (q + 1)] - row, 0.0)))
    return out


def fwd_kernel(stream_ref, w_ref, rows_ref, heads_ref, skip_ref, cols_ref, seg_row_ref,
               next_ref, proj_ref, mixed_ref, normed_ref,
               act_ref, scores, scores_low, step3, log3, log_t, gated, square, yn):
    normed_ref[...] = rms_normed(stream_ref[...], rows_ref[6:7, 0:D]).astype(BF)

    def project(c, carry):
        here = cols_at(c * 256, 256)
        proj_ref[:, here] = nn(normed_ref[...], w_ref[:, here])
        return carry

    lax.fori_loop(0, 13, project, 0)
    proj_ref[:, GC:] = nn(normed_ref[...], w_ref[:, STEP0:])
    prepare_scan(proj_ref[:, GC:], heads_ref, step3, log3, log_t)
    conv_pass(proj_ref, rows_ref, cols_ref, act_ref)
    score_pass(act_ref, cols_ref, seg_row_ref, scores, scores_low)
    square[...] = jnp.zeros_like(square)

    def chunk(j, carry):
        here = cols_at(j * 256, 256)
        x, step_e, log_e, wide, xd = scan_chunk_terms(j, act_ref, step3, log3, None, scores)
        xd_low = xd.astype(BF)
        for i in range(3):
            rows = block_rows(i)
            sc = scores[rows, rows]
            left = jnp.concatenate([(sc * e).astype(BF) for e in decays(i, j, wide, log_t)], axis=1)
            part = xd_low[rows]
            right = jnp.concatenate([jnp.where(lane_heads(q), part, 0) for q in range(4)], axis=0)
            y = nn(left, right)
            if i:
                edge = log_e[128 * i - 1 : 128 * i, :]
                before = slice(0, 128 * i)
                carried = (xd[before] * jnp.exp(jnp.minimum(edge - log_e[before], 0.0))).astype(BF)
                y = y + jnp.exp(jnp.minimum(log_e[rows] - edge, 0.0)) * nn(scores_low[rows, before], carried)
            mixed = y + skip_ref[0:1, here] * x[rows]
            mixed_ref[rows, here] = mixed
            gate = proj_ref[rows, here]
            u = mixed * (gate * sigmoid(gate))
            gated[rows, here] = u
            uu = u * u
            square[rows, :] += uu[:, :128] + uu[:, 128:]
        return carry

    lax.fori_loop(0, 6, chunk, 0)
    r = lax.rsqrt(jnp.sum(square[...], axis=-1, keepdims=True) * (1.0 / INNER) + EPS)

    def gain(c, carry):
        here = cols_at(c * 256, 256)
        yn[:, here] = (gated[:, here] * r * rows_ref[5:6, here]).astype(BF)
        return carry

    lax.fori_loop(0, 6, gain, 0)
    for n in range(3):
        there = slice(256 * n, 256 * (n + 1))
        next_ref[:, there] = stream_ref[:, there] + nt(yn[...], w_ref[there, OUT0:STEP0])


def bwd_kernel(grad_ref, stream_ref, normed_ref, proj_ref, mixed_ref, w_ref, rows_ref, heads_ref, skip_ref, cols_ref, seg_row_ref,
               prev_ref, g_ref, small_ref,
               act_ref, scores, scores_low, step3, log3, log_t, dyn, dact, dproj, dscores, dlog, dstep, gl, gl_t, sum_u, sum_d, row_skip):
    gl[...] = grad_ref[...].astype(BF)
    gl_t[...] = jnp.transpose(gl[...])
    small_ref[...] = jnp.zeros_like(small_ref)
    sum_u[...] = jnp.zeros_like(sum_u)
    sum_d[...] = jnp.zeros_like(sum_d)
    dscores[...] = jnp.zeros_like(dscores)
    dlog[...] = jnp.zeros_like(dlog)
    dstep[...] = jnp.zeros_like(dstep)

    def first(c, carry):
        here = cols_at(c * 256, 256)
        dy = nn(gl[...], w_ref[:, cols_at(OUT0 + c * 256, 256)])
        dyn[:, here] = dy
        gate = proj_ref[:, here]
        u = mixed_ref[:, here] * (gate * sigmoid(gate))
        uu = u * u
        ud = u * dy * rows_ref[5:6, here]
        sum_u[...] += uu[:, :128] + uu[:, 128:]
        sum_d[...] += ud[:, :128] + ud[:, 128:]
        return carry

    lax.fori_loop(0, 6, first, 0)
    rate, xstep, step = prepare_scan(proj_ref[:, GC:], heads_ref, step3, log3, log_t)
    conv_pass(proj_ref, rows_ref, cols_ref, act_ref)
    score_pass(act_ref, cols_ref, seg_row_ref, scores, scores_low)
    r = lax.rsqrt(jnp.sum(sum_u[...], axis=-1, keepdims=True) * (1.0 / INNER) + EPS)
    pull = r * r * r * (jnp.sum(sum_d[...], axis=-1, keepdims=True) * (1.0 / INNER))
    sum_u[...] = jnp.broadcast_to(r, (T, 128))
    sum_d[...] = jnp.broadcast_to(pull, (T, 128))

    def chunk(j, carry):
        here = cols_at(j * 256, 256)
        r = sum_u[:, 0:1]
        pull = sum_d[:, 0:1]
        x, step_e, log_e, wide, xd = scan_chunk_terms(j, act_ref, step3, log3, None, scores)
        xd_low = xd.astype(BF)
        dy = dyn[:, here]
        gate = proj_ref[:, here]
        mixed = mixed_ref[:, here]
        sg = sigmoid(gate)
        silu = gate * sg
        gain = rows_ref[5:6, here]
        u = mixed * silu
        ur = u * r
        small_ref[5:6, here] = jnp.sum(dy * ur, axis=0, keepdims=True)
        yn = (ur * gain).astype(BF)
        g_ref[:, cols_at(OUT0 + j * 256, 256)] = nn(gl_t[...], yn).astype(BF)
        du = r * (gain * dy) - u * pull
        dproj[:, here] = (du * mixed * (sg * (1.0 + gate * (1.0 - sg)))).astype(BF)
        dm = du * silu
        row_skip[0:1, here] = jnp.sum(dm * x, axis=0, keepdims=True)
        dm_low = dm.astype(BF)
        v_parts, dxd_parts = [], []
        for i in range(3):
            rows = block_rows(i)
            sc = scores[rows, rows]
            es = decays(i, j, wide, log_t)
            ws = [(sc * e).astype(BF) for e in es]
            part, dpart = xd_low[rows], dm_low[rows]
            right = jnp.concatenate([jnp.where(lane_heads(q), part, 0) for q in range(4)], axis=0)
            dright = jnp.concatenate([jnp.where(lane_heads(q), dpart, 0) for q in range(4)], axis=0)
            y = nn(jnp.concatenate(ws, axis=1), right)
            dxd = tn(jnp.concatenate(ws, axis=0), dright)
            g = nt(dright, part)
            ds = g[0:128] * es[0]
            for q in range(1, 4):
                ds = ds + g[128 * q : 128 * (q + 1)] * es[q]
            dscores[rows, rows] += ds
            v_parts.append(dpart.astype(F32) * y - part.astype(F32) * dxd)
            dxd_parts.append(dxd)
        for i in range(1, 3):
            rows = block_rows(i)
            before = slice(0, 128 * i)
            edge = log_e[128 * i - 1 : 128 * i, :]
            fade = jnp.exp(jnp.minimum(edge - log_e[before], 0.0))
            carried = (xd[before] * fade).astype(BF)
            de = (dm[rows] * jnp.exp(jnp.minimum(log_e[rows] - edge, 0.0))).astype(BF)
            z = nn(scores_low[rows, before], carried)
            dz = tn(scores_low[rows, before], de)
            dscores[rows, before] += nt(de, carried)
            v_parts[i] = v_parts[i] + de.astype(F32) * z
            back = carried.astype(F32) * dz
            faded = fade * dz
            for k in range(i):
                v_parts[k] = v_parts[k] - back[block_rows(k)]
                dxd_parts[k] = dxd_parts[k] + faded[block_rows(k)]
        v = jnp.concatenate(v_parts, axis=0)
        dxd = jnp.concatenate(dxd_parts, axis=0)
        dact[:, here] = step_e * dxd + skip_ref[0:1, here] * dm
        gather = ones_where(4 * j + ((iota((512, 128), 0) & 255) >> 6) == iota((512, 128), 1)).astype(BF)

        def head_sums(a):
            hi = a.astype(BF)
            return nn(jnp.concatenate([hi, (a - hi.astype(F32)).astype(BF)], axis=1), gather)

        dlog[...] += head_sums(v)
        dstep[...] += head_sums(x * dxd)
        return carry

    lax.fori_loop(0, 6, chunk, 0)

    linked = (cols_ref[:, 0:1] == seg_row_ref[0:1, :]) & (iota((T, T), 0) >= iota((T, T), 1))
    ds = jnp.where(linked, dscores[...], 0.0).astype(BF)
    b = act_ref[:, INNER : INNER + STATE].astype(BF)
    c = act_ref[:, INNER + STATE :].astype(BF)
    dact[:, INNER : INNER + STATE] = tn(ds, c)
    dact[:, INNER + STATE :] = nn(ds, b)

    upper = ones_where(iota((T, T), 0) <= iota((T, T), 1)).astype(BF)
    dsum = unpack3(nn(upper, pack3(dlog[...])))
    dsum = jnp.where(head_mask(), dsum, 0.0)
    dx = (dstep[...] + rate * dsum) * sigmoid(xstep)
    dx = jnp.where(head_mask(), dx, 0.0)
    dproj[:, GC:] = dx.astype(BF)
    small_ref[7:8, 0:128] = jnp.sum(dsum * step, axis=0, keepdims=True) * jnp.where(head_mask((1, 128)), rate, 0.0)
    small_ref[7:8, 128:256] = jnp.sum(dx, axis=0, keepdims=True)
    which = ones_where((iota((INNER, 128), 0) >> 6) == iota((INNER, 128), 1))
    small_ref[7:8, 256:384] = lax.dot_general(jnp.broadcast_to(row_skip[0:1, :], (8, INNER)), which, (((1,), (0,)), ((), ())),
                                              precision=lax.Precision.HIGHEST, preferred_element_type=F32)[0:1]

    def conv_back(c, carry):
        ci = proj_ref[:, cols_at(INNER + c * 128, 128)]
        here = cols_at(c * 128, 128)
        taps = [rows_ref[4 - k : 5 - k, here] for k in range(4)]
        masks = [ones_where(cols_ref[:, k : k + 1] == cols_ref[:, 0:1]) for k in range(1, 7)]
        shifted = [ci] + [pltpu.roll(ci, k, 0) * masks[k - 1] for k in range(1, 4)]
        total = rows_ref[0:1, here] + ci * taps[0]
        for k in range(1, 4):
            total = total + shifted[k] * taps[k]
        sg = sigmoid(total)
        dc = dact[:, here] * (sg * (1.0 + total * (1.0 - sg)))
        small_ref[0:1, here] = jnp.sum(dc, axis=0, keepdims=True)
        dci = dc * taps[0]
        for k in range(4):
            small_ref[4 - k : 5 - k, here] = jnp.sum(dc * shifted[k], axis=0, keepdims=True)
            if k:
                dci = dci + pltpu.roll(dc, T - k, 0) * masks[k + 2] * taps[k]
        dproj[:, cols_at(INNER + c * 128, 128)] = dci.astype(BF)
        return carry

    lax.fori_loop(0, 14, conv_back, 0)

    gl_t[...] = jnp.transpose(normed_ref[...])

    def in_grad(c, carry):
        here = cols_at(c * 256, 256)
        g_ref[:, here] = nn(gl_t[...], dproj[:, here]).astype(BF)
        return carry

    lax.fori_loop(0, 13, in_grad, 0)
    g_ref[:, STEP0:] = nn(gl_t[...], dproj[:, GC:]).astype(BF)
    for n in range(3):
        there = slice(256 * n, 256 * (n + 1))
        dyn[:, there] = nt(dproj[:, :GC], w_ref[there, :GC]) + nt(dproj[:, GC:], w_ref[there, STEP0:])
    dn = dyn[:, 0:D]
    stream = stream_ref[...]
    gain = rows_ref[6:7, 0:D]
    r = lax.rsqrt(jnp.mean(stream * stream, axis=-1, keepdims=True) + EPS)
    small_ref[6:7, 0:D] = jnp.sum(dn * stream * r, axis=0, keepdims=True)
    gd = gain * dn
    prev_ref[...] = grad_ref[...] + r * gd - stream * (r * r * r * jnp.mean(stream * gd, axis=-1, keepdims=True))


def vm(count):
    return [pl.BlockSpec(memory_space=pltpu.VMEM)] * count


PARAMS = dict(vmem_limit_bytes=60 * 1024 * 1024)


def scan_scratch():
    return [
        pltpu.VMEM((T, CONV), F32),
        pltpu.VMEM((T, T), F32),
        pltpu.VMEM((T, T), BF),
        pltpu.VMEM((T, 128), BF),
        pltpu.VMEM((T, 128), BF),
        pltpu.VMEM((HEADS, 1, T), F32),
    ]


def layer_forward(stream, w, rows, heads, skip, cols, seg_row):
    return pl.pallas_call(
        fwd_kernel,
        out_shape=(
            jax.ShapeDtypeStruct((T, D), F32),
            jax.ShapeDtypeStruct((T, PROJW), F32),
            jax.ShapeDtypeStruct((T, INNER), F32),
            jax.ShapeDtypeStruct((T, D), BF),
        ),
        in_specs=vm(7),
        out_specs=tuple(vm(4)),
        scratch_shapes=scan_scratch()
        + [pltpu.VMEM((T, INNER), F32), pltpu.VMEM((T, 128), F32), pltpu.VMEM((T, INNER), BF)],
        compiler_params=pltpu.CompilerParams(**PARAMS),
        name="layer_forward",
    )(stream, w, rows, heads, skip, cols, seg_row)


def layer_backward(grad, stream, normed, proj, mixed, w, rows, heads, skip, cols, seg_row):
    return pl.pallas_call(
        bwd_kernel,
        out_shape=(
            jax.ShapeDtypeStruct((T, D), F32),
            jax.ShapeDtypeStruct((D, WIDE), BF),
            jax.ShapeDtypeStruct((8, CONV), F32),
        ),
        in_specs=vm(11),
        out_specs=tuple(vm(3)),
        scratch_shapes=scan_scratch()
        + [
            pltpu.VMEM((T, INNER), F32),
            pltpu.VMEM((T, CONV), F32),
            pltpu.VMEM((T, PROJW), BF),
            pltpu.VMEM((T, T), F32),
            pltpu.VMEM((T, 128), F32),
            pltpu.VMEM((T, 128), F32),
            pltpu.VMEM((T, D), BF),
            pltpu.VMEM((D, T), BF),
            pltpu.VMEM((T, 128), F32),
            pltpu.VMEM((T, 128), F32),
            pltpu.VMEM((8, INNER), F32),
        ],
        compiler_params=pltpu.CompilerParams(**PARAMS),
        name="layer_backward",
    )(grad, stream, normed, proj, mixed, w, rows, heads, skip, cols, seg_row)


def wide_shard(in_weight, out_weight):
    pad = jnp.zeros((in_weight.shape[0], WIDE - STEP0 - HEADS), BF)
    return jnp.concatenate([in_weight[:, :GC], out_weight.T, in_weight[:, GC:], pad], axis=1)


def local(tokens, cotangent, segments, counts, norm_gain, in_weight, conv_weight, conv_bias, a_log, dt_bias, skip, gate_gain, out_weight):
    layers = in_weight.shape[0]
    me = lax.axis_index("fsdp")
    seg = segments.astype(F32)
    ahead = [jnp.concatenate([jnp.full((k,), -1.0, F32), seg[: T - k]]) for k in range(1, 4)]
    after = [jnp.concatenate([seg[k:], jnp.full((k,), -1.0, F32)]) for k in range(1, 4)]
    live = (jnp.arange(T, dtype=jnp.int32) < counts[0]).astype(F32)
    cols = jnp.stack([seg] + ahead + after + [live], axis=1)
    seg_row = seg[None, :]
    small = jnp.concatenate([conv_bias[:, :, None], conv_weight], axis=2).reshape(layers, -1)
    small = lax.all_gather(jnp.concatenate([small, gate_gain, norm_gain], axis=1), "fsdp", axis=0)
    widths = (CONV // 128 * 5, INNER // 128, D // 128)
    stream = tokens.astype(F32)
    kept = []
    for l in range(layers):
        w = lax.all_gather(wide_shard(in_weight[l], out_weight[l]), "fsdp", axis=0, tiled=True)
        part = small[:, l, :].astype(F32)
        conv = part[:, : widths[0]].reshape(CONV, 5).T
        gate = part[:, widths[0] : widths[0] + widths[1]].reshape(1, INNER)
        norm = part[:, widths[0] + widths[1] :].reshape(1, D)
        rows = jnp.concatenate([conv, jnp.pad(gate, ((0, 0), (0, CONV - INNER))), jnp.pad(norm, ((0, 0), (0, CONV - D))), jnp.zeros((1, CONV), F32)])
        heads = jnp.pad(jnp.stack([a_log[l], dt_bias[l], skip[l]]), ((0, 5), (0, 128 - HEADS)))
        wide_skip = jnp.repeat(skip[l], 64)[None, :]
        shared = (w, rows, heads, wide_skip, cols, seg_row)
        following, proj, mixed, normed = layer_forward(stream, *shared)
        kept.append((stream, normed, proj, mixed) + shared)
        stream = following
    output = (stream * live[:, None]).astype(BF)
    gradient = cotangent.astype(F32) * live[:, None]
    wide_grads, small_grads = [None] * layers, [None] * layers
    for l in reversed(range(layers)):
        gradient, wide, small_grads[l] = layer_backward(gradient, *kept[l])
        wide_grads[l] = lax.psum_scatter(wide, "fsdp", scatter_dimension=0, tiled=True).astype(F32)
    total = lax.psum(jnp.stack(small_grads), "fsdp")
    wide = jnp.stack(wide_grads)
    conv = lax.dynamic_slice_in_dim(total[:, 0:5], me * 14, 14, axis=2)
    gate = lax.dynamic_slice_in_dim(total[:, 5], me * 12, 12, axis=1)
    norm = lax.dynamic_slice_in_dim(total[:, 6], me * 6, 6, axis=1)
    return (
        output,
        gradient.astype(BF),
        norm,
        jnp.concatenate([wide[:, :, :GC], wide[:, :, STEP0 : STEP0 + HEADS]], axis=2),
        jnp.transpose(conv[:, 1:5], (0, 2, 1)),
        conv[:, 0],
        total[:, 7, 0:HEADS],
        total[:, 7, 128 : 128 + HEADS],
        total[:, 7, 256 : 256 + HEADS],
        gate,
        jnp.transpose(wide[:, :, OUT0:STEP0], (0, 2, 1)),
    )


def solution(mesh):
    axis = P("fsdp")
    rows, second, third = P("fsdp", None), P(None, "fsdp"), P(None, None, "fsdp")
    middle = P(None, "fsdp", None)
    return jax.shard_map(
        local,
        mesh=mesh,
        in_specs=(rows, rows, axis, axis, second, middle, middle, second, P(), P(), P(), second, third),
        out_specs=(rows, rows, second, middle, middle, second, P(), P(), P(), second, third),
        check_vma=False,
    )
```

```python
from functools import partial

import jax
import jax.numpy as jnp
from jax import lax
from jax.experimental import pallas as pl
from jax.experimental.pallas import tpu as pltpu
from jax.sharding import PartitionSpec as P

D = 768
HEADS = 24
STATE = 128
INNER = 1536
CONV = 1792
T = 384
STEP = 1792
USED = 1920
SMALL = 1920
REST = 2048
EPS = 1e-05
F32 = jnp.float32
BF = jnp.bfloat16
HIGHEST = lax.Precision.HIGHEST
MESH = pl.DeviceIdType.MESH


def nn(a, b):
    return lax.dot_general(a, b, (((1,), (0,)), ((), ())), preferred_element_type=F32)


def nt(a, b):
    return lax.dot_general(a, b, (((1,), (1,)), ((), ())), preferred_element_type=F32)


def tn(a, b):
    return lax.dot_general(a, b, (((0,), (0,)), ((), ())), preferred_element_type=F32)


def exact(a, b):
    return lax.dot_general(a, b, (((1,), (0,)), ((), ())), precision=HIGHEST, preferred_element_type=F32)


def iota(shape, dim):
    return lax.broadcasted_iota(jnp.int32, shape, dim)


def ones_where(cond):
    return jnp.where(cond, 1.0, 0.0)


def tiles(start, width):
    if isinstance(start, int):
        return pl.ds(start, width)
    return pl.ds(pl.multiple_of(start, 128), width)


def sigmoid(v):
    return 1.0 / (1.0 + jnp.exp(-v))


def weight(w, cols):
    v = w[:, :, :, cols]
    return v.reshape(D, v.shape[-1])


def put_rows(g, cols, v):
    g[:, :, :, cols] = v.astype(BF).reshape(4, 4, 48, v.shape[-1])


def pack3(v):
    hi = v.astype(BF).astype(F32)
    rest = v - hi
    mid = rest.astype(BF).astype(F32)
    low = rest - mid
    return (hi + pltpu.roll(mid, 32, 1) + pltpu.roll(low, 64, 1)).astype(BF)


def unpack3(v):
    return v + pltpu.roll(v, 96, 1) + pltpu.roll(v, 64, 1)


def head_mask(shape=(T, 128)):
    return iota(shape, 1) < HEADS


def spread_matrix(j, width, shift):
    return ones_where((iota((128, width), 0) & 31) == 4 * j + (iota((128, width), 1) >> shift)).astype(BF)


UNITS = ((14, 4682), (12, 5462), (6, 10923))


def small_rows(w_rest, heads, rows, skip):
    pick = ones_where(iota((128, D), 1) == 6 * iota((128, D), 0)).astype(BF)
    held = nn(pick, weight(w_rest, tiles(SMALL, 128))).astype(BF)

    def row(entries, magic, offset, width):
        c = iota((128, width), 1)
        unit = (c * magic) >> 16
        spread = ones_where(iota((128, width), 0) == offset + c - unit * entries).astype(BF)
        return jnp.sum(jnp.where(unit == iota((128, width), 0), nn(held, spread), 0.0), axis=0, keepdims=True)

    for n in range(5):
        rows[n : n + 1, :] = row(*UNITS[0], 14 * n, CONV)
    rows[5:6, 0:INNER] = row(*UNITS[1], 70, INNER)
    rows[6:7, 0:D] = row(*UNITS[2], 82, D)
    which = ones_where((iota((128, INNER), 1) >> 6) == iota((128, INNER), 0))
    skip[...] = exact(heads[...], which)


def rms_normed(stream, gain):
    r = lax.rsqrt(jnp.mean(stream * stream, axis=-1, keepdims=True) + EPS)
    return stream * r * gain


def step_terms(raw, heads):
    mask = head_mask()
    rate = -jnp.exp(heads[0:1, :])
    x = jnp.where(mask, raw + heads[1:2, :], 0.0)
    step = jnp.where(mask, jnp.maximum(x, 0.0) + jnp.log1p(jnp.exp(-jnp.abs(x))), 0.0)
    return rate, x, step


def prepare_scan(raw, heads, step3, log3, log_t):
    rate, x, step = step_terms(raw, heads)
    lower = ones_where(iota((T, T), 0) >= iota((T, T), 1)).astype(BF)
    total = unpack3(nn(lower, pack3(jnp.where(head_mask(), step * rate, 0.0))))
    total = jnp.where(head_mask(), total, 0.0)
    step3[...] = pack3(step)
    log3[...] = pack3(total)
    flipped = jnp.transpose(total)
    for h in range(HEADS):
        log_t[h] = flipped[h : h + 1]


def conv_pass(rest, rows, cols, act):
    masks = [ones_where(cols[:, k : k + 1] == cols[:, 0:1]) for k in range(1, 4)]

    def body(c, carry):
        here = tiles(c * 128, 128)
        ci = rest[:, here]
        total = rows[0:1, here] + ci * rows[4:5, here]
        for k in range(1, 4):
            total = total + pltpu.roll(ci, k, 0) * masks[k - 1] * rows[4 - k : 5 - k, here]
        act[:, here] = total * sigmoid(total)
        return carry

    lax.fori_loop(0, 14, body, 0)


def linked_pairs(cols, seg_row):
    return (cols[:, 0:1] == seg_row[0:1, :]) & (iota((T, T), 0) >= iota((T, T), 1))


def score_pass(act, cols, seg_row, scores, scores_low):
    b = act[:, INNER : INNER + STATE]
    c = act[:, INNER + STATE :]
    s = lax.dot_general(c, b, (((1,), (1,)), ((), ())), precision=HIGHEST, preferred_element_type=F32)
    s = jnp.where(linked_pairs(cols, seg_row), s, 0.0)
    scores[...] = s
    scores_low[...] = s.astype(BF)


def lane_heads(q):
    return (iota((128, 256), 1) >> 6) == q


def block_rows(i):
    return slice(128 * i, 128 * (i + 1))


def chunk_terms(j, act, step3, log3):
    x = act[:, tiles(j * 256, 256)]
    spread = spread_matrix(j, 256, 6)
    step_e = nn(step3[...], spread)
    log_e = nn(log3[...], spread)
    wide = nn(log3[...], spread_matrix(j, 512, 7))
    return x, step_e, log_e, wide, x * step_e


def decays(i, j, wide, log_t):
    out = []
    for q in range(4):
        row = log_t[4 * j + q, :, block_rows(i)]
        out.append(jnp.exp(jnp.minimum(wide[block_rows(i), 128 * q : 128 * (q + 1)] - row, 0.0)))
    return out


def project(c, normed, w, proj):
    here = tiles(c * 256, 256)
    proj[:, here] = nn(normed[...], weight(w, here))


def forward_chunk(j, rows, skip, gate_ref, act, scores, scores_low, step3, log3, log_t, mixed_ref, gated, square):
    here = tiles(j * 256, 256)
    x, step_e, log_e, wide, xd = chunk_terms(j, act, step3, log3)
    xd_low = xd.astype(BF)
    for i in range(3):
        at = block_rows(i)
        sc = scores[at, at]
        left = jnp.concatenate([(sc * e).astype(BF) for e in decays(i, j, wide, log_t)], axis=1)
        part = xd_low[at]
        right = jnp.concatenate([jnp.where(lane_heads(q), part, 0) for q in range(4)], axis=0)
        y = nn(left, right)
        if i:
            edge = log_e[128 * i - 1 : 128 * i, :]
            before = slice(0, 128 * i)
            carried = (xd[before] * jnp.exp(jnp.minimum(edge - log_e[before], 0.0))).astype(BF)
            y = y + jnp.exp(jnp.minimum(log_e[at] - edge, 0.0)) * nn(scores_low[at, before], carried)
        mixed = y + skip[2:3, here] * x[at]
        mixed_ref[at, here] = mixed
        gate = gate_ref[at, here]
        u = mixed * (gate * sigmoid(gate))
        gated[at, here] = u
        uu = u * u
        square[at, :] += uu[:, :128] + uu[:, 128:]


def gate_norm(rows, gated, square, yn):
    r = lax.rsqrt(jnp.sum(square[...], axis=-1, keepdims=True) * (1.0 / INNER) + EPS)

    def gain(c, carry):
        here = tiles(c * 256, 256)
        yn[:, here] = (gated[:, here] * r * rows[5:6, here]).astype(BF)
        return carry

    lax.fori_loop(0, 6, gain, 0)


def first_backward(c, gl, w_out, rows, gate_ref, mixed_ref, dyn, sum_u, sum_d):
    here = tiles(c * 256, 256)
    dy = nn(gl[...], weight(w_out, here))
    dyn[:, here] = dy
    gate = gate_ref[:, here]
    u = mixed_ref[:, here] * (gate * sigmoid(gate))
    uu = u * u
    ud = u * dy * rows[5:6, here]
    sum_u[...] += uu[:, :128] + uu[:, 128:]
    sum_d[...] += ud[:, :128] + ud[:, 128:]


def norm_pull(sum_u, sum_d):
    r = lax.rsqrt(jnp.sum(sum_u[...], axis=-1, keepdims=True) * (1.0 / INNER) + EPS)
    pull = r * r * r * (jnp.sum(sum_d[...], axis=-1, keepdims=True) * (1.0 / INNER))
    sum_u[...] = jnp.broadcast_to(r, (T, 128))
    sum_d[...] = jnp.broadcast_to(pull, (T, 128))


def backward_chunk(j, rows, skip, gate_ref, act, scores, scores_low, step3, log3, log_t, mixed_ref, dyn, sum_u, sum_d,
                   gl_t, norm_t, g_out, g_gate, small, dgate, dact, dscores, dlog, dstep, row_skip):
    here = tiles(j * 256, 256)
    r = sum_u[:, 0:1]
    pull = sum_d[:, 0:1]
    x, step_e, log_e, wide, xd = chunk_terms(j, act, step3, log3)
    xd_low = xd.astype(BF)
    dy = dyn[:, here]
    gate = gate_ref[:, here]
    mixed = mixed_ref[:, here]
    sg = sigmoid(gate)
    silu = gate * sg
    gain = rows[5:6, here]
    u = mixed * silu
    ur = u * r
    small[5:6, here] = jnp.sum(dy * ur, axis=0, keepdims=True)
    put_rows(g_out, here, nn(gl_t[...], (ur * gain).astype(BF)))
    du = r * (gain * dy) - u * pull
    dg = (du * mixed * (sg * (1.0 + gate * (1.0 - sg)))).astype(BF)
    dgate[:, here] = dg
    put_rows(g_gate, here, nn(norm_t[...], dg))
    dm = du * silu
    row_skip[0:1, here] = jnp.sum(dm * x, axis=0, keepdims=True)
    dm_low = dm.astype(BF)
    v_parts, dxd_parts = [], []
    for i in range(3):
        at = block_rows(i)
        sc = scores[at, at]
        es = decays(i, j, wide, log_t)
        ws = [(sc * e).astype(BF) for e in es]
        part, dpart = xd_low[at], dm_low[at]
        right = jnp.concatenate([jnp.where(lane_heads(q), part, 0) for q in range(4)], axis=0)
        dright = jnp.concatenate([jnp.where(lane_heads(q), dpart, 0) for q in range(4)], axis=0)
        y = nn(jnp.concatenate(ws, axis=1), right)
        dxd = tn(jnp.concatenate(ws, axis=0), dright)
        g = nt(dright, part)
        ds = g[0:128] * es[0]
        for q in range(1, 4):
            ds = ds + g[128 * q : 128 * (q + 1)] * es[q]
        dscores[at, at] += ds
        v_parts.append(dpart.astype(F32) * y - part.astype(F32) * dxd)
        dxd_parts.append(dxd)
    for i in range(1, 3):
        at = block_rows(i)
        before = slice(0, 128 * i)
        edge = log_e[128 * i - 1 : 128 * i, :]
        fade = jnp.exp(jnp.minimum(edge - log_e[before], 0.0))
        carried = (xd[before] * fade).astype(BF)
        de = (dm[at] * jnp.exp(jnp.minimum(log_e[at] - edge, 0.0))).astype(BF)
        z = nn(scores_low[at, before], carried)
        dz = tn(scores_low[at, before], de)
        dscores[at, before] += nt(de, carried)
        v_parts[i] = v_parts[i] + de.astype(F32) * z
        back = carried.astype(F32) * dz
        faded = fade * dz
        for k in range(i):
            v_parts[k] = v_parts[k] - back[block_rows(k)]
            dxd_parts[k] = dxd_parts[k] + faded[block_rows(k)]
    v = jnp.concatenate(v_parts, axis=0)
    dxd = jnp.concatenate(dxd_parts, axis=0)
    dact[:, here] = step_e * dxd + skip[2:3, here] * dm
    gather = ones_where(4 * j + ((iota((512, 128), 0) & 255) >> 6) == iota((512, 128), 1)).astype(BF)

    def head_sums(a):
        hi = a.astype(BF)
        return nn(jnp.concatenate([hi, (a - hi.astype(F32)).astype(BF)], axis=1), gather)

    dlog[...] += head_sums(v)
    dstep[...] += head_sums(x * dxd)


def scores_backward(act, cols, seg_row, dscores, dact):
    ds = jnp.where(linked_pairs(cols, seg_row), dscores[...], 0.0).astype(BF)
    b = act[:, INNER : INNER + STATE].astype(BF)
    c = act[:, INNER + STATE :].astype(BF)
    dact[:, INNER : INNER + STATE] = tn(ds, c)
    dact[:, INNER + STATE :] = nn(ds, b)


def steps_backward(raw, heads, dlog, dstep, drest, small, row_skip):
    rate, x, step = step_terms(raw, heads)
    upper = ones_where(iota((T, T), 0) <= iota((T, T), 1)).astype(BF)
    dsum = unpack3(nn(upper, pack3(dlog[...])))
    dsum = jnp.where(head_mask(), dsum, 0.0)
    dx = jnp.where(head_mask(), (dstep[...] + rate * dsum) * sigmoid(x), 0.0)
    drest[:, STEP:USED] = dx.astype(BF)
    rates = jnp.sum(dsum * step, axis=0, keepdims=True) * jnp.where(head_mask((1, 128)), rate, 0.0)
    biases = jnp.sum(dx, axis=0, keepdims=True)
    which = ones_where((iota((INNER, 128), 0) >> 6) == iota((INNER, 128), 1))
    skips = exact(row_skip[...], which)[0:1]
    small[7:8, 0:128] = rates + pltpu.roll(biases, 32, 1) + pltpu.roll(skips, 64, 1)


def conv_backward(c, rest, rows, cols, dact, small, drest):
    here = tiles(c * 128, 128)
    ci = rest[:, here]
    taps = [rows[4 - k : 5 - k, here] for k in range(4)]
    masks = [ones_where(cols[:, k : k + 1] == cols[:, 0:1]) for k in range(1, 7)]
    shifted = [ci] + [pltpu.roll(ci, k, 0) * masks[k - 1] for k in range(1, 4)]
    total = rows[0:1, here] + ci * taps[0]
    for k in range(1, 4):
        total = total + shifted[k] * taps[k]
    sg = sigmoid(total)
    dc = dact[:, here] * (sg * (1.0 + total * (1.0 - sg)))
    small[0:1, here] = jnp.sum(dc, axis=0, keepdims=True)
    dci = dc * taps[0]
    for k in range(4):
        small[4 - k : 5 - k, here] = jnp.sum(dc * shifted[k], axis=0, keepdims=True)
        if k:
            dci = dci + pltpu.roll(dc, T - k, 0) * masks[k + 2] * taps[k]
    drest[:, here] = dci.astype(BF)


def rest_grad(norm_t, drest, g_rest):
    def body(c, carry):
        here = tiles(c * 256, 256)
        put_rows(g_rest, here, nn(norm_t[...], drest[:, here]))
        return carry

    lax.fori_loop(0, 7, body, 0)
    put_rows(g_rest, pl.ds(STEP, 128), nn(norm_t[...], drest[:, STEP:USED]))
    g_rest[:, :, :, SMALL:] = jnp.zeros((4, 4, 48, 128), BF)


def normed_backward(dgate, drest, w_gate, w_rest, dn):
    for n in range(2):
        gate = w_gate[2 * n : 2 * n + 2].reshape(T, INNER)
        rest = w_rest[2 * n : 2 * n + 2, :, :, 0:USED].reshape(T, USED)
        dn[:, T * n : T * (n + 1)] = nt(dgate[...], gate) + nt(drest[...], rest)


def stream_backward(dn, stream, gain, grad, small):
    r = lax.rsqrt(jnp.mean(stream * stream, axis=-1, keepdims=True) + EPS)
    small[6:7, 0:D] = jnp.sum(dn * stream * r, axis=0, keepdims=True)
    gd = gain * dn
    return grad + r * gd - stream * (r * r * r * jnp.mean(stream * gd, axis=-1, keepdims=True))


class Place:
    def __init__(self):
        me = lax.axis_index("fsdp")
        self.me = me
        self.x = lax.div(me, 32)
        self.y = lax.rem(lax.div(me, 8), 4)
        self.z = lax.rem(lax.div(me, 2), 4)
        self.c = lax.rem(me, 2)

    def at(self, dx=0, dy=0, dz=0, dc=0):
        x = lax.rem(self.x + dx, 4)
        y = lax.rem(self.y + dy, 4)
        z = lax.rem(self.z + dz, 4)
        c = lax.rem(self.c + dc, 2)
        return ((x * 4 + y) * 4 + z) * 2 + c

    def along(self, axis, step):
        return self.at(dx=step) if axis == 0 else self.at(dy=step)

    def half(self, core, size, color=0, colors=1):
        return pl.ds(pl.multiple_of(core * size + color * (size // 2), 128), size // colors)


def greet(places):
    barrier = pltpu.get_barrier_semaphore()
    for place in places:
        pl.semaphore_signal(barrier, inc=1, device_id=(place,), device_id_type=MESH)
    pl.semaphore_wait(barrier, len(places))


class Semaphores:
    def __init__(self, send, recv):
        self.send, self.recv, self.count = send, recv, 0

    def next(self):
        self.count += 1
        return self.send.at[self.count - 1], self.recv.at[self.count - 1]


class Copies:
    def __init__(self, semaphores):
        self.semaphores, self.made, self.over = semaphores, {}, set()

    def make(self, name, src, dst, device):
        send, recv = self.semaphores.next()
        self.made[name] = pltpu.make_async_remote_copy(
            src_ref=src, dst_ref=dst, send_sem=send, recv_sem=recv, device_id=(device,), device_id_type=MESH
        )

    def start(self, *name):
        self.made[name].start()

    def got(self, *name):
        self.made[name].wait_recv()

    def sent(self, *name):
        self.made[name].wait_send()
        self.over.add(name)

    def finish(self):
        for name in self.made:
            if name not in self.over:
                self.sent(*name)


STEPS = (1, 3, 2)
OFFSETS = (0, 3, 1, 2)
GROUP = [(dz, dc) for dz in (1, 3, 2, 0) for dc in (0, 1) if (dz, dc) != (0, 0)]


class GatherGroup:
    def __init__(self, at, shard, slots, semaphores):
        self.at, self.shard, self.slots, self.size = at, shard, slots, slots.shape[2]
        self.mine = at.z * 2 + at.c
        self.copies = Copies(semaphores)
        for dz, dc in GROUP:
            core = lax.rem(at.c + dc, 2)
            self.copies.make((dz, dc), shard.at[:, at.half(core, self.size)], slots.at[self.mine], at.at(dz=dz, dc=dc))

    def begin(self):
        for name in GROUP:
            self.copies.start(*name)
        self.slots[self.mine] = self.shard[:, self.at.half(self.at.c, self.size)]

    def end(self, first, second):
        for name in GROUP:
            self.copies.got(*name)
        row, k = iota((96, 128), 0), iota((96, 128), 1)
        within = k & 15
        block = jnp.where(within >= 6, 1, 0)
        aim = block * 48 + (k >> 4) * 6 + within - 6 * block
        select = ones_where((row == aim) & (within < 12)).astype(BF)
        got = nn(select, self.slots[...].reshape(128, self.size)).astype(BF)
        at = self.at
        first[at.x, at.y, :, at.half(at.c, self.size)] = got[:48]
        second[at.x, at.y, :, at.half(at.c, self.size)] = got[48:]


class GatherPlane:
    def __init__(self, at, w, semaphores):
        self.copies = c = Copies(semaphores)
        size = w.shape[3] // 2

        def block(color, first, second):
            dx, dy = (first, second) if color == 0 else (second, first)
            return w.at[lax.rem(at.x + dx, 4), lax.rem(at.y + dy, 4), :, at.half(at.c, size, color, 2)]

        for color in range(2):
            near, far = color, 1 - color
            for step in STEPS:
                own = block(color, 0, 0)
                c.make(("a", color, step), own, own, at.along(near, step))
                for o in OFFSETS:
                    there = block(color, o, 0)
                    c.make(("c", color, o, step), there, there, at.along(far, step))
            for o in OFFSETS:
                cols = at.half(at.c, size, color, 2)
                there = w.at[:, lax.rem(at.y + o, 4), :, cols] if color == 0 else w.at[lax.rem(at.x + o, 4), :, :, cols]
                c.make(("p", color, o), there, there, at.at(dc=1))

    def begin(self):
        for step in STEPS:
            for color in range(2):
                self.copies.start("a", color, step)
        for step in STEPS:
            for color in range(2):
                self.copies.start("c", color, 0, step)

    def near(self):
        for step in STEPS:
            for color in range(2):
                self.copies.got("a", color, step)
                for further in STEPS:
                    self.copies.start("c", color, 4 - step, further)
        for color in range(2):
            self.copies.start("p", color, 0)

    def far(self):
        for step in STEPS:
            for color in range(2):
                for o in OFFSETS:
                    self.copies.got("c", color, o, step)
                self.copies.start("p", color, 4 - step)

    def end(self):
        for o in OFFSETS:
            for color in range(2):
                self.copies.got("p", color, o)


def plus(a, b):
    return a.astype(F32) + b.astype(F32)


class Reduce:
    SENDS = 18

    def __init__(self, at, g, out, scratch, semaphores):
        self.h, self.rb, self.rb1, self.zs, self.zr, self.xs = scratch
        self.at, self.g, self.out = at, g, out
        self.size = g.shape[3] // 2
        self.copies = c = Copies(semaphores)
        other = lax.rem(at.c + 1, 2)
        for color in range(2):
            cols = self.here(color)
            c.make(("p", color), g.at[:, :, :, at.half(other, self.size, color, 2)], self.h.at[:, :, :, cols], at.at(dc=1))
            for step in STEPS:
                c.make(("a", color, step), self.rows(color, step), self.rb.at[color, step - 1], at.along(color, step))
                c.make(("d", color, step), self.block(color, step), self.rb1.at[color, step - 1], at.along(1 - color, step))
        for dz in STEPS:
            c.make(("z", dz), self.zs.at[lax.rem(at.z + dz, 4)], self.zr.at[at.z], at.at(dz=dz))
        c.make(("x",), self.xs, out.at[:, at.half(at.c, self.size)], at.at(dc=1))

    def here(self, color):
        return pl.ds(color * (self.size // 2), self.size // 2)

    def rows(self, color, o):
        if color == 0:
            return self.h.at[lax.rem(self.at.x + o, 4), :, :, self.here(color)]
        return self.h.at[:, lax.rem(self.at.y + o, 4), :, self.here(color)]

    def block(self, color, o):
        dx, dy = (0, o) if color == 0 else (o, 0)
        return self.h.at[lax.rem(self.at.x + dx, 4), lax.rem(self.at.y + dy, 4), :, self.here(color)]

    def begin(self):
        for color in range(2):
            self.copies.start("p", color)

    def pair(self, color):
        at = self.at
        self.copies.got("p", color)
        cols = self.here(color)

        def add(n, carry):
            x, y = lax.div(n, 4), lax.rem(n, 4)
            own = self.g[x, y, :, at.half(at.c, self.size, color, 2)]
            self.h[x, y, :, cols] = plus(own, self.h[x, y, :, cols]).astype(BF)
            return carry

        lax.fori_loop(0, 16, add, 0)
        for step in STEPS:
            self.copies.start("a", color, step)

    def near(self, color):
        for step in STEPS:
            self.copies.got("a", color, step)
        cols = self.here(color)

        def add(n, carry):
            x, y = (self.at.x, n) if color == 0 else (n, self.at.y)
            there = (x, y, slice(None), cols)
            self.h[there] = (plus(self.h[there], self.rb[color, 0, n]) + plus(self.rb[color, 1, n], self.rb[color, 2, n])).astype(BF)
            return carry

        lax.fori_loop(0, 4, add, 0)
        for step in STEPS:
            self.copies.start("d", color, step)

    def far(self, color):
        for step in STEPS:
            self.copies.got("d", color, step)
        there = self.block(color, 0)
        there[...] = (plus(there[...], self.rb1[color, 0]) + plus(self.rb1[color, 1], self.rb1[color, 2])).astype(BF)

    def along_z(self):
        at = self.at
        row, k = iota((64, 48), 0), iota((64, 48), 1)
        select = ones_where(((row & 15) < 12) & (k == 12 * (row >> 4) + (row & 15))).astype(BF)
        self.zs[...] = nn(select, self.h[at.x, at.y]).astype(BF).reshape(4, 16, self.size)
        for dz in STEPS:
            self.copies.start("z", dz)
        self.zr[at.z] = self.zs[at.z]

    def along_core(self):
        at = self.at
        for dz in STEPS:
            self.copies.got("z", dz)
        total = plus(self.zr[0], self.zr[1]) + plus(self.zr[2], self.zr[3])
        low, high = total[0:8], jnp.concatenate([total[6:12], total[0:2]], axis=0)
        core = jnp.broadcast_to(at.c, (8, self.size))
        self.xs[...] = jnp.where(core == 0, high, low)
        for color in range(2):
            for step in STEPS:
                self.copies.sent("a", color, step)
                self.copies.sent("d", color, step)
        self.copies.start("x")
        self.out[:, at.half(at.c, self.size)] = jnp.where(core == 0, low, high)

    def end(self):
        self.copies.got("x")


class SmallReduce:
    SENDS = 10

    def __init__(self, at, small, out, scratch, semaphores):
        self.at, self.small, self.out = at, small, out
        self.sx, self.sy, self.sz, self.sc = scratch
        self.copies = c = Copies(semaphores)
        for d in STEPS:
            c.make(("sx", d), self.sx.at[at.x], self.sx.at[at.x], at.at(dx=d))
            c.make(("sy", d), self.sy.at[at.y], self.sy.at[at.y], at.at(dy=d))
            c.make(("sz", d), self.sz.at[at.z], self.sz.at[at.z], at.at(dz=d))
        c.make(("sc",), self.sc.at[at.c], self.sc.at[at.c], at.at(dc=1))

    def begin(self):
        self.sx[self.at.x] = self.small[...]
        for d in STEPS:
            self.copies.start("sx", d)

    def step(self, name, here, following, index):
        for d in STEPS:
            self.copies.got(name, d)
        following[index] = (here[0] + here[1]) + (here[2] + here[3])

    def along_y(self):
        self.step("sx", self.sx, self.sy, self.at.y)
        for d in STEPS:
            self.copies.start("sy", d)

    def along_z(self):
        self.step("sy", self.sy, self.sz, self.at.z)
        for d in STEPS:
            self.copies.start("sz", d)

    def along_core(self):
        self.step("sz", self.sz, self.sc, self.at.c)
        self.copies.start("sc")

    def end(self):
        self.copies.got("sc")
        total = self.sc[0] + self.sc[1]

        def own(entries, width):
            pick = ones_where(iota((width, 128), 0) == entries * self.at.me + iota((width, 128), 1))
            pick = jnp.where(iota((width, 128), 1) < entries, pick, 0.0)
            return exact(total[:, :width], pick)

        self.out[0:5, :] = own(14, CONV)[0:5]
        self.out[5:6, :] = own(12, INNER)[5:6]
        self.out[6:7, :] = own(6, D)[6:7]
        self.out[7:8, :] = total[7:8, 0:128]


def dma_pair(count):
    return [pltpu.SemaphoreType.DMA((count,)), pltpu.SemaphoreType.DMA((count,))]


def wide_scratch(width):
    size = width // 2
    return [
        pltpu.VMEM((4, 4, 48, size), BF),
        pltpu.VMEM((2, 3, 4, 48, size // 2), BF),
        pltpu.VMEM((2, 3, 48, size // 2), BF),
    ]


def narrow_scratch(width):
    size = width // 2
    return [
        pltpu.VMEM((4, 16, size), BF),
        pltpu.VMEM((4, 16, size), BF),
        pltpu.VMEM((8, size), F32),
    ]


def small_scratch():
    return [pltpu.VMEM((4, 8, CONV), F32)] * 3 + [pltpu.VMEM((2, 8, CONV), F32)]


WIDTHS = (REST, INNER, INNER)


def vm(count):
    return [pl.BlockSpec(memory_space=pltpu.VMEM)] * count


def shape(*dims, dtype=F32):
    return jax.ShapeDtypeStruct(dims, dtype)


def whole(width):
    return shape(4, 4, 48, width, dtype=BF)


LIMIT = 62 * 1024 * 1024


def scan_scratch():
    return [
        pltpu.VMEM((T, CONV), F32),
        pltpu.VMEM((T, T), F32),
        pltpu.VMEM((T, T), BF),
        pltpu.VMEM((T, 128), BF),
        pltpu.VMEM((T, 128), BF),
        pltpu.VMEM((HEADS, 1, T), F32),
    ]


def forward_scratch():
    return [
        pltpu.VMEM((T, D), BF),
        pltpu.VMEM((T, INNER), F32),
        pltpu.VMEM((T, 128), F32),
        pltpu.VMEM((T, INNER), BF),
    ]


def backward_scratch():
    return [
        pltpu.VMEM((T, 128), F32),
        pltpu.VMEM((T, 128), F32),
        pltpu.VMEM((T, D), BF),
        pltpu.VMEM((D, T), BF),
        pltpu.VMEM((D, T), BF),
        pltpu.VMEM((T, INNER), BF),
        pltpu.VMEM((T, USED), BF),
        pltpu.VMEM((T, CONV), F32),
        pltpu.VMEM((T, T), F32),
        pltpu.VMEM((T, 128), F32),
        pltpu.VMEM((T, 128), F32),
        pltpu.VMEM((8, INNER), F32),
    ]


def nothing(name):
    return None


def run_forward(stream, w, heads, cols, seg_row, rows, skip, rest, gate, mixed, following, scan, scratch, then=nothing):
    w_rest, w_gate, w_out = w
    act, scores, scores_low, step3, log3, log_t = scan
    normed, gated, square, yn = scratch
    small_rows(w_rest, heads, rows, skip)
    normed[...] = rms_normed(stream[...], rows[6:7, 0:D]).astype(BF)
    then("normed")

    def rest_part(c, carry):
        project(c, normed, w_rest, rest)
        return carry

    lax.fori_loop(0, 7, rest_part, 0)
    rest[:, STEP:USED] = nn(normed[...], weight(w_rest, pl.ds(STEP, 128)))
    then("rest")
    prepare_scan(rest[:, STEP:USED], heads, step3, log3, log_t)
    conv_pass(rest, rows, cols, act)
    then("conv")
    score_pass(act, cols, seg_row, scores, scores_low)
    then("scores")
    square[...] = jnp.zeros_like(square)

    def chunk(j, carry):
        project(j, normed, w_gate, gate)
        forward_chunk(j, rows, skip, gate, act, scores, scores_low, step3, log3, log_t, mixed, gated, square)
        for n in range(6):
            if then is not nothing:
                pl.when(j == n)(lambda: then("chunk%d" % n))
        return carry

    lax.fori_loop(0, 6, chunk, 0)
    gate_norm(rows, gated, square, yn)
    then("yn")
    for n in range(2):
        there = slice(T * n, T * (n + 1))
        following[:, there] = stream[:, there] + nt(yn[...], w_out[2 * n : 2 * n + 2].reshape(T, INNER))


def run_backward(grad, stream, normed, w, heads, cols, seg_row, rows, skip, rest, gate, mixed, g, small, finish, scan, scratch, ready, then=nothing):
    w_rest, w_gate, w_out = w
    g_rest, g_gate, g_out = g
    act, scores, scores_low, step3, log3, log_t = scan
    sum_u, sum_d, gl, gl_t, norm_t, dgate, drest, dact, dscores, dlog, dstep, row_skip = scratch
    dyn = dact
    gl[...] = grad[...].astype(BF)
    gl_t[...] = jnp.transpose(gl[...])
    norm_t[...] = jnp.transpose(normed[...])
    for ref in (small, sum_u, sum_d, dscores, dlog, dstep, row_skip):
        ref[...] = jnp.zeros_like(ref)

    def first(c, carry):
        first_backward(c, gl, w_out, rows, gate, mixed, dyn, sum_u, sum_d)
        return carry

    lax.fori_loop(0, 6, first, 0)
    then("first")
    if not ready:
        prepare_scan(rest[:, STEP:USED], heads, step3, log3, log_t)
        conv_pass(rest, rows, cols, act)
        then("conv")
        score_pass(act, cols, seg_row, scores, scores_low)
        then("scores")
    norm_pull(sum_u, sum_d)

    def chunk(j, carry):
        backward_chunk(j, rows, skip, gate, act, scores, scores_low, step3, log3, log_t, mixed, dyn, sum_u, sum_d,
                       gl_t, norm_t, g_out, g_gate, small, dgate, dact, dscores, dlog, dstep, row_skip)
        for n in range(6):
            if then is not nothing:
                pl.when(j == n)(lambda: then("chunk%d" % n))
        return carry

    lax.fori_loop(0, 6, chunk, 0)
    then("chunks")
    scores_backward(act, cols, seg_row, dscores, dact)
    steps_backward(rest[:, STEP:USED], heads, dlog, dstep, drest, small, row_skip)
    then("steps")

    def conv(c, carry):
        conv_backward(c, rest, rows, cols, dact, small, drest)
        return carry

    lax.fori_loop(0, 14, conv, 0)
    then("conv_back")
    rest_grad(norm_t, drest, g_rest)
    then("rest_grad")
    normed_backward(dgate, drest, w_gate, w_rest, dyn)
    then("normed_back")
    finish(stream_backward(dyn[:, 0:D], stream[...], rows[6:7, 0:D], grad[...], small))
    then("done")


def block0_kernel(shard_rest, shard_gate, shard_out, tokens, heads, cols, seg_row,
                  w0r, w0g, w0o, w1r, w1g, w1o, following, rest, gate, mixed, rows,
                  slots_r, slots_g, slots_o, skip, stream, *scratch):
    scan, forward, (send, recv) = scratch[:6], scratch[6:10], scratch[10:]
    at = Place()
    greet([at.at(dx=d) for d in STEPS] + [at.at(dy=d) for d in STEPS] + [at.at(dz=dz, dc=dc) for dz, dc in GROUP])
    semaphores = Semaphores(send, recv)
    a_rest, a_gate, a_out = [GatherGroup(at, s, t, semaphores) for s, t in ((shard_rest, slots_r), (shard_gate, slots_g), (shard_out, slots_o))]
    r0, g0, o0, r1, g1, o1 = planes = [GatherPlane(at, w, semaphores) for w in (w0r, w0g, w0o, w1r, w1g, w1o)]
    a_rest.begin()
    stream[...] = tokens[...].astype(F32)
    a_rest.end(w0r, w1r)
    r0.begin()
    a_gate.begin()
    a_out.begin()
    a_gate.end(w0g, w1g)
    a_out.end(w0o, w1o)
    r0.near()
    g0.begin()
    r0.far()
    r0.end()

    plan = {
        "normed": [g0.near],
        "rest": [o0.begin, g0.far],
        "conv": [o0.near, r1.begin],
        "scores": [g0.end, o0.far],
        "chunk0": [r1.near, g1.begin],
        "chunk2": [r1.far, g1.near, o1.begin],
        "chunk4": [g1.far, o1.near],
        "yn": [o0.end, r1.end, g1.end, o1.far],
    }

    def then(name):
        for step in plan.get(name, ()):
            step()

    run_forward(stream, (w0r, w0g, w0o), heads, cols, seg_row, rows, skip, rest, gate, mixed, following, scan, forward, then)
    o1.end()
    for each in [a_rest, a_gate, a_out] + planes:
        each.copies.finish()


GATHERS = 3 * 7 + 6 * 38


def block0(shards, tokens, heads, cols, seg_row):
    weights = tuple(whole(w) for w in WIDTHS)
    return pl.pallas_call(
        block0_kernel,
        out_shape=weights + weights + (shape(T, D), shape(T, USED), shape(T, INNER), shape(T, INNER), shape(8, CONV)),
        in_specs=vm(7),
        out_specs=tuple(vm(11)),
        scratch_shapes=[pltpu.VMEM((8, 16, w // 2), BF) for w in WIDTHS]
        + [pltpu.VMEM((8, INNER), F32), pltpu.VMEM((T, D), F32)]
        + scan_scratch()
        + forward_scratch()
        + dma_pair(GATHERS),
        compiler_params=pltpu.CompilerParams(collective_id=0, has_side_effects=True, vmem_limit_bytes=LIMIT),
        name="gather_and_block0",
    )(*shards, tokens, heads, cols, seg_row)


def block1_kernel(stream, w_rest, w_gate, w_out, heads, cols, seg_row, cotangent,
                  output, prev, g_rest, g_gate, g_out, small,
                  skip, rows, rest, gate, mixed, following, grad, *scratch):
    scan, forward, backward = scratch[:6], scratch[6:10], scratch[10:]
    w = (w_rest, w_gate, w_out)
    live = cols[:, 7:8]
    run_forward(stream, w, heads, cols, seg_row, rows, skip, rest, gate, mixed, following, scan, forward)
    output[...] = (following[...] * live).astype(BF)
    grad[...] = cotangent[...].astype(F32) * live

    def finish(value):
        prev[...] = value

    run_backward(grad, stream, forward[0], w, heads, cols, seg_row, rows, skip, rest, gate, mixed,
                 (g_rest, g_gate, g_out), small, finish, scan, backward, True)


def block1(stream, weights, heads, cols, seg_row, cotangent):
    return pl.pallas_call(
        block1_kernel,
        out_shape=(shape(T, D, dtype=BF), shape(T, D)) + tuple(whole(w) for w in WIDTHS) + (shape(8, CONV),),
        in_specs=vm(8),
        out_specs=tuple(vm(6)),
        scratch_shapes=[
            pltpu.VMEM((8, INNER), F32),
            pltpu.VMEM((8, CONV), F32),
            pltpu.VMEM((T, USED), F32),
            pltpu.VMEM((T, INNER), F32),
            pltpu.VMEM((T, INNER), F32),
            pltpu.VMEM((T, D), F32),
            pltpu.VMEM((T, D), F32),
        ]
        + scan_scratch()
        + forward_scratch()
        + backward_scratch(),
        compiler_params=pltpu.CompilerParams(vmem_limit_bytes=LIMIT),
        name="block1",
    )(stream, *weights, heads, cols, seg_row, cotangent)


def back0_kernel(grad, tokens, w_rest, w_gate, w_out, rows, heads, cols, seg_row, rest, gate, mixed, g1r, g1g, g1o, small1,
                 tokens_grad, o0r, o0g, o0o, s0, o1r, o1g, o1o, s1,
                 g0r, g0g, g0o, small0, stream, normed, skip, *scratch):
    scan, backward = scratch[:6], scratch[6:18]
    places = iter(scratch[18:])
    take = lambda n: [next(places) for _ in range(n)]
    r, g, o = [take(3) for _ in range(3)]
    buffers = [wide + take(3) for wide in (r, g, o, r, o, g)]
    small_buffers = [take(4) for _ in range(2)]
    semaphores = Semaphores(*take(2))
    at = Place()
    greet([at.at(dx=d) for d in STEPS] + [at.at(dy=d) for d in STEPS] + [at.at(dz=d) for d in STEPS] + [at.at(dc=1)])
    outs = ((g1r, o1r), (g1g, o1g), (g1o, o1o), (g0r, o0r), (g0g, o0g), (g0o, o0o))
    r1, g1, o1, r0, g0, o0 = sums = [Reduce(at, g, out, buffer, semaphores) for (g, out), buffer in zip(outs, buffers)]
    t1, t0 = smalls = [SmallReduce(at, *v, semaphores) for v in ((small1, s1, small_buffers[0]), (small0, s0, small_buffers[1]))]

    def two(step):
        return [partial(step, 0), partial(step, 1)]

    plan = {
        "begin": [r1.begin, g1.begin, o1.begin, t1.begin],
        "first": two(r1.pair) + [t1.along_y],
        "conv": two(r1.near) + two(g1.pair) + [t1.along_z],
        "scores": two(r1.far) + [t1.along_core],
        "chunk0": two(g1.near) + two(o1.pair) + [r1.along_z],
        "chunk1": two(g1.far) + [t1.end, r1.along_core],
        "chunk2": two(o1.near) + [g1.along_z, r1.end],
        "chunk3": two(o1.far) + [g1.along_core],
        "chunk4": [o1.along_z, g1.end],
        "chunk5": [o1.along_core],
        "chunks": [o1.end, o0.begin, g0.begin],
        "steps": two(o0.pair),
        "conv_back": two(o0.near) + two(g0.pair),
        "rest_grad": [r0.begin] + two(o0.far) + two(g0.near),
        "normed_back": two(r0.pair) + [o0.along_z] + two(g0.far),
        "done": [t0.begin, g0.along_z, o0.along_core]
        + two(r0.near)
        + [t0.along_y, g0.along_core]
        + two(r0.far)
        + [r0.along_z, t0.along_z, r0.along_core, t0.along_core, o0.end, g0.end, r0.end, t0.end],
    }

    def then(name):
        for step in plan.get(name, ()):
            step()

    then("begin")
    stream[...] = tokens[...].astype(F32)
    normed[...] = rms_normed(stream[...], rows[6:7, 0:D]).astype(BF)
    which = ones_where((iota((128, INNER), 1) >> 6) == iota((128, INNER), 0))
    skip[...] = exact(heads[...], which)

    def finish(value):
        tokens_grad[...] = value.astype(BF)

    run_backward(grad, stream, normed, (w_rest, w_gate, w_out), heads, cols, seg_row, rows, skip, rest, gate, mixed,
                 (g0r, g0g, g0o), small0, finish, scan, backward, False, then)
    for each in sums + smalls:
        each.copies.finish()


def back0(grad, tokens, weights, rows, heads, cols, seg_row, rest, gate, mixed, grads1, small1):
    outs = tuple(shape(8, w) for w in WIDTHS) + (shape(8, 128),)
    buffers = []
    for width in WIDTHS:
        buffers += wide_scratch(width)
    for width in WIDTHS * 2:
        buffers += narrow_scratch(width)
    return pl.pallas_call(
        back0_kernel,
        out_shape=(shape(T, D, dtype=BF),) + outs + outs,
        in_specs=vm(16),
        out_specs=tuple(vm(9)),
        scratch_shapes=[pltpu.VMEM((4, 4, 48, w), BF) for w in WIDTHS]
        + [pltpu.VMEM((8, CONV), F32), pltpu.VMEM((T, D), F32), pltpu.VMEM((T, D), BF), pltpu.VMEM((8, INNER), F32)]
        + scan_scratch()
        + backward_scratch()
        + buffers
        + small_scratch() * 2
        + dma_pair(6 * Reduce.SENDS + 2 * SmallReduce.SENDS),
        compiler_params=pltpu.CompilerParams(collective_id=1, has_side_effects=True, vmem_limit_bytes=LIMIT),
        name="back0_and_reduce",
    )(grad, tokens, *weights, rows, heads, cols, seg_row, rest, gate, mixed, *grads1, small1)


def shards_of(norm_gain, in_weight, conv_weight, conv_bias, gate_gain, out_weight):
    taps = jnp.transpose(conv_weight, (0, 2, 1)).reshape(2, 56)
    small = jnp.concatenate([conv_bias, taps, gate_gain, norm_gain, jnp.zeros((2, 40), BF)], axis=1)
    tile = jnp.concatenate([small[:, None, :], jnp.zeros((2, 5, 128), BF)], axis=1)
    rest = jnp.concatenate([in_weight[:, :, INNER:], jnp.zeros((2, 6, SMALL - CONV - HEADS), BF), tile], axis=2)

    def stacked(v):
        return jnp.concatenate([v.reshape(12, -1), jnp.zeros((4, v.shape[2]), BF)], axis=0)

    return stacked(rest), stacked(in_weight[:, :, :INNER]), stacked(jnp.transpose(out_weight, (0, 2, 1)))


def local(tokens, cotangent, segments, counts, norm_gain, in_weight, conv_weight, conv_bias, a_log, dt_bias, skip, gate_gain, out_weight):
    seg = segments.astype(F32)
    ahead = [jnp.concatenate([jnp.full((k,), -1.0, F32), seg[: T - k]]) for k in range(1, 4)]
    after = [jnp.concatenate([seg[k:], jnp.full((k,), -1.0, F32)]) for k in range(1, 4)]
    live = (jnp.arange(T, dtype=jnp.int32) < counts[0]).astype(F32)
    cols = jnp.stack([seg] + ahead + after + [live], axis=1)
    seg_row = seg[None, :]
    heads = jnp.pad(jnp.stack([a_log, dt_bias, skip], axis=1), ((0, 0), (0, 5), (0, 128 - HEADS)))
    shards = shards_of(norm_gain, in_weight, conv_weight, conv_bias, gate_gain, out_weight)
    done = block0(shards, tokens, heads[0], cols, seg_row)
    weights0, weights1, (stream, rest, gate, mixed, rows) = done[0:3], done[3:6], done[6:]
    output, gradient, *grads1, small1 = block1(stream, weights1, heads[1], cols, seg_row, cotangent)
    tokens_grad, *sums = back0(gradient, tokens, weights0, rows, heads[0], cols, seg_row, rest, gate, mixed, grads1, small1)
    rest_sum, gate_sum, out_sum, small = [jnp.stack([sums[n], sums[n + 4]]) for n in range(4)]
    return (
        output,
        tokens_grad,
        small[:, 6, 0:6],
        jnp.concatenate([gate_sum[:, 0:6], rest_sum[:, 0:6, 0 : CONV + HEADS]], axis=2),
        jnp.transpose(small[:, 1:5, 0:14], (0, 2, 1)),
        small[:, 0, 0:14],
        small[:, 7, 0:24],
        small[:, 7, 32:56],
        small[:, 7, 64:88],
        small[:, 5, 0:12],
        jnp.transpose(out_sum[:, 0:6], (0, 2, 1)),
    )


def solution(mesh):
    axis = P("fsdp")
    rows, second, third = P("fsdp", None), P(None, "fsdp"), P(None, None, "fsdp")
    middle = P(None, "fsdp", None)
    return jax.shard_map(
        local,
        mesh=mesh,
        in_specs=(rows, rows, axis, axis, second, middle, middle, second, P(), P(), P(), second, third),
        out_specs=(rows, rows, second, middle, middle, second, P(), P(), P(), second, third),
        check_vma=False,
    )
```

```python
from functools import partial

import jax
import jax.numpy as jnp
from jax import lax
from jax.experimental import pallas as pl
from jax.experimental.pallas import tpu as pltpu
from jax.sharding import PartitionSpec as P

D = 768
HEADS = 24
STATE = 128
INNER = 1536
CONV = 1792
T = 384
PART = 512
Q = 1536
STEP = 256
USED = 384
SMALL = 384
B = 512
EPS = 1e-05
F32 = jnp.float32
BF = jnp.bfloat16
HIGHEST = lax.Precision.HIGHEST
MESH = pl.DeviceIdType.MESH


def nn(a, b):
    return lax.dot_general(a, b, (((1,), (0,)), ((), ())), preferred_element_type=F32)


def nt(a, b):
    return lax.dot_general(a, b, (((1,), (1,)), ((), ())), preferred_element_type=F32)


def tn(a, b):
    return lax.dot_general(a, b, (((0,), (0,)), ((), ())), preferred_element_type=F32)


def exact(a, b):
    return lax.dot_general(a, b, (((1,), (0,)), ((), ())), precision=HIGHEST, preferred_element_type=F32)


def iota(shape, dim):
    return lax.broadcasted_iota(jnp.int32, shape, dim)


def ones_where(cond):
    return jnp.where(cond, 1.0, 0.0)


def tiles(start, width):
    if isinstance(start, int):
        return pl.ds(start, width)
    return pl.ds(pl.multiple_of(start, 128), width)


def sigmoid(v):
    return 1.0 / (1.0 + jnp.exp(-v))


def weight(w, cols):
    v = w[:, :, :, cols]
    return v.reshape(D, v.shape[-1])


def part_of(j, kind):
    return lax.div(j, 2), tiles(PART * kind + 256 * lax.rem(j, 2), 256)


def weight_chunk(wq, j, kind):
    n, cols = part_of(j, kind)
    return wq[n, :, :, :, cols].reshape(D, 256)


def put_product(g, cols, left, right):
    for n in range(2):
        v = nn(left[T * n : T * (n + 1), :], right)
        g[2 * n : 2 * n + 2, :, :, cols] = v.astype(BF).reshape(2, 4, 48, v.shape[-1])


def put_chunk(gq, j, kind, left, right):
    n, cols = part_of(j, kind)
    put_product(gq.at[n], cols, left, right)


def pack3(v):
    hi = v.astype(BF).astype(F32)
    rest = v - hi
    mid = rest.astype(BF).astype(F32)
    low = rest - mid
    return (hi + pltpu.roll(mid, 32, 1) + pltpu.roll(low, 64, 1)).astype(BF)


def unpack3(v):
    return v + pltpu.roll(v, 96, 1) + pltpu.roll(v, 64, 1)


def head_mask(shape=(T, 128)):
    return iota(shape, 1) < HEADS


def spread_matrix(j, width, shift):
    return ones_where((iota((128, width), 0) & 31) == 4 * j + (iota((128, width), 1) >> shift)).astype(BF)


UNITS = ((14, 4682), (12, 5462), (6, 10923))


def small_rows(wb, heads, rows, skip):
    pick = ones_where(iota((128, D), 1) == 6 * iota((128, D), 0)).astype(BF)
    held = nn(pick, weight(wb, tiles(SMALL, 128))).astype(BF)

    kinds = [UNITS[0] + (14 * n,) for n in range(5)] + [UNITS[1] + (70,), UNITS[2] + (82,)]

    def body(c, carry):
        channel = iota((128, 128), 1) + 128 * c
        units = [(channel * magic) >> 16 for _, magic in UNITS]
        spreads = []
        for n, (entries, _, offset) in enumerate(kinds):
            unit = units[max(n - 4, 0)]
            spreads.append(ones_where(iota((128, 128), 0) == offset + channel - unit * entries).astype(BF))
        got = nn(held, jnp.concatenate(spreads, axis=1))
        for n in range(7):
            mine = jnp.where(units[max(n - 4, 0)] == iota((128, 128), 0), got[:, 128 * n : 128 * (n + 1)], 0.0)
            rows[n : n + 1, tiles(128 * c, 128)] = jnp.sum(mine, axis=0, keepdims=True)
        return carry

    lax.fori_loop(0, 14, body, 0)
    which = ones_where((iota((128, INNER), 1) >> 6) == iota((128, INNER), 0))
    skip[...] = exact(heads[...], which)


def by_rows(body, count=12):
    size = T // count

    def step(n, carry):
        body(pl.ds(pl.multiple_of(n * size, size), size))
        return carry

    lax.fori_loop(0, count, step, 0)


def rms_normed(stream, gain, normed):
    def body(at):
        v = stream[at, :].astype(F32)
        r = lax.rsqrt(jnp.mean(v * v, axis=-1, keepdims=True) + EPS)
        normed[at, :] = (v * r * gain).astype(BF)

    by_rows(body)


def step_terms(raw, heads):
    mask = head_mask()
    rate = -jnp.exp(heads[0:1, :])
    x = jnp.where(mask, raw + heads[1:2, :], 0.0)
    step = jnp.where(mask, jnp.maximum(x, 0.0) + jnp.log1p(jnp.exp(-jnp.abs(x))), 0.0)
    return rate, x, step


def prepare_scan(raw, heads, step3, log3, log_t):
    rate, x, step = step_terms(raw, heads)
    lower = ones_where(iota((T, T), 0) >= iota((T, T), 1)).astype(BF)
    total = unpack3(nn(lower, pack3(jnp.where(head_mask(), step * rate, 0.0))))
    total = jnp.where(head_mask(), total, 0.0)
    step3[...] = pack3(step)
    log3[...] = pack3(total)
    flipped = jnp.transpose(total)
    for h in range(HEADS):
        log_t[h] = flipped[h : h + 1]


def conv_masks(cols, masks):
    for k in range(1, 7):
        masks[k - 1] = jnp.broadcast_to(ones_where(cols[:, k : k + 1] == cols[:, 0:1]), (T, 128))


def taken(src, masks, i, here):
    at = block_rows(i)
    if i == 0:
        ci = src[at, here]
        return [ci] + [pltpu.roll(ci, k, 0) * masks[k - 1, at, :] for k in range(1, 4)]
    slab = src[128 * i - 8 : 128 * (i + 1), here]
    return [slab[8:]] + [pltpu.roll(slab, k, 0)[8:] * masks[k - 1, at, :] for k in range(1, 4)]


def conv_forward(src, here, rows, channels, masks, out, there, slope=None):
    for i in range(3):
        ci = taken(src, masks, i, here)
        total = rows[0:1, channels] + ci[0] * rows[4:5, channels]
        for k in range(1, 4):
            total = total + ci[k] * rows[4 - k : 5 - k, channels]
        sg = sigmoid(total)
        out[block_rows(i), there] = total * sg
        if slope is not None:
            slope[block_rows(i), there] = sg * (1.0 + total * (1.0 - sg))


def conv_backward(src, here, rows, channels, masks, dact, slope, there, small, out, padded):
    sums = [0.0] * 5
    for i in range(3):
        ci = taken(src, masks, i, here)
        dc = dact[block_rows(i), there] * slope[block_rows(i), there]
        padded[block_rows(i), :] = dc
        for n, v in enumerate([dc] + [dc * ci[3 - m] for m in range(4)]):
            sums[n] = sums[n] + jnp.sum(v.reshape(16, 8, 128), axis=0)
    for n in range(5):
        small[n : n + 1, channels] = jnp.sum(sums[n], axis=0, keepdims=True)
    for i in range(3):
        at = block_rows(i)
        slab = padded[128 * i : 128 * (i + 1) + 8, :]
        dci = slab[:128] * rows[4:5, channels]
        for k in range(1, 4):
            dci = dci + pltpu.roll(slab, 136 - k, 0)[:128] * masks[k + 2, at, :] * rows[4 - k : 5 - k, channels]
        out[at, here] = dci.astype(BF)


def linked_pairs(cols, seg_row):
    return (cols[:, 0:1] == seg_row[0:1, :]) & (iota((T, T), 0) >= iota((T, T), 1))


def score_pass(act, cols, seg_row, scores):
    b = act[:, 0:STATE]
    c = act[:, STATE:]
    s = lax.dot_general(c, b, (((1,), (1,)), ((), ())), precision=HIGHEST, preferred_element_type=F32)
    s = jnp.where(linked_pairs(cols, seg_row), s, 0.0)
    scores[...] = s


def lane_heads(q):
    return (iota((128, 256), 1) >> 6) == q


def block_rows(i):
    return slice(128 * i, 128 * (i + 1))


def decays(at, j, log3, log_t):
    wide = nn(log3[at, :], spread_matrix(j, 512, 7))
    out = []
    for q in range(4):
        out.append(jnp.exp(jnp.minimum(wide[:, 128 * q : 128 * (q + 1)] - log_t[4 * j + q, :, at], 0.0)))
    return out


def by_head(part):
    return jnp.concatenate([jnp.where(lane_heads(q), part, 0) for q in range(4)], axis=0)


def halves(v):
    return v[:, :128] + v[:, 128:]


def dynamic_block(i):
    return pl.ds(pl.multiple_of(128 * i, 128), 128)


def value_chunk(j, values, rows, masks, x, slope=None):
    for n in range(2):
        here = tiles(j * 256 + 128 * n, 128)
        conv_forward(values, here, rows, here, masks, x, slice(128 * n, 128 * (n + 1)), slope)


def forward_chunk(j, rows, skip, gate_ref, scores, step3, log3, log_t, mixed_ref, gated, square, work):
    here = tiles(j * 256, 256)
    log_e, xd_ref, xd_low, y_ref, act = work[0], work[5], work[3], work[2], work[7]

    def inside(i, carry):
        at = dynamic_block(i)
        spread = spread_matrix(j, 256, 6)
        log_e[at, :] = nn(log3[at, :], spread)
        xd = act[at, :] * nn(step3[at, :], spread)
        xd_ref[at, :] = xd
        sc = scores[at, at]
        left = jnp.concatenate([(sc * e).astype(BF) for e in decays(at, j, log3, log_t)], axis=1)
        y_ref[at, :] = nn(left, by_head(xd.astype(BF)))
        return carry

    lax.fori_loop(0, 3, inside, 0)
    for i in range(1, 3):
        at, before = block_rows(i), slice(0, 128 * i)
        edge = log_e[128 * i - 1 : 128 * i, :]
        for k in range(i):
            part = block_rows(k)
            xd_low[part, :] = (xd_ref[part, :] * jnp.exp(jnp.minimum(edge - log_e[part, :], 0.0))).astype(BF)
        y_ref[at, :] += jnp.exp(jnp.minimum(log_e[at, :] - edge, 0.0)) * nn(scores[at, before].astype(BF), xd_low[before, :])

    def gating(i, carry):
        at = dynamic_block(i)
        mixed = y_ref[at, :] + skip[2:3, here] * act[at, :]
        mixed_ref[at, here] = mixed
        gate = gate_ref[at, here]
        u = mixed * (gate * sigmoid(gate))
        gated[at, here] = u
        square[at, :] += halves(u * u)
        return carry

    lax.fori_loop(0, 3, gating, 0)


def gate_norm(rows, gated, square, yn):
    r = lax.rsqrt(jnp.sum(square[...], axis=-1, keepdims=True) * (1.0 / INNER) + EPS)

    def gain(c, carry):
        here = tiles(c * 256, 256)
        yn[:, here] = (gated[:, here] * r * rows[5:6, here]).astype(BF)
        return carry

    lax.fori_loop(0, 6, gain, 0)


def first_backward(c, gl, wq, rows, gate_ref, mixed_ref, dyn, sum_u, sum_d):
    here = tiles(c * 256, 256)
    dyn[:, here] = nn(gl[...], weight_chunk(wq, c, 0))

    def body(i, carry):
        at = dynamic_block(i)
        gate = gate_ref[at, here]
        u = mixed_ref[at, here] * (gate * sigmoid(gate))
        sum_u[at, :] += halves(u * u)
        sum_d[at, :] += halves(u * dyn[at, here] * rows[5:6, here])
        return carry

    lax.fori_loop(0, 3, body, 0)


def norm_pull(sum_u, sum_d):
    r = lax.rsqrt(jnp.sum(sum_u[...], axis=-1, keepdims=True) * (1.0 / INNER) + EPS)
    pull = r * r * r * (jnp.sum(sum_d[...], axis=-1, keepdims=True) * (1.0 / INNER))
    sum_u[...] = jnp.broadcast_to(r, (T, 128))
    sum_d[...] = jnp.broadcast_to(pull, (T, 128))


def backward_chunk(j, rows, skip, gate_ref, values, masks, padded, scores, step3, log3, log_t, mixed_ref, dyn, sum_u, sum_d,
                   gl_t, norm_t, gq, small, dgate, dvalues, dscores, dlog, dstep, skip_sum, work):
    here = tiles(j * 256, 256)
    log_e, dm_ref, v_ref, low, dxd_ref, step_e, yn, act, slope = work
    value_chunk(j, values, rows, masks, act, slope)
    skips = skip_sum.at[0:8, 0:256]
    skips[...] = jnp.zeros((8, 256), F32)
    small[5:6, here] = jnp.zeros((1, 256), F32)

    def inside(i, carry):
        at = dynamic_block(i)
        spread = spread_matrix(j, 256, 6)
        log_e[at, :] = nn(log3[at, :], spread)
        step_e[at, :] = nn(step3[at, :], spread)
        x = act[at, :]
        xd = x * step_e[at, :]
        r, pull = sum_u[at, 0:1], sum_d[at, 0:1]
        dy = dyn[at, here]
        gate = gate_ref[at, here]
        mixed = mixed_ref[at, here]
        sg = sigmoid(gate)
        silu = gate * sg
        gain = rows[5:6, here]
        u = mixed * silu
        ur = u * r
        small[5:6, here] += jnp.sum(dy * ur, axis=0, keepdims=True)
        yn[at, :] = (ur * gain).astype(BF)
        du = r * (gain * dy) - u * pull
        dgate[at, here] = (du * mixed * (sg * (1.0 + gate * (1.0 - sg)))).astype(BF)
        dm = du * silu
        dm_ref[at, :] = dm
        skips[...] += jnp.sum((dm * x).reshape(16, 8, 256), axis=0)
        sc = scores[at, at]
        es = decays(at, j, log3, log_t)
        ws = [(sc * e).astype(BF) for e in es]
        part, dpart = xd.astype(BF), dm.astype(BF)
        dright = by_head(dpart)
        y = nn(jnp.concatenate(ws, axis=1), by_head(part))
        dxd = tn(jnp.concatenate(ws, axis=0), dright)
        g = nt(dright, part)
        ds = g[0:128] * es[0]
        for q in range(1, 4):
            ds = ds + g[128 * q : 128 * (q + 1)] * es[q]
        dscores[at, at] += ds
        v_ref[at, :] = dpart.astype(F32) * y - part.astype(F32) * dxd
        dxd_ref[at, :] = dxd
        return carry

    lax.fori_loop(0, 3, inside, 0)
    put_chunk(gq, j, 0, gl_t, yn[...])
    put_chunk(gq, j, 1, norm_t, dgate[:, here])
    for i in range(1, 3):
        at, before = block_rows(i), slice(0, 128 * i)
        edge = log_e[128 * i - 1 : 128 * i, :]
        for k in range(i):
            part = block_rows(k)
            low[part, :] = (act[part, :] * step_e[part, :] * jnp.exp(jnp.minimum(edge - log_e[part, :], 0.0))).astype(BF)
        de = (dm_ref[at, :] * jnp.exp(jnp.minimum(log_e[at, :] - edge, 0.0))).astype(BF)
        linked = scores[at, before].astype(BF)
        z = nn(linked, low[before, :])
        dscores[at, before] += nt(de, low[before, :])
        v_ref[at, :] += de.astype(F32) * z
        for k in range(i):
            part = block_rows(k)
            dz = tn(linked[:, part], de)
            v_ref[part, :] -= low[part, :].astype(F32) * dz
            dxd_ref[part, :] += jnp.exp(jnp.minimum(edge - log_e[part, :], 0.0)) * dz

    def outside(i, carry):
        at = dynamic_block(i)
        dxd = dxd_ref[at, :]
        gather = ones_where(4 * j + ((iota((512, 128), 0) & 255) >> 6) == iota((512, 128), 1)).astype(BF)

        def head_sums(a):
            hi = a.astype(BF)
            return nn(jnp.concatenate([hi, (a - hi.astype(F32)).astype(BF)], axis=1), gather)

        dlog[at, :] += head_sums(v_ref[at, :])
        dstep[at, :] += head_sums(act[at, :] * dxd)
        dxd_ref[at, :] = step_e[at, :] * dxd + skip[2:3, here] * dm_ref[at, :]
        return carry

    lax.fori_loop(0, 3, outside, 0)
    which = ones_where(4 * j + (iota((256, 128), 0) >> 6) == iota((256, 128), 1))
    skip_sum[8:16, 0:128] += exact(skips[...], which)
    for n in range(2):
        there = tiles(j * 256 + 128 * n, 128)
        conv_backward(values, there, rows, there, masks, dxd_ref, slope, slice(128 * n, 128 * (n + 1)), small, dvalues, padded)
    put_chunk(gq, j, 2, norm_t, dvalues[:, here])


def scores_backward(act, cols, seg_row, dscores, dact):
    ds = jnp.where(linked_pairs(cols, seg_row), dscores[...], 0.0).astype(BF)
    b = act[:, 0:STATE].astype(BF)
    c = act[:, STATE:].astype(BF)
    dact[:, 0:STATE] = tn(ds, c)
    dact[:, STATE:] = nn(ds, b)


def steps_backward(raw, heads, dlog, dstep, drest, small, skip_sum):
    rate, x, step = step_terms(raw, heads)
    upper = ones_where(iota((T, T), 0) <= iota((T, T), 1)).astype(BF)
    dsum = unpack3(nn(upper, pack3(dlog[...])))
    dsum = jnp.where(head_mask(), dsum, 0.0)
    dx = jnp.where(head_mask(), (dstep[...] + rate * dsum) * sigmoid(x), 0.0)
    drest[:, STEP:USED] = dx.astype(BF)
    rates = jnp.sum(dsum * step, axis=0, keepdims=True) * jnp.where(head_mask((1, 128)), rate, 0.0)
    biases = jnp.sum(dx, axis=0, keepdims=True)
    skips = jnp.sum(skip_sum[8:16, 0:128], axis=0, keepdims=True)
    small[7:8, 0:128] = rates + pltpu.roll(biases, 32, 1) + pltpu.roll(skips, 64, 1)


def normed_backward(dgate, dvalues, db, wq, wb, dn):
    for n in range(2):
        half = slice(2 * n, 2 * n + 2)
        total = nt(db[...], wb[half, :, :, 0:USED].reshape(T, USED))
        for s in range(3):
            cols = slice(PART * s, PART * (s + 1))
            total += nt(dgate[:, cols], wq[s, half, :, :, PART : 2 * PART].reshape(T, PART))
            total += nt(dvalues[:, cols], wq[s, half, :, :, 2 * PART :].reshape(T, PART))
        dn[:, T * n : T * (n + 1)] = total


def stream_backward(dn, stream, gain, grad, small, give):
    small[6:7, 0:D] = jnp.zeros((1, D), F32)

    def body(at):
        v, d = stream[at, :].astype(F32), dn[at, 0:D]
        r = lax.rsqrt(jnp.mean(v * v, axis=-1, keepdims=True) + EPS)
        small[6:7, 0:D] += jnp.sum(d * v * r, axis=0, keepdims=True)
        gd = gain * d
        give(at, grad[at, :] + r * gd - v * (r * r * r * jnp.mean(v * gd, axis=-1, keepdims=True)))

    by_rows(body)


class Place:
    def __init__(self):
        me = lax.axis_index("fsdp")
        self.me = me
        self.x = lax.div(me, 32)
        self.y = lax.rem(lax.div(me, 8), 4)
        self.z = lax.rem(lax.div(me, 2), 4)
        self.c = lax.rem(me, 2)

    def at(self, dx=0, dy=0, dz=0, dc=0):
        x = lax.rem(self.x + dx, 4)
        y = lax.rem(self.y + dy, 4)
        z = lax.rem(self.z + dz, 4)
        c = lax.rem(self.c + dc, 2)
        return ((x * 4 + y) * 4 + z) * 2 + c

    def along(self, axis, step):
        return self.at(dx=step) if axis == 0 else self.at(dy=step)

    def half(self, core, size, color=0, colors=1):
        return pl.ds(pl.multiple_of(core * size + color * (size // 2), 128), size // colors)


def greet(places):
    barrier = pltpu.get_barrier_semaphore()
    for place in places:
        pl.semaphore_signal(barrier, inc=1, device_id=(place,), device_id_type=MESH)
    pl.semaphore_wait(barrier, len(places))


class Semaphores:
    def __init__(self, send, recv):
        self.send, self.recv, self.count = send, recv, 0

    def next(self):
        self.count += 1
        return self.send.at[self.count - 1], self.recv.at[self.count - 1]


class Copies:
    def __init__(self, semaphores):
        self.semaphores, self.made, self.over = semaphores, {}, set()

    def make(self, name, src, dst, device):
        send, recv = self.semaphores.next()
        self.made[name] = pltpu.make_async_remote_copy(
            src_ref=src, dst_ref=dst, send_sem=send, recv_sem=recv, device_id=(device,), device_id_type=MESH
        )

    def start(self, *name):
        self.made[name].start()

    def got(self, *name):
        self.made[name].wait_recv()

    def sent(self, *name):
        self.made[name].wait_send()
        self.over.add(name)

    def finish(self):
        for name in self.made:
            if name not in self.over:
                self.sent(*name)


STEPS = (1, 3, 2)
OFFSETS = (0, 3, 1, 2)
GROUP = [(dz, dc) for dz in (1, 3, 2, 0) for dc in (0, 1) if (dz, dc) != (0, 0)]


class GatherGroup:
    def __init__(self, at, shard, room, semaphores):
        self.at, self.shard, self.size = at, shard, room.shape[3]
        self.slots = room.at[0:2, :, 0:16, :]
        self.mine = (lax.div(at.z, 2), lax.rem(at.z, 2) * 2 + at.c)
        self.copies = Copies(semaphores)
        for dz, dc in GROUP:
            core = lax.rem(at.c + dc, 2)
            self.copies.make((dz, dc), shard.at[:, at.half(core, self.size)], self.slots.at[self.mine], at.at(dz=dz, dc=dc))

    def begin(self):
        for name in GROUP:
            self.copies.start(*name)
        self.slots[self.mine] = self.shard[:, self.at.half(self.at.c, self.size)]

    def end(self, first, second):
        for name in GROUP:
            self.copies.got(*name)
        row, k = iota((96, 128), 0), iota((96, 128), 1)
        within = k & 15
        block = jnp.where(within >= 6, 1, 0)
        aim = block * 48 + (k >> 4) * 6 + within - 6 * block
        select = ones_where((row == aim) & (within < 12)).astype(BF)
        got = nn(select, self.slots[...].reshape(128, self.size)).astype(BF)
        at = self.at
        first[at.x, at.y, :, at.half(at.c, self.size)] = got[:48]
        second[at.x, at.y, :, at.half(at.c, self.size)] = got[48:]


class GatherPlane:
    SENDS = 20

    def __init__(self, at, w, semaphores):
        self.copies = c = Copies(semaphores)
        size = w.shape[3] // 2
        for color in range(2):
            cols = at.half(at.c, size, color, 2)
            own = w.at[at.x, at.y, :, cols]
            for step in STEPS:
                c.make(("a", color, step), own, own, at.along(color, step))
            for o in OFFSETS:
                line = w.at[:, lax.rem(at.y + o, 4), :, cols] if color == 0 else w.at[lax.rem(at.x + o, 4), :, :, cols]
                if o == 0:
                    for step in STEPS:
                        c.make(("c", color, step), line, line, at.along(1 - color, step))
                c.make(("p", color, o), line, line, at.at(dc=1))

    def begin(self):
        for step in STEPS:
            for color in range(2):
                self.copies.start("a", color, step)

    def near(self):
        for color in range(2):
            for step in STEPS:
                self.copies.got("a", color, step)
            for step in STEPS:
                self.copies.start("c", color, step)
            self.copies.start("p", color, 0)

    def far(self):
        for step in STEPS:
            for color in range(2):
                self.copies.got("c", color, step)
                self.copies.start("p", color, 4 - step)

    def end(self):
        for o in OFFSETS:
            for color in range(2):
                self.copies.got("p", color, o)


def plus(a, b):
    return a.astype(F32) + b.astype(F32)


class Reduce:
    SENDS = 18

    def __init__(self, at, g, out, scratch, semaphores):
        self.h, self.rb, self.rb1, self.zs, self.zr, self.xs = scratch
        self.at, self.g, self.out = at, g, out
        self.size = g.shape[3] // 2
        self.copies = c = Copies(semaphores)
        other = lax.rem(at.c + 1, 2)
        for color in range(2):
            cols = self.here(color)
            c.make(("p", color), g.at[:, :, :, at.half(other, self.size, color, 2)], self.h.at[:, :, :, cols], at.at(dc=1))
            for step in STEPS:
                c.make(("a", color, step), self.rows(color, step), self.rb.at[color, step - 1], at.along(color, step))
                c.make(("d", color, step), self.block(color, step), self.rb1.at[color, step - 1], at.along(1 - color, step))
        for dz in STEPS:
            c.make(("z", dz), self.zs.at[lax.rem(at.z + dz, 4)], self.zr.at[at.z], at.at(dz=dz))
        c.make(("x",), self.xs, out.at[:, at.half(at.c, self.size)], at.at(dc=1))

    def here(self, color):
        return pl.ds(color * (self.size // 2), self.size // 2)

    def rows(self, color, o):
        if color == 0:
            return self.h.at[lax.rem(self.at.x + o, 4), :, :, self.here(color)]
        return self.h.at[:, lax.rem(self.at.y + o, 4), :, self.here(color)]

    def block(self, color, o):
        dx, dy = (0, o) if color == 0 else (o, 0)
        return self.h.at[lax.rem(self.at.x + dx, 4), lax.rem(self.at.y + dy, 4), :, self.here(color)]

    def begin(self):
        for color in range(2):
            self.copies.start("p", color)

    def pair(self, color):
        at = self.at
        self.copies.got("p", color)
        cols = self.here(color)

        def add(n, carry):
            x, y = lax.div(n, 4), lax.rem(n, 4)
            own = self.g[x, y, :, at.half(at.c, self.size, color, 2)]
            self.h[x, y, :, cols] = plus(own, self.h[x, y, :, cols]).astype(BF)
            return carry

        lax.fori_loop(0, 16, add, 0)
        for step in STEPS:
            self.copies.start("a", color, step)

    def near(self, color):
        for step in STEPS:
            self.copies.got("a", color, step)
        cols = self.here(color)

        def add(n, carry):
            x, y = (self.at.x, n) if color == 0 else (n, self.at.y)
            there = (x, y, slice(None), cols)
            self.h[there] = (plus(self.h[there], self.rb[color, 0, n]) + plus(self.rb[color, 1, n], self.rb[color, 2, n])).astype(BF)
            return carry

        lax.fori_loop(0, 4, add, 0)
        for step in STEPS:
            self.copies.start("d", color, step)

    def far(self, color):
        for step in STEPS:
            self.copies.got("d", color, step)
        there = self.block(color, 0)
        there[...] = (plus(there[...], self.rb1[color, 0]) + plus(self.rb1[color, 1], self.rb1[color, 2])).astype(BF)

    def along_z(self):
        at = self.at
        row, k = iota((64, 48), 0), iota((64, 48), 1)
        select = ones_where(((row & 15) < 12) & (k == 12 * (row >> 4) + (row & 15))).astype(BF)
        self.zs[...] = nn(select, self.h[at.x, at.y]).astype(BF).reshape(4, 16, self.size)
        for dz in STEPS:
            self.copies.start("z", dz)
        self.zr[at.z] = self.zs[at.z]

    def along_core(self):
        at = self.at
        for dz in STEPS:
            self.copies.got("z", dz)
        total = plus(self.zr[0], self.zr[1]) + plus(self.zr[2], self.zr[3])
        low, high = total[0:8], jnp.concatenate([total[6:12], total[0:2]], axis=0)
        core = jnp.broadcast_to(at.c, (8, self.size))
        self.xs[...] = jnp.where(core == 0, high, low)
        for color in range(2):
            for step in STEPS:
                self.copies.sent("a", color, step)
                self.copies.sent("d", color, step)
        for dz in STEPS:
            self.copies.sent("z", dz)
        self.copies.start("x")
        self.out[:, at.half(at.c, self.size)] = jnp.where(core == 0, low, high)

    def end(self):
        self.copies.got("x")
        self.copies.sent("x")


class SmallReduce:
    SENDS = 10

    def __init__(self, at, small, out, scratch, semaphores):
        self.at, self.small, self.out = at, small, out
        self.sx, self.sy, self.sz, self.sc = scratch
        self.copies = c = Copies(semaphores)
        for d in STEPS:
            c.make(("sx", d), self.sx.at[at.x], self.sx.at[at.x], at.at(dx=d))
            c.make(("sy", d), self.sy.at[at.y], self.sy.at[at.y], at.at(dy=d))
            c.make(("sz", d), self.sz.at[at.z], self.sz.at[at.z], at.at(dz=d))
        c.make(("sc",), self.sc.at[at.c], self.sc.at[at.c], at.at(dc=1))

    def begin(self):
        self.sx[self.at.x] = self.small[...]
        for d in STEPS:
            self.copies.start("sx", d)

    def step(self, name, here, following, index):
        for d in STEPS:
            self.copies.got(name, d)
        following[index] = (here[0] + here[1]) + (here[2] + here[3])

    def along_y(self):
        self.step("sx", self.sx, self.sy, self.at.y)
        for d in STEPS:
            self.copies.start("sy", d)

    def along_z(self):
        self.step("sy", self.sy, self.sz, self.at.z)
        for d in STEPS:
            self.copies.start("sz", d)

    def along_core(self):
        self.step("sz", self.sz, self.sc, self.at.c)
        self.copies.start("sc")

    def end(self):
        self.copies.got("sc")
        for name in list(self.copies.made):
            self.copies.sent(*name)
        total = self.sc[0] + self.sc[1]

        self.sc[0] = total

        def own(entries, width):
            def part(n, sums):
                pick = (iota((128, 128), 0) + 128 * n == entries * self.at.me + iota((128, 128), 1)) & (iota((128, 128), 1) < entries)
                return sums + exact(self.sc[0, :, tiles(128 * n, 128)], ones_where(pick))

            return lax.fori_loop(0, width // 128, part, jnp.zeros((8, 128), F32))

        self.out[0:5, :] = own(14, CONV)[0:5]
        self.out[5:6, :] = own(12, INNER)[5:6]
        self.out[6:7, :] = own(6, D)[6:7]
        self.out[7:8, :] = total[7:8, 0:128]


def dma_pair(count):
    return [pltpu.SemaphoreType.DMA((count,)), pltpu.SemaphoreType.DMA((count,))]


def wide_scratch(width):
    size = width // 2
    return [
        pltpu.VMEM((4, 4, 48, size), BF),
        pltpu.VMEM((2, 3, 4, 48, size // 2), BF),
        pltpu.VMEM((2, 3, 48, size // 2), BF),
    ]


def narrow_scratch(width):
    size = width // 2
    return [
        pltpu.VMEM((4, 16, size), BF),
        pltpu.VMEM((4, 16, size), BF),
        pltpu.VMEM((8, size), F32),
    ]


def small_scratch():
    return [pltpu.VMEM((4, 8, CONV), F32)] * 3 + [pltpu.VMEM((2, 8, CONV), F32)]


WIDTHS = (Q, Q, Q, B)


def vm(count):
    return [pl.BlockSpec(memory_space=pltpu.VMEM)] * count


def shape(*dims, dtype=F32):
    return jax.ShapeDtypeStruct(dims, dtype)


def whole(width):
    return shape(4, 4, 48, width, dtype=BF)


LIMIT = 63 * 1024 * 1024


def scan_scratch():
    return [
        pltpu.VMEM((T, T), F32),
        pltpu.VMEM((T, 128), BF),
        pltpu.VMEM((T, 128), BF),
        pltpu.VMEM((HEADS, 1, T), F32),
        pltpu.VMEM((6, T, 128), F32),
        pltpu.VMEM((T + 8, 128), F32),
        pltpu.VMEM((T, 256), F32),
        pltpu.VMEM((T, 256), F32),
    ] + [pltpu.VMEM((T, 256), dtype) for dtype in (F32, F32, F32, BF, F32, F32, BF, F32, F32)]


def backward_scratch():
    return [
        pltpu.VMEM((T, 128), F32),
        pltpu.VMEM((T, 128), F32),
        pltpu.VMEM((D, T), BF),
        pltpu.VMEM((D, T), BF),
        pltpu.VMEM((T, INNER), BF),
        pltpu.VMEM((T, INNER), BF),
        pltpu.VMEM((T, USED), BF),
        pltpu.VMEM((T, INNER), F32),
        pltpu.VMEM((T, T), F32),
        pltpu.VMEM((T, 128), F32),
        pltpu.VMEM((T, 128), F32),
        pltpu.VMEM((16, 256), F32),
    ]


class Plan:
    def __init__(self, prefix, steps):
        self.prefix, self.steps = prefix, steps

    def __call__(self, name):
        for step in self.steps.get(self.prefix + name, ()):
            step()

    def at_chunk(self, j):
        for n in range(6):
            if self.prefix + "chunk%d" % n in self.steps:
                pl.when(j == n)(partial(self, "chunk%d" % n))


def first_terms(rb, heads, rows, cols, seg_row, scan, then):
    scores, step3, log3, log_t, masks, padded, act, slope, *work = scan
    prepare_scan(rb[:, STEP:USED], heads, step3, log3, log_t)
    for n in range(2):
        here = slice(128 * n, 128 * (n + 1))
        conv_forward(rb, here, rows, slice(INNER + 128 * n, INNER + 128 * (n + 1)), masks, act, here, slope)
    score_pass(act, cols, seg_row, scores)
    then("scores")


def run_forward(stream, wq, wb, heads, cols, seg_row, rows, skip, rb, values, gate, mixed, following, scan, scratch, then):
    scores, step3, log3, log_t, masks, padded, act, slope, *work = scan
    normed, gated, square, yn = scratch
    small_rows(wb, heads, rows, skip)
    then("rows")
    rms_normed(stream, rows[6:7, 0:D], normed)
    rb[...] = nn(normed[...], weight(wb, pl.ds(0, USED)))
    then("normed")
    first_terms(rb, heads, rows, cols, seg_row, scan, then)
    square[...] = jnp.zeros_like(square)

    def chunk(j, carry):
        here = tiles(j * 256, 256)
        values[:, here] = nn(normed[...], weight_chunk(wq, j, 2))
        gate[:, here] = nn(normed[...], weight_chunk(wq, j, 1))
        value_chunk(j, values, rows, masks, work[7])
        forward_chunk(j, rows, skip, gate, scores, step3, log3, log_t, mixed, gated, square, work)
        then.at_chunk(j)
        return carry

    lax.fori_loop(0, 6, chunk, 0)
    gate_norm(rows, gated, square, yn)
    then("yn")
    for n in range(2):
        there = slice(T * n, T * (n + 1))
        total = stream[:, there].astype(F32)
        for s in range(3):
            total += nt(yn[:, PART * s : PART * (s + 1)], wq[s, 2 * n : 2 * n + 2, :, :, 0:PART].reshape(T, PART))
        following[:, there] = total


def run_backward(grad, stream, normed, wq, wb, heads, cols, seg_row, rows, skip, rb, values, gate, mixed, gq, gb, small, finish, scan, scratch, ready, then):
    scores, step3, log3, log_t, masks, padded, act, slope, *work = scan
    sum_u, sum_d, gl_t, norm_t, dgate, dvalues, db, dyn, dscores, dlog, dstep, skip_sum = scratch

    def lower(at):
        gl[at, :] = grad[at, :].astype(BF)

    norm_t[...] = jnp.transpose(normed[...])
    gl = normed
    by_rows(lower)
    gl_t[...] = jnp.transpose(gl[...])
    for ref in (small, sum_u, sum_d, dscores, dlog, dstep, skip_sum):
        ref[...] = jnp.zeros_like(ref)

    def first(c, carry):
        first_backward(c, gl, wq, rows, gate, mixed, dyn, sum_u, sum_d)
        return carry

    lax.fori_loop(0, 6, first, 0)
    then("first")
    if not ready:
        first_terms(rb, heads, rows, cols, seg_row, scan, then)
    norm_pull(sum_u, sum_d)

    def chunk(j, carry):
        backward_chunk(j, rows, skip, gate, values, masks, padded, scores, step3, log3, log_t, mixed, dyn, sum_u, sum_d,
                       gl_t, norm_t, gq, small, dgate, dvalues, dscores, dlog, dstep, skip_sum, work)
        then.at_chunk(j)
        return carry

    lax.fori_loop(0, 6, chunk, 0)
    then("chunks")
    dact = work[0]
    scores_backward(act, cols, seg_row, dscores, dact)
    steps_backward(rb[:, STEP:USED], heads, dlog, dstep, db, small, skip_sum)
    then("steps")
    for n in range(2):
        here = slice(128 * n, 128 * (n + 1))
        conv_backward(rb, here, rows, slice(INNER + 128 * n, INNER + 128 * (n + 1)), masks, dact, slope, here, small, db, padded)
    put_product(gb, pl.ds(0, USED), norm_t, db[...])
    gb[:, :, :, USED:] = jnp.zeros((4, 4, 48, 128), BF)
    then("b_grad")
    normed_backward(dgate, dvalues, db, wq, wb, dyn)
    then("normed_back")
    stream_backward(dyn, stream, rows[6:7, 0:D], grad, small, finish)
    then("done")


def whole_kernel(shard_b, shard_q, tokens, cotangent, heads, cols, seg_row,
                 output, tokens_grad, ob0, oq0, s0, ob1, oq1, s1, far_rb, far_values, far_gate, far_mixed,
                 wb0, wq0, wb1, wq1, gb1, gq1,
                 second, grad, rb, values, gate, mixed, rows0, rows1, skip0, skip1, small0, small1, normed, square, local_sem, *scratch):
    places = iter(scratch)
    take = lambda n: [next(places) for _ in range(n)]
    scan, backward = take(17), take(12)
    dgate, dyn = backward[4], backward[7]
    forward = (normed, dyn, square, dgate)
    wide = [take(3) for _ in range(4)]
    narrow = [take(3) for _ in range(4)]
    sums_by_axis = take(4)
    semaphores = Semaphores(*take(2))
    at = Place()
    greet([at.at(dx=d) for d in STEPS] + [at.at(dy=d) for d in STEPS] + [at.at(dz=dz, dc=dc) for dz, dc in GROUP])

    parts = range(3)
    ab, *aq = groups = [GatherGroup(at, s, t, semaphores) for s, t in [(shard_b, wide[3][0])] + [(shard_q.at[n], wide[n][0]) for n in parts]]
    b0, x0, y0, z0, b1, x1, y1, z1 = planes = [
        GatherPlane(at, w, semaphores) for wb, wq in ((wb0, wq0), (wb1, wq1)) for w in [wb] + [wq.at[n] for n in parts]
    ]
    def sums_of(gb, gq, ob, oq):
        pairs = [(gq.at[n], oq.at[n]) for n in parts] + [(gb, ob)]
        return [Reduce(at, g, o, wide[n] + narrow[n], semaphores) for n, (g, o) in enumerate(pairs)]

    X1, Y1, Z1, B1 = sums1 = sums_of(gb1, gq1, ob1, oq1)
    X0, Y0, Z0, B0 = sums0 = sums_of(wb1, wq1, ob0, oq0)
    S1, S0 = [SmallReduce(at, *v, semaphores) for v in ((small1, s1, sums_by_axis), (small0, s0, sums_by_axis))]

    def two(step):
        return [partial(step, 0), partial(step, 1)]

    away, back = [], []
    for n, (near, far) in enumerate(((rb, far_rb), (values, far_values), (gate, far_gate), (mixed, far_mixed))):
        away.append(pltpu.make_async_copy(near, far, local_sem.at[n]))
        back.append(pltpu.make_async_copy(far, near, local_sem.at[4 + n]))

    steps = {
        "f0.rows": [x0.near, y0.begin],
        "f0.normed": [z0.begin, y0.near],
        "f0.scores": [away[0].start, x0.far, z0.near, x0.end],
        "f0.chunk0": [b1.begin, x1.begin],
        "f0.chunk1": [y0.far, b1.near, y0.end],
        "f0.chunk2": [y1.begin, x1.near, b1.far],
        "f0.chunk3": [z0.far, z1.begin, z0.end],
        "f0.chunk4": [b1.end, y1.near],
        "f0.chunk5": [x1.far, z1.near],
        "f0.yn": [each.start for each in away[1:]],
        "f1.begin": [away[0].wait],
        "f1.scores": [each.wait for each in away[1:]] + [x1.end],
        "f1.chunk0": [y1.far],
        "f1.chunk1": [y1.end],
        "f1.chunk2": [z1.far],
        "f1.chunk3": [z1.end],
        "b1.first": [each.copies.finish for each in groups + planes],
        "b1.chunk1": [X1.begin],
        "b1.chunk2": two(X1.pair),
        "b1.chunk3": [Y1.begin] + two(X1.near),
        "b1.chunk4": two(Y1.pair) + two(X1.far),
        "b1.chunk5": [Z1.begin] + two(Y1.near) + [X1.along_z],
        "b1.chunks": [each.start for each in back[1:]],
        "b1.steps": two(Z1.pair) + [X1.along_core],
        "b1.b_grad": [back[0].start, B1.begin] + two(Y1.far),
        "b1.normed_back": two(B1.pair) + two(Z1.near) + [Y1.along_z, X1.end],
        "b1.done": [each.wait for each in back] + two(B1.near) + two(Z1.far) + [Y1.along_core, S1.begin],
        "b0.first": two(B1.far) + [Z1.along_z, Y1.end, S1.along_y],
        "b0.scores": [B1.along_z, Z1.along_core, S1.along_z],
        "b0.chunk0": [B1.along_core, Z1.end, S1.along_core],
        "b0.chunk1": [B1.end, S1.end, X0.begin],
        "b0.chunk2": two(X0.pair),
        "b0.chunk3": [Y0.begin] + two(X0.near),
        "b0.chunk4": two(Y0.pair) + two(X0.far),
        "b0.chunk5": [Z0.begin] + two(Y0.near) + [X0.along_z],
        "b0.steps": two(Z0.pair) + [X0.along_core],
        "b0.b_grad": [B0.begin] + two(Y0.far),
        "b0.normed_back": two(B0.pair) + two(Z0.near) + [Y0.along_z, X0.end],
        "b0.done": [S0.begin]
        + two(B0.near)
        + two(Z0.far)
        + [Y0.along_core, S0.along_y]
        + two(B0.far)
        + [Z0.along_z, S0.along_z, B0.along_z, Y0.end, Z0.along_core, S0.along_core, B0.along_core, Z0.end, B0.end, S0.end],
    }

    ab.begin()
    for each in aq:
        each.begin()
    conv_masks(cols, scan[4])
    scan[5][T:, :] = jnp.zeros((8, 128), F32)
    ab.end(wb0, wb1)
    b0.begin()
    aq[0].end(wq0.at[0], wq1.at[0])
    x0.begin()
    b0.near()
    for n in (1, 2):
        aq[n].end(wq0.at[n], wq1.at[n])
    b0.far()
    b0.end()

    head0, head1 = heads.at[0], heads.at[1]
    run_forward(tokens, wq0, wb0, head0, cols, seg_row, rows0, skip0, rb, values, gate, mixed, second, scan, forward, Plan("f0.", steps))
    Plan("f1.", steps)("begin")
    run_forward(second, wq1, wb1, head1, cols, seg_row, rows1, skip1, rb, values, gate, mixed, grad, scan, forward, Plan("f1.", steps))

    def turn(at):
        live = cols[at, 7:8]
        output[at, :] = (grad[at, :] * live).astype(BF)
        grad[at, :] = cotangent[at, :].astype(F32) * live

    by_rows(turn)

    def keep(at, value):
        grad[at, :] = value

    run_backward(grad, second, normed, wq1, wb1, head1, cols, seg_row, rows1, skip1, rb, values, gate, mixed,
                 gq1, gb1, small1, keep, scan, backward, True, Plan("b1.", steps))
    rms_normed(tokens, rows0[6:7, 0:D], normed)

    def give(at, value):
        tokens_grad[at, :] = value.astype(BF)

    run_backward(grad, tokens, normed, wq0, wb0, head0, cols, seg_row, rows0, skip0, rb, values, gate, mixed,
                 wq1, wb1, small0, give, scan, backward, False, Plan("b0.", steps))
    for each in sums1 + sums0 + [S1, S0]:
        each.copies.finish()


SENDS = 4 * 7 + 8 * GatherPlane.SENDS + 8 * Reduce.SENDS + 2 * SmallReduce.SENDS


def two_blocks(shards, tokens, cotangent, heads, cols, seg_row):
    outs = (shape(8, B), shape(3, 8, Q), shape(8, 128))
    wb, wq = pltpu.VMEM((4, 4, 48, B), BF), pltpu.VMEM((3, 4, 4, 48, Q), BF)
    buffers = []
    for width in WIDTHS:
        buffers += wide_scratch(width)
    for width in WIDTHS:
        buffers += narrow_scratch(width)
    return pl.pallas_call(
        whole_kernel,
        out_shape=(shape(T, D, dtype=BF), shape(T, D, dtype=BF)) + outs + outs + (shape(T, USED),) + (shape(T, INNER),) * 3,
        in_specs=vm(7),
        out_specs=tuple(vm(8)) + (pl.BlockSpec(memory_space=pl.ANY),) * 4,
        scratch_shapes=[wb, wq] * 3
        + [pltpu.VMEM((T, D), F32)] * 2
        + [pltpu.VMEM((T, USED), F32)]
        + [pltpu.VMEM((T, INNER), F32)] * 3
        + [pltpu.VMEM((8, CONV), F32)] * 2
        + [pltpu.VMEM((8, INNER), F32)] * 2
        + [pltpu.VMEM((8, CONV), F32)] * 2
        + [pltpu.VMEM((T, D), BF), pltpu.VMEM((T, 128), F32), pltpu.SemaphoreType.DMA((8,))]
        + scan_scratch()
        + backward_scratch()
        + buffers
        + small_scratch()
        + dma_pair(SENDS),
        compiler_params=pltpu.CompilerParams(collective_id=0, has_side_effects=True, vmem_limit_bytes=LIMIT),
        name="two_blocks",
    )(*shards, tokens, cotangent, heads, cols, seg_row)


def shards_of(norm_gain, in_weight, conv_weight, conv_bias, gate_gain, out_weight):
    taps = jnp.transpose(conv_weight, (0, 2, 1)).reshape(2, 56)
    small = jnp.concatenate([conv_bias, taps, gate_gain, norm_gain, jnp.zeros((2, 40), BF)], axis=1)
    tile = jnp.concatenate([small[:, None, :], jnp.zeros((2, 5, 128), BF)], axis=1)
    wide = jnp.concatenate([in_weight[:, :, INNER + INNER :], jnp.zeros((2, 6, SMALL - STEP - HEADS), BF), tile], axis=2)
    kinds = [jnp.transpose(out_weight, (0, 2, 1)), in_weight[:, :, :INNER], in_weight[:, :, INNER : 2 * INNER]]
    q = jnp.stack([v.reshape(12, 3, PART) for v in kinds], axis=2).reshape(12, 3, Q).transpose(1, 0, 2)
    return jnp.pad(wide.reshape(12, B), ((0, 4), (0, 0))), jnp.pad(q, ((0, 0), (0, 4), (0, 0)))


def local(tokens, cotangent, segments, counts, norm_gain, in_weight, conv_weight, conv_bias, a_log, dt_bias, skip, gate_gain, out_weight):
    seg = segments.astype(F32)
    ahead = [jnp.concatenate([jnp.full((k,), -1.0, F32), seg[: T - k]]) for k in range(1, 4)]
    after = [jnp.concatenate([seg[k:], jnp.full((k,), -1.0, F32)]) for k in range(1, 4)]
    live = (jnp.arange(T, dtype=jnp.int32) < counts[0]).astype(F32)
    cols = jnp.stack([seg] + ahead + after + [live], axis=1)
    seg_row = seg[None, :]
    heads = jnp.pad(jnp.stack([a_log, dt_bias, skip], axis=1), ((0, 0), (0, 5), (0, 128 - HEADS)))
    shards = shards_of(norm_gain, in_weight, conv_weight, conv_bias, gate_gain, out_weight)
    output, tokens_grad, ob0, oq0, s0, ob1, oq1, s1, *_ = two_blocks(shards, tokens, cotangent, heads, cols, seg_row)
    small = jnp.stack([s0, s1])
    sums = jnp.stack([oq0, oq1])[:, :, 0:6].reshape(2, 3, 6, 3, PART).transpose(3, 0, 2, 1, 4).reshape(3, 2, 6, INNER)
    return (
        output,
        tokens_grad,
        small[:, 6, 0:6],
        jnp.concatenate([sums[1], sums[2], jnp.stack([ob0, ob1])[:, 0:6, 0 : STEP + HEADS]], axis=2),
        jnp.transpose(small[:, 1:5, 0:14], (0, 2, 1)),
        small[:, 0, 0:14],
        small[:, 7, 0:24],
        small[:, 7, 32:56],
        small[:, 7, 64:88],
        small[:, 5, 0:12],
        jnp.transpose(sums[0], (0, 2, 1)),
    )


def solution(mesh):
    axis = P("fsdp")
    rows, second, third = P("fsdp", None), P(None, "fsdp"), P(None, None, "fsdp")
    middle = P(None, "fsdp", None)
    return jax.shard_map(
        local,
        mesh=mesh,
        in_specs=(rows, rows, axis, axis, second, middle, middle, second, P(), P(), P(), second, third),
        out_specs=(rows, rows, second, middle, middle, second, P(), P(), P(), second, third),
        check_vma=False,
    )
```

```python
from functools import partial

import jax
import jax.numpy as jnp
from jax import lax
from jax.experimental import pallas as pl
from jax.experimental.pallas import tpu as pltpu
from jax.sharding import PartitionSpec as P

D = 768
HEADS = 24
STATE = 128
INNER = 1536
CONV = 1792
T = 384
PART = 512
Q = 1536
STEP = 256
USED = 384
SMALL = 384
B = 512
EPS = 1e-05
F32 = jnp.float32
BF = jnp.bfloat16
HIGHEST = lax.Precision.HIGHEST
MESH = pl.DeviceIdType.MESH


def nn(a, b):
    return lax.dot_general(a, b, (((1,), (0,)), ((), ())), preferred_element_type=F32)


def nt(a, b):
    return lax.dot_general(a, b, (((1,), (1,)), ((), ())), preferred_element_type=F32)


def tn(a, b):
    return lax.dot_general(a, b, (((0,), (0,)), ((), ())), preferred_element_type=F32)


def exact(a, b):
    return lax.dot_general(a, b, (((1,), (0,)), ((), ())), precision=HIGHEST, preferred_element_type=F32)


def iota(shape, dim):
    return lax.broadcasted_iota(jnp.int32, shape, dim)


def ones_where(cond):
    return jnp.where(cond, 1.0, 0.0)


def tiles(start, width):
    if isinstance(start, int):
        return pl.ds(start, width)
    return pl.ds(pl.multiple_of(start, 128), width)


def sigmoid(v):
    return 1.0 / (1.0 + jnp.exp(-v))


def weight(w, cols):
    v = w[:, :, :, cols]
    return v.reshape(D, v.shape[-1])


def part_of(j, kind):
    return lax.div(j, 2), tiles(PART * kind + 256 * lax.rem(j, 2), 256)


def weight_chunk(wq, j, kind):
    n, cols = part_of(j, kind)
    return wq[n, :, :, :, cols].reshape(D, 256)


def put_product(g, cols, left, right):
    for n in range(2):
        v = nn(left[T * n : T * (n + 1), :], right)
        g[2 * n : 2 * n + 2, :, :, cols] = v.astype(BF).reshape(2, 4, 48, v.shape[-1])


def put_chunk(gq, j, kind, left, right):
    n, cols = part_of(j, kind)
    put_product(gq.at[n], cols, left, right)


def pack3(v):
    hi = v.astype(BF).astype(F32)
    rest = v - hi
    mid = rest.astype(BF).astype(F32)
    low = rest - mid
    return (hi + pltpu.roll(mid, 32, 1) + pltpu.roll(low, 64, 1)).astype(BF)


def unpack3(v):
    return v + pltpu.roll(v, 96, 1) + pltpu.roll(v, 64, 1)


def head_mask(shape=(T, 128)):
    return iota(shape, 1) < HEADS


def spread_matrix(j, width, shift):
    return ones_where((iota((128, width), 0) & 31) == 4 * j + (iota((128, width), 1) >> shift)).astype(BF)


UNITS = ((14, 4682), (12, 5462), (6, 10923))


def small_rows(wb, heads, rows, skip):
    pick = ones_where(iota((128, D), 1) == 6 * iota((128, D), 0)).astype(BF)
    held = nn(pick, weight(wb, tiles(SMALL, 128))).astype(BF)

    kinds = [UNITS[0] + (14 * n,) for n in range(5)] + [UNITS[1] + (70,), UNITS[2] + (82,)]

    def body(c, carry):
        channel = iota((128, 128), 1) + 128 * c
        units = [(channel * magic) >> 16 for _, magic in UNITS]
        spreads = []
        for n, (entries, _, offset) in enumerate(kinds):
            unit = units[max(n - 4, 0)]
            spreads.append(ones_where(iota((128, 128), 0) == offset + channel - unit * entries).astype(BF))
        got = nn(held, jnp.concatenate(spreads, axis=1))
        for n in range(7):
            mine = jnp.where(units[max(n - 4, 0)] == iota((128, 128), 0), got[:, 128 * n : 128 * (n + 1)], 0.0)
            rows[n : n + 1, tiles(128 * c, 128)] = jnp.sum(mine, axis=0, keepdims=True)
        return carry

    lax.fori_loop(0, 14, body, 0)
    which = ones_where((iota((128, INNER), 1) >> 6) == iota((128, INNER), 0))
    skip[...] = exact(heads[...], which)


def by_rows(body, count=12):
    size = T // count

    def step(n, carry):
        body(pl.ds(pl.multiple_of(n * size, size), size))
        return carry

    lax.fori_loop(0, count, step, 0)


def rms_normed(stream, gain, normed):
    def body(at):
        v = stream[at, :].astype(F32)
        r = lax.rsqrt(jnp.mean(v * v, axis=-1, keepdims=True) + EPS)
        normed[at, :] = (v * r * gain).astype(BF)

    by_rows(body)


def step_terms(raw, heads):
    mask = head_mask()
    rate = -jnp.exp(heads[0:1, :])
    x = jnp.where(mask, raw + heads[1:2, :], 0.0)
    step = jnp.where(mask, jnp.maximum(x, 0.0) + jnp.log1p(jnp.exp(-jnp.abs(x))), 0.0)
    return rate, x, step


def prepare_scan(raw, heads, step3, log3, log_t):
    rate, x, step = step_terms(raw, heads)
    lower = ones_where(iota((T, T), 0) >= iota((T, T), 1)).astype(BF)
    total = unpack3(nn(lower, pack3(jnp.where(head_mask(), step * rate, 0.0))))
    total = jnp.where(head_mask(), total, 0.0)
    step3[...] = pack3(step)
    log3[...] = pack3(total)
    flipped = jnp.transpose(total)
    for h in range(HEADS):
        log_t[h] = flipped[h : h + 1]


def slot_columns(segments, counts, cols, seg_row):
    seg = jnp.broadcast_to(segments[...].astype(F32), (8, T))
    slot, row = iota((8, T), 1), iota((8, T), 0)
    seg_row[...] = seg
    lines = seg
    for k in range(1, 4):
        lines = jnp.where(row == k, jnp.where(slot >= k, pltpu.roll(seg, k, 1), -1.0), lines)
        lines = jnp.where(row == k + 3, jnp.where(slot < T - k, pltpu.roll(seg, T - k, 1), -1.0), lines)
    lines = jnp.where(row == 7, ones_where(slot < counts[...]), lines)
    cols[...] = jnp.transpose(jnp.concatenate([lines, jnp.zeros((120, T), F32)], axis=0))


def conv_masks(cols, masks):
    for k in range(1, 7):
        masks[k - 1] = jnp.broadcast_to(ones_where(cols[:, k : k + 1] == cols[:, 0:1]), (T, 128))


def taken(src, masks, i, here):
    at = block_rows(i)
    if i == 0:
        ci = src[at, here]
        return [ci] + [pltpu.roll(ci, k, 0) * masks[k - 1, at, :] for k in range(1, 4)]
    slab = src[128 * i - 8 : 128 * (i + 1), here]
    return [slab[8:]] + [pltpu.roll(slab, k, 0)[8:] * masks[k - 1, at, :] for k in range(1, 4)]


def conv_forward(src, here, rows, channels, masks, out, there, slope=None):
    for i in range(3):
        ci = taken(src, masks, i, here)
        total = rows[0:1, channels] + ci[0] * rows[4:5, channels]
        for k in range(1, 4):
            total = total + ci[k] * rows[4 - k : 5 - k, channels]
        sg = sigmoid(total)
        out[block_rows(i), there] = total * sg
        if slope is not None:
            slope[block_rows(i), there] = sg * (1.0 + total * (1.0 - sg))


def conv_backward(src, here, rows, channels, masks, dact, slope, there, small, out, padded):
    sums = [0.0] * 5
    for i in range(3):
        ci = taken(src, masks, i, here)
        dc = dact[block_rows(i), there] * slope[block_rows(i), there]
        padded[block_rows(i), :] = dc
        for n, v in enumerate([dc] + [dc * ci[3 - m] for m in range(4)]):
            sums[n] = sums[n] + jnp.sum(v.reshape(16, 8, 128), axis=0)
    for n in range(5):
        small[n : n + 1, channels] = jnp.sum(sums[n], axis=0, keepdims=True)
    for i in range(3):
        at = block_rows(i)
        slab = padded[128 * i : 128 * (i + 1) + 8, :]
        dci = slab[:128] * rows[4:5, channels]
        for k in range(1, 4):
            dci = dci + pltpu.roll(slab, 136 - k, 0)[:128] * masks[k + 2, at, :] * rows[4 - k : 5 - k, channels]
        out[at, here] = dci.astype(BF)


def linked_pairs(cols, seg_row):
    return (cols[:, 0:1] == seg_row[0:1, :]) & (iota((T, T), 0) >= iota((T, T), 1))


def score_pass(act, cols, seg_row, scores):
    b = act[:, 0:STATE]
    c = act[:, STATE:]
    s = lax.dot_general(c, b, (((1,), (1,)), ((), ())), precision=HIGHEST, preferred_element_type=F32)
    s = jnp.where(linked_pairs(cols, seg_row), s, 0.0)
    scores[...] = s


def lane_heads(q):
    return (iota((128, 256), 1) >> 6) == q


def block_rows(i):
    return slice(128 * i, 128 * (i + 1))


def decays(at, j, log3, log_t):
    wide = nn(log3[at, :], spread_matrix(j, 512, 7))
    out = []
    for q in range(4):
        out.append(jnp.exp(jnp.minimum(wide[:, 128 * q : 128 * (q + 1)] - log_t[4 * j + q, :, at], 0.0)))
    return out


def by_head(part):
    return jnp.concatenate([jnp.where(lane_heads(q), part, 0) for q in range(4)], axis=0)


def halves(v):
    return v[:, :128] + v[:, 128:]


def dynamic_block(i):
    return pl.ds(pl.multiple_of(128 * i, 128), 128)


def value_chunk(j, values, rows, masks, x, slope=None):
    for n in range(2):
        here = tiles(j * 256 + 128 * n, 128)
        conv_forward(values, here, rows, here, masks, x, slice(128 * n, 128 * (n + 1)), slope)


def forward_chunk(j, rows, skip, gate_ref, scores, step3, log3, log_t, mixed_ref, gated, square, work):
    here = tiles(j * 256, 256)
    log_e, xd_ref, xd_low, y_ref, act = work[0], work[5], work[3], work[2], work[7]

    def inside(i, carry):
        at = dynamic_block(i)
        spread = spread_matrix(j, 256, 6)
        log_e[at, :] = nn(log3[at, :], spread)
        xd = act[at, :] * nn(step3[at, :], spread)
        xd_ref[at, :] = xd
        sc = scores[at, at]
        left = jnp.concatenate([(sc * e).astype(BF) for e in decays(at, j, log3, log_t)], axis=1)
        y_ref[at, :] = nn(left, by_head(xd.astype(BF)))
        return carry

    lax.fori_loop(0, 3, inside, 0)
    for i in range(1, 3):
        at, before = block_rows(i), slice(0, 128 * i)
        edge = log_e[128 * i - 1 : 128 * i, :]
        for k in range(i):
            part = block_rows(k)
            xd_low[part, :] = (xd_ref[part, :] * jnp.exp(jnp.minimum(edge - log_e[part, :], 0.0))).astype(BF)
        y_ref[at, :] += jnp.exp(jnp.minimum(log_e[at, :] - edge, 0.0)) * nn(scores[at, before].astype(BF), xd_low[before, :])

    def gating(i, carry):
        at = dynamic_block(i)
        mixed = y_ref[at, :] + skip[2:3, here] * act[at, :]
        mixed_ref[at, here] = mixed
        gate = gate_ref[at, here]
        u = mixed * (gate * sigmoid(gate))
        gated[at, here] = u
        square[at, :] += halves(u * u)
        return carry

    lax.fori_loop(0, 3, gating, 0)


def gate_norm(rows, gated, square, yn):
    r = lax.rsqrt(jnp.sum(square[...], axis=-1, keepdims=True) * (1.0 / INNER) + EPS)

    def gain(c, carry):
        here = tiles(c * 256, 256)
        yn[:, here] = (gated[:, here] * r * rows[5:6, here]).astype(BF)
        return carry

    lax.fori_loop(0, 6, gain, 0)


def first_backward(c, gl, wq, rows, gate_ref, mixed_ref, dyn, sum_u, sum_d):
    here = tiles(c * 256, 256)
    dyn[:, here] = nn(gl[...], weight_chunk(wq, c, 0))

    def body(i, carry):
        at = dynamic_block(i)
        gate = gate_ref[at, here]
        u = mixed_ref[at, here] * (gate * sigmoid(gate))
        sum_u[at, :] += halves(u * u)
        sum_d[at, :] += halves(u * dyn[at, here] * rows[5:6, here])
        return carry

    lax.fori_loop(0, 3, body, 0)


def norm_pull(sum_u, sum_d):
    r = lax.rsqrt(jnp.sum(sum_u[...], axis=-1, keepdims=True) * (1.0 / INNER) + EPS)
    pull = r * r * r * (jnp.sum(sum_d[...], axis=-1, keepdims=True) * (1.0 / INNER))
    sum_u[...] = jnp.broadcast_to(r, (T, 128))
    sum_d[...] = jnp.broadcast_to(pull, (T, 128))


def backward_chunk(j, rows, skip, gate_ref, values, masks, padded, scores, step3, log3, log_t, mixed_ref, dyn, sum_u, sum_d,
                   gl_t, norm_t, gq, small, dgate, dvalues, dscores, dlog, dstep, skip_sum, work):
    here = tiles(j * 256, 256)
    log_e, dm_ref, v_ref, low, dxd_ref, step_e, yn, act, slope = work
    value_chunk(j, values, rows, masks, act, slope)
    skips = skip_sum.at[0:8, 0:256]
    skips[...] = jnp.zeros((8, 256), F32)
    small[5:6, here] = jnp.zeros((1, 256), F32)

    def inside(i, carry):
        at = dynamic_block(i)
        spread = spread_matrix(j, 256, 6)
        log_e[at, :] = nn(log3[at, :], spread)
        step_e[at, :] = nn(step3[at, :], spread)
        x = act[at, :]
        xd = x * step_e[at, :]
        r, pull = sum_u[at, 0:1], sum_d[at, 0:1]
        dy = dyn[at, here]
        gate = gate_ref[at, here]
        mixed = mixed_ref[at, here]
        sg = sigmoid(gate)
        silu = gate * sg
        gain = rows[5:6, here]
        u = mixed * silu
        ur = u * r
        small[5:6, here] += jnp.sum(dy * ur, axis=0, keepdims=True)
        yn[at, :] = (ur * gain).astype(BF)
        du = r * (gain * dy) - u * pull
        dgate[at, here] = (du * mixed * (sg * (1.0 + gate * (1.0 - sg)))).astype(BF)
        dm = du * silu
        dm_ref[at, :] = dm
        skips[...] += jnp.sum((dm * x).reshape(16, 8, 256), axis=0)
        sc = scores[at, at]
        es = decays(at, j, log3, log_t)
        ws = [(sc * e).astype(BF) for e in es]
        part, dpart = xd.astype(BF), dm.astype(BF)
        dright = by_head(dpart)
        y = nn(jnp.concatenate(ws, axis=1), by_head(part))
        dxd = tn(jnp.concatenate(ws, axis=0), dright)
        g = nt(dright, part)
        ds = g[0:128] * es[0]
        for q in range(1, 4):
            ds = ds + g[128 * q : 128 * (q + 1)] * es[q]
        dscores[at, at] += ds
        v_ref[at, :] = dpart.astype(F32) * y - part.astype(F32) * dxd
        dxd_ref[at, :] = dxd
        return carry

    lax.fori_loop(0, 3, inside, 0)
    put_chunk(gq, j, 0, gl_t, yn[...])
    put_chunk(gq, j, 1, norm_t, dgate[:, here])
    for i in range(1, 3):
        at, before = block_rows(i), slice(0, 128 * i)
        edge = log_e[128 * i - 1 : 128 * i, :]
        for k in range(i):
            part = block_rows(k)
            low[part, :] = (act[part, :] * step_e[part, :] * jnp.exp(jnp.minimum(edge - log_e[part, :], 0.0))).astype(BF)
        de = (dm_ref[at, :] * jnp.exp(jnp.minimum(log_e[at, :] - edge, 0.0))).astype(BF)
        linked = scores[at, before].astype(BF)
        z = nn(linked, low[before, :])
        dscores[at, before] += nt(de, low[before, :])
        v_ref[at, :] += de.astype(F32) * z
        for k in range(i):
            part = block_rows(k)
            dz = tn(linked[:, part], de)
            v_ref[part, :] -= low[part, :].astype(F32) * dz
            dxd_ref[part, :] += jnp.exp(jnp.minimum(edge - log_e[part, :], 0.0)) * dz

    def outside(i, carry):
        at = dynamic_block(i)
        dxd = dxd_ref[at, :]
        gather = ones_where(4 * j + ((iota((512, 128), 0) & 255) >> 6) == iota((512, 128), 1)).astype(BF)

        def head_sums(a):
            hi = a.astype(BF)
            return nn(jnp.concatenate([hi, (a - hi.astype(F32)).astype(BF)], axis=1), gather)

        dlog[at, :] += head_sums(v_ref[at, :])
        dstep[at, :] += head_sums(act[at, :] * dxd)
        dxd_ref[at, :] = step_e[at, :] * dxd + skip[2:3, here] * dm_ref[at, :]
        return carry

    lax.fori_loop(0, 3, outside, 0)
    which = ones_where(4 * j + (iota((256, 128), 0) >> 6) == iota((256, 128), 1))
    skip_sum[8:16, 0:128] += exact(skips[...], which)
    for n in range(2):
        there = tiles(j * 256 + 128 * n, 128)
        conv_backward(values, there, rows, there, masks, dxd_ref, slope, slice(128 * n, 128 * (n + 1)), small, dvalues, padded)
    put_chunk(gq, j, 2, norm_t, dvalues[:, here])


def scores_backward(act, cols, seg_row, dscores, dact):
    ds = jnp.where(linked_pairs(cols, seg_row), dscores[...], 0.0).astype(BF)
    b = act[:, 0:STATE].astype(BF)
    c = act[:, STATE:].astype(BF)
    dact[:, 0:STATE] = tn(ds, c)
    dact[:, STATE:] = nn(ds, b)


def steps_backward(raw, heads, dlog, dstep, drest, small, skip_sum):
    rate, x, step = step_terms(raw, heads)
    upper = ones_where(iota((T, T), 0) <= iota((T, T), 1)).astype(BF)
    dsum = unpack3(nn(upper, pack3(dlog[...])))
    dsum = jnp.where(head_mask(), dsum, 0.0)
    dx = jnp.where(head_mask(), (dstep[...] + rate * dsum) * sigmoid(x), 0.0)
    drest[:, STEP:USED] = dx.astype(BF)
    rates = jnp.sum(dsum * step, axis=0, keepdims=True) * jnp.where(head_mask((1, 128)), rate, 0.0)
    biases = jnp.sum(dx, axis=0, keepdims=True)
    skips = jnp.sum(skip_sum[8:16, 0:128], axis=0, keepdims=True)
    small[7:8, 0:128] = rates + pltpu.roll(biases, 32, 1) + pltpu.roll(skips, 64, 1)


def normed_backward(dgate, dvalues, db, wq, wb, dn):
    for n in range(2):
        half = slice(2 * n, 2 * n + 2)
        total = nt(db[...], wb[half, :, :, 0:USED].reshape(T, USED))
        for s in range(3):
            cols = slice(PART * s, PART * (s + 1))
            total += nt(dgate[:, cols], wq[s, half, :, :, PART : 2 * PART].reshape(T, PART))
            total += nt(dvalues[:, cols], wq[s, half, :, :, 2 * PART :].reshape(T, PART))
        dn[:, T * n : T * (n + 1)] = total


def stream_backward(dn, stream, gain, grad, small, give):
    small[6:7, 0:D] = jnp.zeros((1, D), F32)

    def body(at):
        v, d = stream[at, :].astype(F32), dn[at, 0:D]
        r = lax.rsqrt(jnp.mean(v * v, axis=-1, keepdims=True) + EPS)
        small[6:7, 0:D] += jnp.sum(d * v * r, axis=0, keepdims=True)
        gd = gain * d
        give(at, grad[at, :] + r * gd - v * (r * r * r * jnp.mean(v * gd, axis=-1, keepdims=True)))

    by_rows(body)


class Place:
    def __init__(self):
        me = lax.axis_index("fsdp")
        self.me = me
        self.x = lax.div(me, 32)
        self.y = lax.rem(lax.div(me, 8), 4)
        self.z = lax.rem(lax.div(me, 2), 4)
        self.c = lax.rem(me, 2)

    def at(self, dx=0, dy=0, dz=0, dc=0):
        x = lax.rem(self.x + dx, 4)
        y = lax.rem(self.y + dy, 4)
        z = lax.rem(self.z + dz, 4)
        c = lax.rem(self.c + dc, 2)
        return ((x * 4 + y) * 4 + z) * 2 + c

    def along(self, axis, step):
        return self.at(dx=step) if axis == 0 else self.at(dy=step)

    def half(self, core, size, color=0, colors=1):
        return pl.ds(pl.multiple_of(core * size + color * (size // 2), 128), size // colors)


def greet(places):
    barrier = pltpu.get_barrier_semaphore()
    for place in places:
        pl.semaphore_signal(barrier, inc=1, device_id=(place,), device_id_type=MESH)
    pl.semaphore_wait(barrier, len(places))


class Semaphores:
    def __init__(self, send, recv):
        self.send, self.recv, self.count = send, recv, 0

    def next(self):
        self.count += 1
        return self.send.at[self.count - 1], self.recv.at[self.count - 1]


class Copies:
    def __init__(self, semaphores):
        self.semaphores, self.made, self.over = semaphores, {}, set()

    def make(self, name, src, dst, device):
        send, recv = self.semaphores.next()
        self.made[name] = pltpu.make_async_remote_copy(
            src_ref=src, dst_ref=dst, send_sem=send, recv_sem=recv, device_id=(device,), device_id_type=MESH
        )

    def start(self, *name):
        self.made[name].start()

    def got(self, *name):
        self.made[name].wait_recv()

    def sent(self, *name):
        self.made[name].wait_send()
        self.over.add(name)

    def finish(self):
        for name in self.made:
            if name not in self.over:
                self.sent(*name)


STEPS = (1, 3, 2)
OFFSETS = (0, 3, 1, 2)
GROUP = [(dz, dc) for dz in (1, 3, 2, 0) for dc in (0, 1) if (dz, dc) != (0, 0)]


class GatherGroup:
    def __init__(self, at, shard, room, semaphores):
        self.at, self.shard, self.size = at, shard, room.shape[3]
        self.slots = room.at[0:2, :, 0:16, :]
        self.mine = (lax.div(at.z, 2), lax.rem(at.z, 2) * 2 + at.c)
        self.copies = Copies(semaphores)
        for dz, dc in GROUP:
            core = lax.rem(at.c + dc, 2)
            self.copies.make((dz, dc), shard.at[:, at.half(core, self.size)], self.slots.at[self.mine], at.at(dz=dz, dc=dc))

    def begin(self):
        for name in GROUP:
            self.copies.start(*name)
        self.slots[self.mine] = self.shard[:, self.at.half(self.at.c, self.size)]

    def end(self, first, second):
        for name in GROUP:
            self.copies.got(*name)
        row, k = iota((96, 128), 0), iota((96, 128), 1)
        within = k & 15
        block = jnp.where(within >= 6, 1, 0)
        aim = block * 48 + (k >> 4) * 6 + within - 6 * block
        select = ones_where((row == aim) & (within < 12)).astype(BF)
        got = nn(select, self.slots[...].reshape(128, self.size)).astype(BF)
        at = self.at
        first[at.x, at.y, :, at.half(at.c, self.size)] = got[:48]
        second[at.x, at.y, :, at.half(at.c, self.size)] = got[48:]


class GatherPlane:
    SENDS = 20

    def __init__(self, at, w, semaphores):
        self.copies = c = Copies(semaphores)
        size = w.shape[3] // 2
        for color in range(2):
            cols = at.half(at.c, size, color, 2)
            own = w.at[at.x, at.y, :, cols]
            for step in STEPS:
                c.make(("a", color, step), own, own, at.along(color, step))
            for o in OFFSETS:
                line = w.at[:, lax.rem(at.y + o, 4), :, cols] if color == 0 else w.at[lax.rem(at.x + o, 4), :, :, cols]
                if o == 0:
                    for step in STEPS:
                        c.make(("c", color, step), line, line, at.along(1 - color, step))
                c.make(("p", color, o), line, line, at.at(dc=1))

    def begin(self):
        for step in STEPS:
            for color in range(2):
                self.copies.start("a", color, step)

    def near(self):
        for color in range(2):
            for step in STEPS:
                self.copies.got("a", color, step)
            for step in STEPS:
                self.copies.start("c", color, step)
            self.copies.start("p", color, 0)

    def far(self):
        for step in STEPS:
            for color in range(2):
                self.copies.got("c", color, step)
                self.copies.start("p", color, 4 - step)

    def end(self):
        for o in OFFSETS:
            for color in range(2):
                self.copies.got("p", color, o)


def plus(a, b):
    return a.astype(F32) + b.astype(F32)


class Reduce:
    SENDS = 18

    def __init__(self, at, g, out, scratch, semaphores):
        self.h, self.rb, self.rb1, self.zs, self.zr, self.xs = scratch
        self.at, self.g, self.out = at, g, out
        self.size = g.shape[3] // 2
        self.copies = c = Copies(semaphores)
        other = lax.rem(at.c + 1, 2)
        for color in range(2):
            cols = self.here(color)
            c.make(("p", color), g.at[:, :, :, at.half(other, self.size, color, 2)], self.h.at[:, :, :, cols], at.at(dc=1))
            for step in STEPS:
                c.make(("a", color, step), self.rows(color, step), self.rb.at[color, step - 1], at.along(color, step))
                c.make(("d", color, step), self.block(color, step), self.rb1.at[color, step - 1], at.along(1 - color, step))
        for dz in STEPS:
            c.make(("z", dz), self.zs.at[lax.rem(at.z + dz, 4)], self.zr.at[at.z], at.at(dz=dz))
        c.make(("x",), self.xs, out.at[:, at.half(at.c, self.size)], at.at(dc=1))

    def here(self, color):
        return pl.ds(color * (self.size // 2), self.size // 2)

    def rows(self, color, o):
        if color == 0:
            return self.h.at[lax.rem(self.at.x + o, 4), :, :, self.here(color)]
        return self.h.at[:, lax.rem(self.at.y + o, 4), :, self.here(color)]

    def block(self, color, o):
        dx, dy = (0, o) if color == 0 else (o, 0)
        return self.h.at[lax.rem(self.at.x + dx, 4), lax.rem(self.at.y + dy, 4), :, self.here(color)]

    def begin(self):
        for color in range(2):
            self.copies.start("p", color)

    def pair(self, color):
        at = self.at
        self.copies.got("p", color)
        cols = self.here(color)

        def add(x, carry):
            self.h[x, :, :, cols] += self.g[x, :, :, at.half(at.c, self.size, color, 2)]
            return carry

        lax.fori_loop(0, 4, add, 0)
        for step in STEPS:
            self.copies.start("a", color, step)

    def near(self, color):
        for step in STEPS:
            self.copies.got("a", color, step)
        cols = self.here(color)

        def add(n, carry):
            x, y = (self.at.x, n) if color == 0 else (n, self.at.y)
            there = (x, y, slice(None), cols)
            self.h[there] = (plus(self.h[there], self.rb[color, 0, n]) + plus(self.rb[color, 1, n], self.rb[color, 2, n])).astype(BF)
            return carry

        lax.fori_loop(0, 4, add, 0)
        for step in STEPS:
            self.copies.start("d", color, step)

    def far(self, color):
        for step in STEPS:
            self.copies.got("d", color, step)
        there = self.block(color, 0)
        there[...] = (plus(there[...], self.rb1[color, 0]) + plus(self.rb1[color, 1], self.rb1[color, 2])).astype(BF)

    def along_z(self):
        at = self.at
        row, k = iota((64, 48), 0), iota((64, 48), 1)
        select = ones_where(((row & 15) < 12) & (k == 12 * (row >> 4) + (row & 15))).astype(BF)
        self.zs[...] = nn(select, self.h[at.x, at.y]).astype(BF).reshape(4, 16, self.size)
        for dz in STEPS:
            self.copies.start("z", dz)
        self.zr[at.z] = self.zs[at.z]

    def along_core(self):
        at = self.at
        for dz in STEPS:
            self.copies.got("z", dz)
        total = plus(self.zr[0], self.zr[1]) + plus(self.zr[2], self.zr[3])
        low, high = total[0:8], jnp.concatenate([total[6:12], total[0:2]], axis=0)
        core = jnp.broadcast_to(at.c, (8, self.size))
        self.xs[...] = jnp.where(core == 0, high, low)
        for color in range(2):
            for step in STEPS:
                self.copies.sent("a", color, step)
                self.copies.sent("d", color, step)
        for dz in STEPS:
            self.copies.sent("z", dz)
        self.copies.start("x")
        self.out[:, at.half(at.c, self.size)] = jnp.where(core == 0, low, high)

    def end(self):
        self.copies.got("x")
        self.copies.sent("x")


class SmallReduce:
    SENDS = 10

    def __init__(self, at, small, out, scratch, semaphores):
        self.at, self.small, self.out = at, small, out
        self.sx, self.sy, self.sz, self.sc = scratch
        self.copies = c = Copies(semaphores)
        for d in STEPS:
            c.make(("sx", d), self.sx.at[at.x], self.sx.at[at.x], at.at(dx=d))
            c.make(("sy", d), self.sy.at[at.y], self.sy.at[at.y], at.at(dy=d))
            c.make(("sz", d), self.sz.at[at.z], self.sz.at[at.z], at.at(dz=d))
        c.make(("sc",), self.sc.at[at.c], self.sc.at[at.c], at.at(dc=1))

    def begin(self):
        self.sx[self.at.x] = self.small[...]
        for d in STEPS:
            self.copies.start("sx", d)

    def step(self, name, here, following, index):
        for d in STEPS:
            self.copies.got(name, d)
        following[index] = (here[0] + here[1]) + (here[2] + here[3])

    def along_y(self):
        self.step("sx", self.sx, self.sy, self.at.y)
        for d in STEPS:
            self.copies.start("sy", d)

    def along_z(self):
        self.step("sy", self.sy, self.sz, self.at.z)
        for d in STEPS:
            self.copies.start("sz", d)

    def along_core(self):
        self.step("sz", self.sz, self.sc, self.at.c)
        self.copies.start("sc")

    def end(self):
        self.copies.got("sc")
        for name in list(self.copies.made):
            self.copies.sent(*name)
        total = self.sc[0] + self.sc[1]

        self.sc[0] = total

        def own(entries, width):
            def part(n, sums):
                pick = (iota((128, 128), 0) + 128 * n == entries * self.at.me + iota((128, 128), 1)) & (iota((128, 128), 1) < entries)
                return sums + exact(self.sc[0, :, tiles(128 * n, 128)], ones_where(pick))

            return lax.fori_loop(0, width // 128, part, jnp.zeros((8, 128), F32))

        self.out[0:5, :] = own(14, CONV)[0:5]
        self.out[5:6, :] = own(12, INNER)[5:6]
        self.out[6:7, :] = own(6, D)[6:7]
        self.out[7:8, :] = total[7:8, 0:128]


def dma_pair(count):
    return [pltpu.SemaphoreType.DMA((count,)), pltpu.SemaphoreType.DMA((count,))]


def wide_scratch(width):
    size = width // 2
    return [
        pltpu.VMEM((4, 4, 48, size), BF),
        pltpu.VMEM((2, 3, 4, 48, size // 2), BF),
        pltpu.VMEM((2, 3, 48, size // 2), BF),
    ]


def narrow_scratch(width):
    size = width // 2
    return [
        pltpu.VMEM((4, 16, size), BF),
        pltpu.VMEM((4, 16, size), BF),
        pltpu.VMEM((8, size), F32),
    ]


def small_scratch():
    return [pltpu.VMEM((4, 8, CONV), F32)] * 3 + [pltpu.VMEM((2, 8, CONV), F32)]


WIDTHS = (Q, Q, Q, B)


def vm(count):
    return [pl.BlockSpec(memory_space=pltpu.VMEM)] * count


def shape(*dims, dtype=F32):
    return jax.ShapeDtypeStruct(dims, dtype)


def whole(width):
    return shape(4, 4, 48, width, dtype=BF)


LIMIT = 63 * 1024 * 1024


def scan_scratch():
    return [
        pltpu.VMEM((T, T), F32),
        pltpu.VMEM((T, 128), BF),
        pltpu.VMEM((T, 128), BF),
        pltpu.VMEM((HEADS, 1, T), F32),
        pltpu.VMEM((6, T, 128), F32),
        pltpu.VMEM((T + 8, 128), F32),
        pltpu.VMEM((T, 256), F32),
        pltpu.VMEM((T, 256), F32),
    ] + [pltpu.VMEM((T, 256), dtype) for dtype in (F32, F32, F32, BF, F32, F32, BF, F32, F32)]


def backward_scratch():
    return [
        pltpu.VMEM((T, 128), F32),
        pltpu.VMEM((T, 128), F32),
        pltpu.VMEM((D, T), BF),
        pltpu.VMEM((D, T), BF),
        pltpu.VMEM((T, INNER), BF),
        pltpu.VMEM((T, INNER), BF),
        pltpu.VMEM((T, USED), BF),
        pltpu.VMEM((T, INNER), F32),
        pltpu.VMEM((T, T), F32),
        pltpu.VMEM((T, 128), F32),
        pltpu.VMEM((T, 128), F32),
        pltpu.VMEM((16, 256), F32),
    ]


class Plan:
    def __init__(self, prefix, steps):
        self.prefix, self.steps = prefix, steps

    def __call__(self, name):
        for step in self.steps.get(self.prefix + name, ()):
            step()

    def at_chunk(self, j):
        for n in range(6):
            if self.prefix + "chunk%d" % n in self.steps:
                pl.when(j == n)(partial(self, "chunk%d" % n))


def first_terms(rb, heads, rows, cols, seg_row, scan, then):
    scores, step3, log3, log_t, masks, padded, act, slope, *work = scan
    prepare_scan(rb[:, STEP:USED], heads, step3, log3, log_t)
    for n in range(2):
        here = slice(128 * n, 128 * (n + 1))
        conv_forward(rb, here, rows, slice(INNER + 128 * n, INNER + 128 * (n + 1)), masks, act, here, slope)
    score_pass(act, cols, seg_row, scores)
    then("scores")


def run_forward(stream, wq, wb, heads, cols, seg_row, rows, skip, rb, values, gate, mixed, following, scan, scratch, then):
    scores, step3, log3, log_t, masks, padded, act, slope, *work = scan
    normed, gated, square, yn = scratch
    small_rows(wb, heads, rows, skip)
    then("rows")
    rms_normed(stream, rows[6:7, 0:D], normed)
    rb[...] = nn(normed[...], weight(wb, pl.ds(0, USED)))
    then("normed")
    first_terms(rb, heads, rows, cols, seg_row, scan, then)
    square[...] = jnp.zeros_like(square)

    def chunk(j, carry):
        here = tiles(j * 256, 256)
        values[:, here] = nn(normed[...], weight_chunk(wq, j, 2))
        gate[:, here] = nn(normed[...], weight_chunk(wq, j, 1))
        value_chunk(j, values, rows, masks, work[7])
        forward_chunk(j, rows, skip, gate, scores, step3, log3, log_t, mixed, gated, square, work)
        then.at_chunk(j)
        return carry

    lax.fori_loop(0, 6, chunk, 0)
    gate_norm(rows, gated, square, yn)
    then("yn")
    for n in range(2):
        there = slice(T * n, T * (n + 1))
        total = stream[:, there].astype(F32)
        for s in range(3):
            total += nt(yn[:, PART * s : PART * (s + 1)], wq[s, 2 * n : 2 * n + 2, :, :, 0:PART].reshape(T, PART))
        following[:, there] = total


def run_backward(grad, stream, normed, wq, wb, heads, cols, seg_row, rows, skip, rb, values, gate, mixed, gq, gb, small, finish, scan, scratch, ready, then):
    scores, step3, log3, log_t, masks, padded, act, slope, *work = scan
    sum_u, sum_d, gl_t, norm_t, dgate, dvalues, db, dyn, dscores, dlog, dstep, skip_sum = scratch

    def lower(at):
        gl[at, :] = grad[at, :].astype(BF)

    norm_t[...] = jnp.transpose(normed[...])
    gl = normed
    by_rows(lower)
    gl_t[...] = jnp.transpose(gl[...])
    for ref in (small, sum_u, sum_d, dscores, dlog, dstep, skip_sum):
        ref[...] = jnp.zeros_like(ref)

    def first(c, carry):
        first_backward(c, gl, wq, rows, gate, mixed, dyn, sum_u, sum_d)
        return carry

    lax.fori_loop(0, 6, first, 0)
    then("first")
    if not ready:
        first_terms(rb, heads, rows, cols, seg_row, scan, then)
    norm_pull(sum_u, sum_d)

    def chunk(j, carry):
        backward_chunk(j, rows, skip, gate, values, masks, padded, scores, step3, log3, log_t, mixed, dyn, sum_u, sum_d,
                       gl_t, norm_t, gq, small, dgate, dvalues, dscores, dlog, dstep, skip_sum, work)
        then.at_chunk(j)
        return carry

    lax.fori_loop(0, 6, chunk, 0)
    then("chunks")
    dact = work[0]
    scores_backward(act, cols, seg_row, dscores, dact)
    steps_backward(rb[:, STEP:USED], heads, dlog, dstep, db, small, skip_sum)
    then("steps")
    for n in range(2):
        here = slice(128 * n, 128 * (n + 1))
        conv_backward(rb, here, rows, slice(INNER + 128 * n, INNER + 128 * (n + 1)), masks, dact, slope, here, small, db, padded)
    put_product(gb, pl.ds(0, USED), norm_t, db[...])
    gb[:, :, :, USED:] = jnp.zeros((4, 4, 48, 128), BF)
    then("b_grad")
    normed_backward(dgate, dvalues, db, wq, wb, dyn)
    then("normed_back")
    stream_backward(dyn, stream, rows[6:7, 0:D], grad, small, finish)
    then("done")


def whole_kernel(shard_b, shard_q, tokens, cotangent, a_log, dt_bias, head_skip, segments, counts,
                 output, tokens_grad, ob0, oq0, s0, ob1, oq1, s1, far_rb, far_values, far_gate, far_mixed,
                 wb0, wq0, wb1, wq1, gb1, gq1,
                 second, grad, rb, values, gate, mixed, rows0, rows1, skip0, skip1, small0, small1, normed, square, local_sem, heads, cols, seg_row, *scratch):
    places = iter(scratch)
    take = lambda n: [next(places) for _ in range(n)]
    scan, backward = take(17), take(12)
    dgate, dyn = backward[4], backward[7]
    forward = (normed, dyn, square, dgate)
    wide = [take(3) for _ in range(4)]
    narrow = [take(3) for _ in range(4)]
    sums_by_axis = take(4)
    semaphores = Semaphores(*take(2))
    at = Place()
    greet([at.at(dx=d) for d in STEPS] + [at.at(dy=d) for d in STEPS] + [at.at(dz=dz, dc=dc) for dz, dc in GROUP])

    parts = range(3)
    ab, *aq = groups = [GatherGroup(at, s, t, semaphores) for s, t in [(shard_b, wide[3][0])] + [(shard_q.at[n], wide[n][0]) for n in parts]]
    b0, x0, y0, z0, b1, x1, y1, z1 = planes = [
        GatherPlane(at, w, semaphores) for wb, wq in ((wb0, wq0), (wb1, wq1)) for w in [wb] + [wq.at[n] for n in parts]
    ]
    def sums_of(gb, gq, ob, oq):
        pairs = [(gq.at[n], oq.at[n]) for n in parts] + [(gb, ob)]
        return [Reduce(at, g, o, wide[n] + narrow[n], semaphores) for n, (g, o) in enumerate(pairs)]

    X1, Y1, Z1, B1 = sums1 = sums_of(gb1, gq1, ob1, oq1)
    X0, Y0, Z0, B0 = sums0 = sums_of(wb1, wq1, ob0, oq0)
    S1, S0 = [SmallReduce(at, *v, semaphores) for v in ((small1, s1, sums_by_axis), (small0, s0, sums_by_axis))]

    def two(step):
        return [partial(step, 0), partial(step, 1)]

    away, back = [], []
    for n, (near, far) in enumerate(((rb, far_rb), (values, far_values), (gate, far_gate), (mixed, far_mixed))):
        away.append(pltpu.make_async_copy(near, far, local_sem.at[n]))
        back.append(pltpu.make_async_copy(far, near, local_sem.at[4 + n]))

    steps = {
        "f0.rows": [y0.begin],
        "f0.normed": [z0.begin],
        "f0.scores": [away[0].start, x0.far, y0.near, x0.end],
        "f0.chunk0": [b1.begin, x1.begin, z0.near],
        "f0.chunk1": [y0.far, b1.near, y0.end],
        "f0.chunk2": [y1.begin, x1.near, b1.far],
        "f0.chunk3": [z0.far, z1.begin, z0.end],
        "f0.chunk4": [b1.end, y1.near],
        "f0.chunk5": [x1.far],
        "f0.yn": [each.start for each in away[1:]] + [z1.near],
        "f1.begin": [away[0].wait],
        "f1.rows": [y1.far],
        "f1.scores": [each.wait for each in away[1:]] + [x1.end, y1.end],
        "f1.chunk1": [z1.far],
        "f1.chunk3": [z1.end],
        "b1.first": [each.copies.finish for each in groups + planes],
        "b1.chunk1": [X1.begin],
        "b1.chunk2": two(X1.pair),
        "b1.chunk3": [Y1.begin],
        "b1.chunk4": two(X1.near) + two(Y1.pair),
        "b1.chunk5": [Z1.begin] + two(X1.far),
        "b1.chunks": [each.start for each in back[1:]],
        "b1.b_grad": [back[0].start, B1.begin],
        "b1.normed_back": two(Y1.near) + two(Z1.pair) + [X1.along_z],
        "b1.done": [each.wait for each in back] + two(Y1.far) + [X1.along_core, S1.begin],
        "b0.first": two(Z1.near) + [S1.along_y] + two(B1.pair) + [Y1.along_z, X1.end],
        "b0.chunk0": two(Z1.far) + two(B1.near) + [Y1.along_core, S1.along_z],
        "b0.chunk1": [X0.begin] + two(B1.far) + [Z1.along_z, Y1.end, S1.along_core],
        "b0.chunk2": two(X0.pair) + [Z1.along_core, B1.along_z, S1.end],
        "b0.chunk3": [Y0.begin, Z1.end, B1.along_core],
        "b0.chunk4": two(X0.near) + two(Y0.pair) + [B1.end],
        "b0.chunk5": [Z0.begin] + two(X0.far) + two(Y0.near) + [X0.along_z],
        "b0.b_grad": [B0.begin] + two(Z0.pair) + two(Y0.far),
        "b0.normed_back": two(B0.pair) + [Y0.along_z, X0.along_core],
        "b0.done": [S0.begin]
        + two(Z0.near)
        + two(B0.near)
        + [Y0.along_core, S0.along_y, X0.end]
        + two(Z0.far)
        + [Z0.along_z]
        + two(B0.far)
        + [B0.along_z, S0.along_z, Z0.along_core, B0.along_core, S0.along_core, Y0.end, Z0.end, B0.end, S0.end],
    }

    ab.begin()
    for each in aq:
        each.begin()
    heads[...] = jnp.zeros_like(heads)
    for l in range(2):
        for n, source in enumerate((a_log, dt_bias, head_skip)):
            heads[l, n : n + 1, 0:HEADS] = source[l : l + 1, :]
    slot_columns(segments, counts, cols, seg_row)
    conv_masks(cols, scan[4])
    scan[5][T:, :] = jnp.zeros((8, 128), F32)
    ab.end(wb0, wb1)
    b0.begin()
    aq[0].end(wq0.at[0], wq1.at[0])
    x0.begin()
    b0.near()
    x0.near()
    b0.far()
    for n in (1, 2):
        aq[n].end(wq0.at[n], wq1.at[n])
    b0.end()

    head0, head1 = heads.at[0], heads.at[1]
    run_forward(tokens, wq0, wb0, head0, cols, seg_row, rows0, skip0, rb, values, gate, mixed, second, scan, forward, Plan("f0.", steps))
    Plan("f1.", steps)("begin")
    run_forward(second, wq1, wb1, head1, cols, seg_row, rows1, skip1, rb, values, gate, mixed, grad, scan, forward, Plan("f1.", steps))

    def turn(at):
        live = cols[at, 7:8]
        output[at, :] = (grad[at, :] * live).astype(BF)
        grad[at, :] = cotangent[at, :].astype(F32) * live

    by_rows(turn)

    def keep(at, value):
        grad[at, :] = value

    run_backward(grad, second, normed, wq1, wb1, head1, cols, seg_row, rows1, skip1, rb, values, gate, mixed,
                 gq1, gb1, small1, keep, scan, backward, True, Plan("b1.", steps))
    rms_normed(tokens, rows0[6:7, 0:D], normed)

    def give(at, value):
        tokens_grad[at, :] = value.astype(BF)

    run_backward(grad, tokens, normed, wq0, wb0, head0, cols, seg_row, rows0, skip0, rb, values, gate, mixed,
                 wq1, wb1, small0, give, scan, backward, False, Plan("b0.", steps))
    for each in sums1 + sums0 + [S1, S0]:
        each.copies.finish()


SENDS = 4 * 7 + 8 * GatherPlane.SENDS + 8 * Reduce.SENDS + 2 * SmallReduce.SENDS


def two_blocks(shards, *rest):
    outs = (shape(8, B), shape(3, 8, Q), shape(8, 128))
    wb, wq = pltpu.VMEM((4, 4, 48, B), BF), pltpu.VMEM((3, 4, 4, 48, Q), BF)
    buffers = []
    for width in WIDTHS:
        buffers += wide_scratch(width)
    for width in WIDTHS:
        buffers += narrow_scratch(width)
    return pl.pallas_call(
        whole_kernel,
        out_shape=(shape(T, D, dtype=BF), shape(T, D, dtype=BF)) + outs + outs + (shape(T, USED),) + (shape(T, INNER),) * 3,
        in_specs=vm(9),
        out_specs=tuple(vm(8)) + (pl.BlockSpec(memory_space=pl.ANY),) * 4,
        scratch_shapes=[wb, wq] * 3
        + [pltpu.VMEM((T, D), F32)] * 2
        + [pltpu.VMEM((T, USED), F32)]
        + [pltpu.VMEM((T, INNER), F32)] * 3
        + [pltpu.VMEM((8, CONV), F32)] * 2
        + [pltpu.VMEM((8, INNER), F32)] * 2
        + [pltpu.VMEM((8, CONV), F32)] * 2
        + [pltpu.VMEM((T, D), BF), pltpu.VMEM((T, 128), F32), pltpu.SemaphoreType.DMA((8,))]
        + [pltpu.VMEM((2, 8, 128), F32), pltpu.VMEM((T, 128), F32), pltpu.VMEM((8, T), F32)]
        + scan_scratch()
        + backward_scratch()
        + buffers
        + small_scratch()
        + dma_pair(SENDS),
        compiler_params=pltpu.CompilerParams(collective_id=0, has_side_effects=True, vmem_limit_bytes=LIMIT),
        name="two_blocks",
    )(*shards, *rest)


def shards_of(norm_gain, in_weight, conv_weight, conv_bias, gate_gain, out_weight):
    taps = jnp.transpose(conv_weight, (0, 2, 1)).reshape(2, 56)
    small = jnp.concatenate([conv_bias, taps, gate_gain, norm_gain, jnp.zeros((2, 40), BF)], axis=1)
    tile = jnp.concatenate([small[:, None, :], jnp.zeros((2, 5, 128), BF)], axis=1)
    wide = jnp.concatenate([in_weight[:, :, INNER + INNER :], jnp.zeros((2, 6, SMALL - STEP - HEADS), BF), tile], axis=2)
    kinds = [jnp.transpose(out_weight, (0, 2, 1)), in_weight[:, :, :INNER], in_weight[:, :, INNER : 2 * INNER]]
    q = jnp.stack([v.reshape(12, 3, PART) for v in kinds], axis=2).reshape(12, 3, Q).transpose(1, 0, 2)
    return jnp.pad(wide.reshape(12, B), ((0, 4), (0, 0))), jnp.pad(q, ((0, 0), (0, 4), (0, 0)))


def local(tokens, cotangent, segments, counts, norm_gain, in_weight, conv_weight, conv_bias, a_log, dt_bias, skip, gate_gain, out_weight):
    shards = shards_of(norm_gain, in_weight, conv_weight, conv_bias, gate_gain, out_weight)
    output, tokens_grad, ob0, oq0, s0, ob1, oq1, s1, *_ = two_blocks(
        shards, tokens, cotangent, a_log, dt_bias, skip, segments.reshape(1, T), counts.reshape(1, 1)
    )
    small = jnp.stack([s0, s1])
    sums = jnp.stack([oq0, oq1])[:, :, 0:6].reshape(2, 3, 6, 3, PART).transpose(3, 0, 2, 1, 4).reshape(3, 2, 6, INNER)
    return (
        output,
        tokens_grad,
        small[:, 6, 0:6],
        jnp.concatenate([sums[1], sums[2], jnp.stack([ob0, ob1])[:, 0:6, 0 : STEP + HEADS]], axis=2),
        jnp.transpose(small[:, 1:5, 0:14], (0, 2, 1)),
        small[:, 0, 0:14],
        small[:, 7, 0:24],
        small[:, 7, 32:56],
        small[:, 7, 64:88],
        small[:, 5, 0:12],
        jnp.transpose(sums[0], (0, 2, 1)),
    )


def solution(mesh):
    axis = P("fsdp")
    rows, second, third = P("fsdp", None), P(None, "fsdp"), P(None, None, "fsdp")
    middle = P(None, "fsdp", None)
    return jax.shard_map(
        local,
        mesh=mesh,
        in_specs=(rows, rows, axis, axis, second, middle, middle, second, P(), P(), P(), second, third),
        out_specs=(rows, rows, second, middle, middle, second, P(), P(), P(), second, third),
        check_vma=False,
    )
```

```python
from functools import partial

import jax
import jax.numpy as jnp
from jax import lax
from jax.experimental import pallas as pl
from jax.experimental.pallas import tpu as pltpu
from jax.sharding import PartitionSpec as P

D = 768
HEADS = 24
STATE = 128
INNER = 1536
CONV = 1792
T = 384
PART = 512
Q = 1536
STEP = 256
USED = 384
SMALL = 384
B = 512
EPS = 1e-05
F32 = jnp.float32
BF = jnp.bfloat16
HIGHEST = lax.Precision.HIGHEST
MESH = pl.DeviceIdType.MESH


def nn(a, b):
    return lax.dot_general(a, b, (((1,), (0,)), ((), ())), preferred_element_type=F32)


def nt(a, b):
    return lax.dot_general(a, b, (((1,), (1,)), ((), ())), preferred_element_type=F32)


def tn(a, b):
    return lax.dot_general(a, b, (((0,), (0,)), ((), ())), preferred_element_type=F32)


def exact(a, b):
    return lax.dot_general(a, b, (((1,), (0,)), ((), ())), precision=HIGHEST, preferred_element_type=F32)


def iota(shape, dim):
    return lax.broadcasted_iota(jnp.int32, shape, dim)


def ones_where(cond):
    return jnp.where(cond, 1.0, 0.0)


def tiles(start, width):
    if isinstance(start, int):
        return pl.ds(start, width)
    return pl.ds(pl.multiple_of(start, 128), width)


def sigmoid(v):
    return 1.0 / (1.0 + jnp.exp(-v))


def weight(w, cols):
    v = w[:, :, :, cols]
    return v.reshape(D, v.shape[-1])


def part_of(j, kind):
    return lax.div(j, 2), tiles(PART * kind + 256 * lax.rem(j, 2), 256)


def weight_chunk(wq, j, kind):
    n, cols = part_of(j, kind)
    return wq[n, :, :, :, cols].reshape(D, 256)


def put_product(g, cols, left, right):
    for n in range(2):
        v = nn(left[T * n : T * (n + 1), :], right)
        g[2 * n : 2 * n + 2, :, :, cols] = v.astype(BF).reshape(2, 4, 48, v.shape[-1])


def put_chunk(gq, j, kind, left, right):
    n, cols = part_of(j, kind)
    put_product(gq.at[n], cols, left, right)


def pack3(v):
    hi = v.astype(BF).astype(F32)
    rest = v - hi
    mid = rest.astype(BF).astype(F32)
    low = rest - mid
    return (hi + pltpu.roll(mid, 32, 1) + pltpu.roll(low, 64, 1)).astype(BF)


def unpack3(v):
    return v + pltpu.roll(v, 96, 1) + pltpu.roll(v, 64, 1)


def head_mask(shape=(T, 128)):
    return iota(shape, 1) < HEADS


def spread_matrix(j, width, shift):
    return ones_where((iota((128, width), 0) & 31) == 4 * j + (iota((128, width), 1) >> shift)).astype(BF)


UNITS = ((14, 4682), (12, 5462), (6, 10923))


def small_rows(wb, heads, rows, skip):
    pick = ones_where(iota((128, D), 1) == 6 * iota((128, D), 0)).astype(BF)
    held = nn(pick, weight(wb, tiles(SMALL, 128))).astype(BF)

    kinds = [UNITS[0] + (14 * n,) for n in range(5)] + [UNITS[1] + (70,), UNITS[2] + (82,)]

    def body(c, carry):
        channel = iota((128, 128), 1) + 128 * c
        units = [(channel * magic) >> 16 for _, magic in UNITS]
        spreads = []
        for n, (entries, _, offset) in enumerate(kinds):
            unit = units[max(n - 4, 0)]
            spreads.append(ones_where(iota((128, 128), 0) == offset + channel - unit * entries).astype(BF))
        got = nn(held, jnp.concatenate(spreads, axis=1))
        for n in range(7):
            mine = jnp.where(units[max(n - 4, 0)] == iota((128, 128), 0), got[:, 128 * n : 128 * (n + 1)], 0.0)
            rows[n : n + 1, tiles(128 * c, 128)] = jnp.sum(mine, axis=0, keepdims=True)
        return carry

    lax.fori_loop(0, 14, body, 0, unroll=2)
    which = ones_where((iota((128, INNER), 1) >> 6) == iota((128, INNER), 0))
    skip[...] = exact(heads[...], which)


def by_rows(body, count=12):
    size = T // count

    def step(n, carry):
        body(pl.ds(pl.multiple_of(n * size, size), size))
        return carry

    lax.fori_loop(0, count, step, 0, unroll=3)


def rms_normed(stream, gain, normed):
    def body(at):
        v = stream[at, :].astype(F32)
        r = lax.rsqrt(jnp.mean(v * v, axis=-1, keepdims=True) + EPS)
        normed[at, :] = (v * r * gain).astype(BF)

    by_rows(body)


def step_terms(raw, heads):
    mask = head_mask()
    rate = -jnp.exp(heads[0:1, :])
    x = jnp.where(mask, raw + heads[1:2, :], 0.0)
    step = jnp.where(mask, jnp.maximum(x, 0.0) + jnp.log1p(jnp.exp(-jnp.abs(x))), 0.0)
    return rate, x, step


def prepare_scan(raw, heads, step3, log3, log_t):
    rate, x, step = step_terms(raw, heads)
    lower = ones_where(iota((T, T), 0) >= iota((T, T), 1)).astype(BF)
    total = unpack3(nn(lower, pack3(jnp.where(head_mask(), step * rate, 0.0))))
    total = jnp.where(head_mask(), total, 0.0)
    step3[...] = pack3(step)
    log3[...] = pack3(total)
    flipped = jnp.transpose(total)
    for h in range(HEADS):
        log_t[h] = flipped[h : h + 1]


def slot_columns(segments, counts, cols, seg_row):
    seg = jnp.broadcast_to(segments[...].astype(F32), (8, T))
    slot, row = iota((8, T), 1), iota((8, T), 0)
    seg_row[...] = seg
    lines = seg
    for k in range(1, 4):
        lines = jnp.where(row == k, jnp.where(slot >= k, pltpu.roll(seg, k, 1), -1.0), lines)
        lines = jnp.where(row == k + 3, jnp.where(slot < T - k, pltpu.roll(seg, T - k, 1), -1.0), lines)
    lines = jnp.where(row == 7, ones_where(slot < counts[...]), lines)
    cols[...] = jnp.transpose(jnp.concatenate([lines, jnp.zeros((120, T), F32)], axis=0))


def conv_masks(cols, masks):
    for k in range(1, 7):
        masks[k - 1] = jnp.broadcast_to(ones_where(cols[:, k : k + 1] == cols[:, 0:1]), (T, 128))


def taken(src, masks, i, here):
    at = block_rows(i)
    if i == 0:
        ci = src[at, here]
        return [ci] + [pltpu.roll(ci, k, 0) * masks[k - 1, at, :] for k in range(1, 4)]
    slab = src[128 * i - 8 : 128 * (i + 1), here]
    return [slab[8:]] + [pltpu.roll(slab, k, 0)[8:] * masks[k - 1, at, :] for k in range(1, 4)]


def conv_forward(src, here, rows, channels, masks, out, there, slope=None):
    for i in range(3):
        ci = taken(src, masks, i, here)
        total = rows[0:1, channels] + ci[0] * rows[4:5, channels]
        for k in range(1, 4):
            total = total + ci[k] * rows[4 - k : 5 - k, channels]
        sg = sigmoid(total)
        out[block_rows(i), there] = total * sg
        if slope is not None:
            slope[block_rows(i), there] = sg * (1.0 + total * (1.0 - sg))


def conv_backward(src, here, rows, channels, masks, dact, slope, there, small, out, padded):
    sums = [0.0] * 5
    for i in range(3):
        ci = taken(src, masks, i, here)
        dc = dact[block_rows(i), there] * slope[block_rows(i), there]
        padded[block_rows(i), :] = dc
        for n, v in enumerate([dc] + [dc * ci[3 - m] for m in range(4)]):
            sums[n] = sums[n] + jnp.sum(v.reshape(16, 8, 128), axis=0)
    for n in range(5):
        small[n : n + 1, channels] = jnp.sum(sums[n], axis=0, keepdims=True)
    for i in range(3):
        at = block_rows(i)
        slab = padded[128 * i : 128 * (i + 1) + 8, :]
        dci = slab[:128] * rows[4:5, channels]
        for k in range(1, 4):
            dci = dci + pltpu.roll(slab, 136 - k, 0)[:128] * masks[k + 2, at, :] * rows[4 - k : 5 - k, channels]
        out[at, here] = dci.astype(BF)


def linked_pairs(cols, seg_row):
    return (cols[:, 0:1] == seg_row[0:1, :]) & (iota((T, T), 0) >= iota((T, T), 1))


def score_pass(act, cols, seg_row, scores):
    b = act[:, 0:STATE]
    c = act[:, STATE:]
    s = lax.dot_general(c, b, (((1,), (1,)), ((), ())), precision=HIGHEST, preferred_element_type=F32)
    s = jnp.where(linked_pairs(cols, seg_row), s, 0.0)
    scores[...] = s


def lane_heads(q):
    return (iota((128, 256), 1) >> 6) == q


def block_rows(i):
    return slice(128 * i, 128 * (i + 1))


def decays(at, j, log3, log_t):
    wide = nn(log3[at, :], spread_matrix(j, 512, 7))
    out = []
    for q in range(4):
        out.append(jnp.exp(jnp.minimum(wide[:, 128 * q : 128 * (q + 1)] - log_t[4 * j + q, :, at], 0.0)))
    return out


def by_head(part):
    return jnp.concatenate([jnp.where(lane_heads(q), part, 0) for q in range(4)], axis=0)


def halves(v):
    return v[:, :128] + v[:, 128:]


def dynamic_block(i):
    return pl.ds(pl.multiple_of(128 * i, 128), 128)


def value_chunk(j, values, rows, masks, x, slope=None):
    for n in range(2):
        here = tiles(j * 256 + 128 * n, 128)
        conv_forward(values, here, rows, here, masks, x, slice(128 * n, 128 * (n + 1)), slope)


def forward_chunk(j, rows, skip, gate_ref, scores, step3, log3, log_t, mixed_ref, gated, square, work):
    here = tiles(j * 256, 256)
    log_e, xd_ref, xd_low, y_ref, act = work[0], work[5], work[3], work[2], work[7]

    def inside(i, carry):
        at = dynamic_block(i)
        spread = spread_matrix(j, 256, 6)
        log_e[at, :] = nn(log3[at, :], spread)
        xd = act[at, :] * nn(step3[at, :], spread)
        xd_ref[at, :] = xd
        sc = scores[at, at]
        left = jnp.concatenate([(sc * e).astype(BF) for e in decays(at, j, log3, log_t)], axis=1)
        y_ref[at, :] = nn(left, by_head(xd.astype(BF)))
        return carry

    lax.fori_loop(0, 3, inside, 0, unroll=True)
    for i in range(1, 3):
        at, before = block_rows(i), slice(0, 128 * i)
        edge = log_e[128 * i - 1 : 128 * i, :]
        for k in range(i):
            part = block_rows(k)
            xd_low[part, :] = (xd_ref[part, :] * jnp.exp(jnp.minimum(edge - log_e[part, :], 0.0))).astype(BF)
        y_ref[at, :] += jnp.exp(jnp.minimum(log_e[at, :] - edge, 0.0)) * nn(scores[at, before].astype(BF), xd_low[before, :])

    def gating(i, carry):
        at = dynamic_block(i)
        mixed = y_ref[at, :] + skip[2:3, here] * act[at, :]
        mixed_ref[at, here] = mixed
        gate = gate_ref[at, here]
        u = mixed * (gate * sigmoid(gate))
        gated[at, here] = u
        square[at, :] += halves(u * u)
        return carry

    lax.fori_loop(0, 3, gating, 0, unroll=True)


def gate_norm(rows, gated, square, yn):
    r = lax.rsqrt(jnp.sum(square[...], axis=-1, keepdims=True) * (1.0 / INNER) + EPS)

    def gain(c, carry):
        here = tiles(c * 256, 256)
        yn[:, here] = (gated[:, here] * r * rows[5:6, here]).astype(BF)
        return carry

    lax.fori_loop(0, 6, gain, 0)


def first_backward(c, gl, wq, rows, gate_ref, mixed_ref, dyn, sum_u, sum_d):
    here = tiles(c * 256, 256)
    dyn[:, here] = nn(gl[...], weight_chunk(wq, c, 0))

    def body(i, carry):
        at = dynamic_block(i)
        gate = gate_ref[at, here]
        u = mixed_ref[at, here] * (gate * sigmoid(gate))
        sum_u[at, :] += halves(u * u)
        sum_d[at, :] += halves(u * dyn[at, here] * rows[5:6, here])
        return carry

    lax.fori_loop(0, 3, body, 0, unroll=True)


def norm_pull(sum_u, sum_d):
    r = lax.rsqrt(jnp.sum(sum_u[...], axis=-1, keepdims=True) * (1.0 / INNER) + EPS)
    pull = r * r * r * (jnp.sum(sum_d[...], axis=-1, keepdims=True) * (1.0 / INNER))
    sum_u[...] = jnp.broadcast_to(r, (T, 128))
    sum_d[...] = jnp.broadcast_to(pull, (T, 128))


def backward_chunk(j, rows, skip, gate_ref, values, masks, padded, scores, step3, log3, log_t, mixed_ref, dyn, sum_u, sum_d,
                   gl_t, norm_t, gq, small, dgate, dvalues, dscores, dlog, dstep, skip_sum, work):
    here = tiles(j * 256, 256)
    log_e, dm_ref, v_ref, low, dxd_ref, step_e, yn, act, slope = work
    value_chunk(j, values, rows, masks, act, slope)
    skips = skip_sum.at[0:8, 0:256]
    skips[...] = jnp.zeros((8, 256), F32)
    small[5:6, here] = jnp.zeros((1, 256), F32)

    def inside(i, carry):
        at = dynamic_block(i)
        spread = spread_matrix(j, 256, 6)
        log_e[at, :] = nn(log3[at, :], spread)
        step_e[at, :] = nn(step3[at, :], spread)
        x = act[at, :]
        xd = x * step_e[at, :]
        r, pull = sum_u[at, 0:1], sum_d[at, 0:1]
        dy = dyn[at, here]
        gate = gate_ref[at, here]
        mixed = mixed_ref[at, here]
        sg = sigmoid(gate)
        silu = gate * sg
        gain = rows[5:6, here]
        u = mixed * silu
        ur = u * r
        small[5:6, here] += jnp.sum(dy * ur, axis=0, keepdims=True)
        yn[at, :] = (ur * gain).astype(BF)
        du = r * (gain * dy) - u * pull
        dgate[at, here] = (du * mixed * (sg * (1.0 + gate * (1.0 - sg)))).astype(BF)
        dm = du * silu
        dm_ref[at, :] = dm
        skips[...] += jnp.sum((dm * x).reshape(16, 8, 256), axis=0)
        sc = scores[at, at]
        es = decays(at, j, log3, log_t)
        ws = [(sc * e).astype(BF) for e in es]
        part, dpart = xd.astype(BF), dm.astype(BF)
        dright = by_head(dpart)
        y = nn(jnp.concatenate(ws, axis=1), by_head(part))
        dxd = tn(jnp.concatenate(ws, axis=0), dright)
        g = nt(dright, part)
        ds = g[0:128] * es[0]
        for q in range(1, 4):
            ds = ds + g[128 * q : 128 * (q + 1)] * es[q]
        dscores[at, at] += ds
        v_ref[at, :] = dpart.astype(F32) * y - part.astype(F32) * dxd
        dxd_ref[at, :] = dxd
        return carry

    lax.fori_loop(0, 3, inside, 0, unroll=True)
    put_chunk(gq, j, 0, gl_t, yn[...])
    put_chunk(gq, j, 1, norm_t, dgate[:, here])
    for i in range(1, 3):
        at, before = block_rows(i), slice(0, 128 * i)
        edge = log_e[128 * i - 1 : 128 * i, :]
        for k in range(i):
            part = block_rows(k)
            low[part, :] = (act[part, :] * step_e[part, :] * jnp.exp(jnp.minimum(edge - log_e[part, :], 0.0))).astype(BF)
        de = (dm_ref[at, :] * jnp.exp(jnp.minimum(log_e[at, :] - edge, 0.0))).astype(BF)
        linked = scores[at, before].astype(BF)
        z = nn(linked, low[before, :])
        dscores[at, before] += nt(de, low[before, :])
        v_ref[at, :] += de.astype(F32) * z
        for k in range(i):
            part = block_rows(k)
            dz = tn(linked[:, part], de)
            v_ref[part, :] -= low[part, :].astype(F32) * dz
            dxd_ref[part, :] += jnp.exp(jnp.minimum(edge - log_e[part, :], 0.0)) * dz

    def outside(i, carry):
        at = dynamic_block(i)
        dxd = dxd_ref[at, :]
        gather = ones_where(4 * j + ((iota((512, 128), 0) & 255) >> 6) == iota((512, 128), 1)).astype(BF)

        def head_sums(a):
            hi = a.astype(BF)
            return nn(jnp.concatenate([hi, (a - hi.astype(F32)).astype(BF)], axis=1), gather)

        dlog[at, :] += head_sums(v_ref[at, :])
        dstep[at, :] += head_sums(act[at, :] * dxd)
        dxd_ref[at, :] = step_e[at, :] * dxd + skip[2:3, here] * dm_ref[at, :]
        return carry

    lax.fori_loop(0, 3, outside, 0, unroll=True)
    which = ones_where(4 * j + (iota((256, 128), 0) >> 6) == iota((256, 128), 1))
    skip_sum[8:16, 0:128] += exact(skips[...], which)
    for n in range(2):
        there = tiles(j * 256 + 128 * n, 128)
        conv_backward(values, there, rows, there, masks, dxd_ref, slope, slice(128 * n, 128 * (n + 1)), small, dvalues, padded)
    put_chunk(gq, j, 2, norm_t, dvalues[:, here])


def scores_backward(act, cols, seg_row, dscores, dact):
    ds = jnp.where(linked_pairs(cols, seg_row), dscores[...], 0.0).astype(BF)
    b = act[:, 0:STATE].astype(BF)
    c = act[:, STATE:].astype(BF)
    dact[:, 0:STATE] = tn(ds, c)
    dact[:, STATE:] = nn(ds, b)


def steps_backward(raw, heads, dlog, dstep, drest, small, skip_sum):
    rate, x, step = step_terms(raw, heads)
    upper = ones_where(iota((T, T), 0) <= iota((T, T), 1)).astype(BF)
    dsum = unpack3(nn(upper, pack3(dlog[...])))
    dsum = jnp.where(head_mask(), dsum, 0.0)
    dx = jnp.where(head_mask(), (dstep[...] + rate * dsum) * sigmoid(x), 0.0)
    drest[:, STEP:USED] = dx.astype(BF)
    rates = jnp.sum(dsum * step, axis=0, keepdims=True) * jnp.where(head_mask((1, 128)), rate, 0.0)
    biases = jnp.sum(dx, axis=0, keepdims=True)
    skips = jnp.sum(skip_sum[8:16, 0:128], axis=0, keepdims=True)
    small[7:8, 0:128] = rates + pltpu.roll(biases, 32, 1) + pltpu.roll(skips, 64, 1)


def normed_backward(dgate, dvalues, db, wq, wb, dn):
    for n in range(2):
        half = slice(2 * n, 2 * n + 2)
        total = nt(db[...], wb[half, :, :, 0:USED].reshape(T, USED))
        for s in range(3):
            cols = slice(PART * s, PART * (s + 1))
            total += nt(dgate[:, cols], wq[s, half, :, :, PART : 2 * PART].reshape(T, PART))
            total += nt(dvalues[:, cols], wq[s, half, :, :, 2 * PART :].reshape(T, PART))
        dn[:, T * n : T * (n + 1)] = total


def stream_backward(dn, stream, gain, grad, small, give):
    small[6:7, 0:D] = jnp.zeros((1, D), F32)

    def body(at):
        v, d = stream[at, :].astype(F32), dn[at, 0:D]
        r = lax.rsqrt(jnp.mean(v * v, axis=-1, keepdims=True) + EPS)
        small[6:7, 0:D] += jnp.sum(d * v * r, axis=0, keepdims=True)
        gd = gain * d
        give(at, grad[at, :] + r * gd - v * (r * r * r * jnp.mean(v * gd, axis=-1, keepdims=True)))

    by_rows(body)


class Place:
    def __init__(self):
        me = lax.axis_index("fsdp")
        self.me = me
        self.x = lax.div(me, 32)
        self.y = lax.rem(lax.div(me, 8), 4)
        self.z = lax.rem(lax.div(me, 2), 4)
        self.c = lax.rem(me, 2)

    def at(self, dx=0, dy=0, dz=0, dc=0):
        x = lax.rem(self.x + dx, 4)
        y = lax.rem(self.y + dy, 4)
        z = lax.rem(self.z + dz, 4)
        c = lax.rem(self.c + dc, 2)
        return ((x * 4 + y) * 4 + z) * 2 + c

    def along(self, axis, step):
        return self.at(dx=step) if axis == 0 else self.at(dy=step)

    def half(self, core, size, color=0, colors=1):
        return pl.ds(pl.multiple_of(core * size + color * (size // 2), 128), size // colors)


def greet(places):
    barrier = pltpu.get_barrier_semaphore()
    for place in places:
        pl.semaphore_signal(barrier, inc=1, device_id=(place,), device_id_type=MESH)
    pl.semaphore_wait(barrier, len(places))


class Semaphores:
    def __init__(self, send, recv):
        self.send, self.recv, self.count = send, recv, 0

    def next(self):
        self.count += 1
        return self.send.at[self.count - 1], self.recv.at[self.count - 1]


class Copies:
    def __init__(self, semaphores):
        self.semaphores, self.made, self.over = semaphores, {}, set()

    def make(self, name, src, dst, device):
        send, recv = self.semaphores.next()
        self.made[name] = pltpu.make_async_remote_copy(
            src_ref=src, dst_ref=dst, send_sem=send, recv_sem=recv, device_id=(device,), device_id_type=MESH
        )

    def start(self, *name):
        self.made[name].start()

    def got(self, *name):
        self.made[name].wait_recv()

    def sent(self, *name):
        self.made[name].wait_send()
        self.over.add(name)

    def finish(self):
        for name in self.made:
            if name not in self.over:
                self.sent(*name)


STEPS = (1, 3, 2)
OFFSETS = (0, 3, 1, 2)
GROUP = [(dz, dc) for dz in (1, 3, 2, 0) for dc in (0, 1) if (dz, dc) != (0, 0)]


class GatherGroup:
    def __init__(self, at, shard, room, semaphores):
        self.at, self.shard, self.size = at, shard, room.shape[3]
        self.slots = room.at[0:2, :, 0:16, :]
        self.mine = (lax.div(at.z, 2), lax.rem(at.z, 2) * 2 + at.c)
        self.copies = Copies(semaphores)
        for dz, dc in GROUP:
            core = lax.rem(at.c + dc, 2)
            self.copies.make((dz, dc), shard.at[:, at.half(core, self.size)], self.slots.at[self.mine], at.at(dz=dz, dc=dc))

    def begin(self):
        for name in GROUP:
            self.copies.start(*name)
        self.slots[self.mine] = self.shard[:, self.at.half(self.at.c, self.size)]

    def end(self, first, second):
        for name in GROUP:
            self.copies.got(*name)
        row, k = iota((96, 128), 0), iota((96, 128), 1)
        within = k & 15
        block = jnp.where(within >= 6, 1, 0)
        aim = block * 48 + (k >> 4) * 6 + within - 6 * block
        select = ones_where((row == aim) & (within < 12)).astype(BF)
        got = nn(select, self.slots[...].reshape(128, self.size)).astype(BF)
        at = self.at
        first[at.x, at.y, :, at.half(at.c, self.size)] = got[:48]
        second[at.x, at.y, :, at.half(at.c, self.size)] = got[48:]


class GatherPlane:
    SENDS = 20

    def __init__(self, at, w, semaphores):
        self.copies = c = Copies(semaphores)
        size = w.shape[3] // 2
        for color in range(2):
            cols = at.half(at.c, size, color, 2)
            own = w.at[at.x, at.y, :, cols]
            for step in STEPS:
                c.make(("a", color, step), own, own, at.along(color, step))
            for o in OFFSETS:
                line = w.at[:, lax.rem(at.y + o, 4), :, cols] if color == 0 else w.at[lax.rem(at.x + o, 4), :, :, cols]
                if o == 0:
                    for step in STEPS:
                        c.make(("c", color, step), line, line, at.along(1 - color, step))
                c.make(("p", color, o), line, line, at.at(dc=1))

    def begin(self):
        for step in STEPS:
            for color in range(2):
                self.copies.start("a", color, step)

    def near(self):
        for color in range(2):
            for step in STEPS:
                self.copies.got("a", color, step)
            for step in STEPS:
                self.copies.start("c", color, step)
            self.copies.start("p", color, 0)

    def far(self):
        for step in STEPS:
            for color in range(2):
                self.copies.got("c", color, step)
                self.copies.start("p", color, 4 - step)

    def end(self):
        for o in OFFSETS:
            for color in range(2):
                self.copies.got("p", color, o)


def plus(a, b):
    return a.astype(F32) + b.astype(F32)


class Reduce:
    SENDS = 18

    def __init__(self, at, g, out, scratch, semaphores):
        self.h, self.rb, self.rb1, self.zs, self.zr, self.xs = scratch
        self.at, self.g, self.out = at, g, out
        self.size = g.shape[3] // 2
        self.copies = c = Copies(semaphores)
        other = lax.rem(at.c + 1, 2)
        for color in range(2):
            cols = self.here(color)
            c.make(("p", color), g.at[:, :, :, at.half(other, self.size, color, 2)], self.h.at[:, :, :, cols], at.at(dc=1))
            for step in STEPS:
                c.make(("a", color, step), self.rows(color, step), self.rb.at[color, step - 1], at.along(color, step))
                c.make(("d", color, step), self.block(color, step), self.rb1.at[color, step - 1], at.along(1 - color, step))
        for dz in STEPS:
            c.make(("z", dz), self.zs.at[lax.rem(at.z + dz, 4)], self.zr.at[at.z], at.at(dz=dz))
        c.make(("x",), self.xs, out.at[:, at.half(at.c, self.size)], at.at(dc=1))

    def here(self, color):
        return pl.ds(color * (self.size // 2), self.size // 2)

    def rows(self, color, o):
        if color == 0:
            return self.h.at[lax.rem(self.at.x + o, 4), :, :, self.here(color)]
        return self.h.at[:, lax.rem(self.at.y + o, 4), :, self.here(color)]

    def block(self, color, o):
        dx, dy = (0, o) if color == 0 else (o, 0)
        return self.h.at[lax.rem(self.at.x + dx, 4), lax.rem(self.at.y + dy, 4), :, self.here(color)]

    def begin(self):
        for color in range(2):
            self.copies.start("p", color)

    def pair(self, color):
        at = self.at
        self.copies.got("p", color)
        cols = self.here(color)

        def add(x, carry):
            self.h[x, :, :, cols] += self.g[x, :, :, at.half(at.c, self.size, color, 2)]
            return carry

        lax.fori_loop(0, 4, add, 0, unroll=True)
        for step in STEPS:
            self.copies.start("a", color, step)

    def near(self, color):
        for step in STEPS:
            self.copies.got("a", color, step)
        cols = self.here(color)

        def add(n, carry):
            x, y = (self.at.x, n) if color == 0 else (n, self.at.y)
            there = (x, y, slice(None), cols)
            self.h[there] = (plus(self.h[there], self.rb[color, 0, n]) + plus(self.rb[color, 1, n], self.rb[color, 2, n])).astype(BF)
            return carry

        lax.fori_loop(0, 4, add, 0, unroll=True)
        for step in STEPS:
            self.copies.start("d", color, step)

    def far(self, color):
        for step in STEPS:
            self.copies.got("d", color, step)
        there = self.block(color, 0)
        there[...] = (plus(there[...], self.rb1[color, 0]) + plus(self.rb1[color, 1], self.rb1[color, 2])).astype(BF)

    def along_z(self):
        at = self.at
        row, k = iota((64, 48), 0), iota((64, 48), 1)
        select = ones_where(((row & 15) < 12) & (k == 12 * (row >> 4) + (row & 15))).astype(BF)
        self.zs[...] = nn(select, self.h[at.x, at.y]).astype(BF).reshape(4, 16, self.size)
        for dz in STEPS:
            self.copies.start("z", dz)
        self.zr[at.z] = self.zs[at.z]

    def along_core(self):
        at = self.at
        for dz in STEPS:
            self.copies.got("z", dz)
        total = plus(self.zr[0], self.zr[1]) + plus(self.zr[2], self.zr[3])
        low, high = total[0:8], jnp.concatenate([total[6:12], total[0:2]], axis=0)
        core = jnp.broadcast_to(at.c, (8, self.size))
        self.xs[...] = jnp.where(core == 0, high, low)
        for color in range(2):
            for step in STEPS:
                self.copies.sent("a", color, step)
                self.copies.sent("d", color, step)
        for dz in STEPS:
            self.copies.sent("z", dz)
        self.copies.start("x")
        self.out[:, at.half(at.c, self.size)] = jnp.where(core == 0, low, high)

    def end(self):
        self.copies.got("x")
        self.copies.sent("x")


class SmallReduce:
    SENDS = 10

    def __init__(self, at, small, out, scratch, semaphores):
        self.at, self.small, self.out = at, small, out
        self.sx, self.sy, self.sz, self.sc = scratch
        self.copies = c = Copies(semaphores)
        for d in STEPS:
            c.make(("sx", d), self.sx.at[at.x], self.sx.at[at.x], at.at(dx=d))
            c.make(("sy", d), self.sy.at[at.y], self.sy.at[at.y], at.at(dy=d))
            c.make(("sz", d), self.sz.at[at.z], self.sz.at[at.z], at.at(dz=d))
        c.make(("sc",), self.sc.at[at.c], self.sc.at[at.c], at.at(dc=1))

    def begin(self):
        self.sx[self.at.x] = self.small[...]
        for d in STEPS:
            self.copies.start("sx", d)

    def step(self, name, here, following, index):
        for d in STEPS:
            self.copies.got(name, d)
        following[index] = (here[0] + here[1]) + (here[2] + here[3])

    def along_y(self):
        self.step("sx", self.sx, self.sy, self.at.y)
        for d in STEPS:
            self.copies.start("sy", d)

    def along_z(self):
        self.step("sy", self.sy, self.sz, self.at.z)
        for d in STEPS:
            self.copies.start("sz", d)

    def along_core(self):
        self.step("sz", self.sz, self.sc, self.at.c)
        self.copies.start("sc")

    def end(self):
        self.copies.got("sc")
        for name in list(self.copies.made):
            self.copies.sent(*name)
        total = self.sc[0] + self.sc[1]

        self.sc[0] = total

        def own(entries, width):
            def part(n, sums):
                pick = (iota((128, 128), 0) + 128 * n == entries * self.at.me + iota((128, 128), 1)) & (iota((128, 128), 1) < entries)
                return sums + exact(self.sc[0, :, tiles(128 * n, 128)], ones_where(pick))

            return lax.fori_loop(0, width // 128, part, jnp.zeros((8, 128), F32))

        self.out[0:5, :] = own(14, CONV)[0:5]
        self.out[5:6, :] = own(12, INNER)[5:6]
        self.out[6:7, :] = own(6, D)[6:7]
        self.out[7:8, :] = total[7:8, 0:128]


def dma_pair(count):
    return [pltpu.SemaphoreType.DMA((count,)), pltpu.SemaphoreType.DMA((count,))]


def wide_scratch(width):
    size = width // 2
    return [
        pltpu.VMEM((4, 4, 48, size), BF),
        pltpu.VMEM((2, 3, 4, 48, size // 2), BF),
        pltpu.VMEM((2, 3, 48, size // 2), BF),
    ]


def narrow_scratch(width):
    size = width // 2
    return [
        pltpu.VMEM((4, 16, size), BF),
        pltpu.VMEM((4, 16, size), BF),
        pltpu.VMEM((8, size), F32),
    ]


def small_scratch():
    return [pltpu.VMEM((4, 8, CONV), F32)] * 3 + [pltpu.VMEM((2, 8, CONV), F32)]


WIDTHS = (Q, Q, Q, B)


def vm(count):
    return [pl.BlockSpec(memory_space=pltpu.VMEM)] * count


def shape(*dims, dtype=F32):
    return jax.ShapeDtypeStruct(dims, dtype)


def whole(width):
    return shape(4, 4, 48, width, dtype=BF)


LIMIT = 63 * 1024 * 1024


def scan_scratch():
    return [
        pltpu.VMEM((T, T), F32),
        pltpu.VMEM((T, 128), BF),
        pltpu.VMEM((T, 128), BF),
        pltpu.VMEM((HEADS, 1, T), F32),
        pltpu.VMEM((6, T, 128), F32),
        pltpu.VMEM((T + 8, 128), F32),
        pltpu.VMEM((T, 256), F32),
        pltpu.VMEM((T, 256), F32),
    ] + [pltpu.VMEM((T, 256), dtype) for dtype in (F32, F32, F32, BF, F32, F32, BF, F32, F32)]


def backward_scratch():
    return [
        pltpu.VMEM((T, 128), F32),
        pltpu.VMEM((T, 128), F32),
        pltpu.VMEM((D, T), BF),
        pltpu.VMEM((D, T), BF),
        pltpu.VMEM((T, INNER), BF),
        pltpu.VMEM((T, INNER), BF),
        pltpu.VMEM((T, USED), BF),
        pltpu.VMEM((T, INNER), F32),
        pltpu.VMEM((T, T), F32),
        pltpu.VMEM((T, 128), F32),
        pltpu.VMEM((T, 128), F32),
        pltpu.VMEM((16, 256), F32),
    ]


class Plan:
    def __init__(self, prefix, steps):
        self.prefix, self.steps = prefix, steps

    def __call__(self, name):
        for step in self.steps.get(self.prefix + name, ()):
            step()

    def at_chunk(self, j):
        for n in range(6):
            if self.prefix + "chunk%d" % n in self.steps:
                pl.when(j == n)(partial(self, "chunk%d" % n))


def first_terms(rb, heads, rows, cols, seg_row, scan, then):
    scores, step3, log3, log_t, masks, padded, act, slope, *work = scan
    prepare_scan(rb[:, STEP:USED], heads, step3, log3, log_t)
    for n in range(2):
        here = slice(128 * n, 128 * (n + 1))
        conv_forward(rb, here, rows, slice(INNER + 128 * n, INNER + 128 * (n + 1)), masks, act, here, slope)
    score_pass(act, cols, seg_row, scores)
    then("scores")


def run_forward(stream, wq, wb, heads, cols, seg_row, rows, skip, rb, values, gate, mixed, following, scan, scratch, then):
    scores, step3, log3, log_t, masks, padded, act, slope, *work = scan
    normed, gated, square, yn = scratch
    small_rows(wb, heads, rows, skip)
    then("rows")
    rms_normed(stream, rows[6:7, 0:D], normed)
    rb[...] = nn(normed[...], weight(wb, pl.ds(0, USED)))
    then("normed")
    first_terms(rb, heads, rows, cols, seg_row, scan, then)
    square[...] = jnp.zeros_like(square)

    def chunk(j, carry):
        here = tiles(j * 256, 256)
        values[:, here] = nn(normed[...], weight_chunk(wq, j, 2))
        gate[:, here] = nn(normed[...], weight_chunk(wq, j, 1))
        value_chunk(j, values, rows, masks, work[7])
        forward_chunk(j, rows, skip, gate, scores, step3, log3, log_t, mixed, gated, square, work)
        then.at_chunk(j)
        return carry

    lax.fori_loop(0, 6, chunk, 0)
    gate_norm(rows, gated, square, yn)
    then("yn")
    for n in range(2):
        there = slice(T * n, T * (n + 1))
        total = stream[:, there].astype(F32)
        for s in range(3):
            total += nt(yn[:, PART * s : PART * (s + 1)], wq[s, 2 * n : 2 * n + 2, :, :, 0:PART].reshape(T, PART))
        following[:, there] = total


def run_backward(grad, stream, normed, wq, wb, heads, cols, seg_row, rows, skip, rb, values, gate, mixed, gq, gb, small, finish, scan, scratch, ready, then):
    scores, step3, log3, log_t, masks, padded, act, slope, *work = scan
    sum_u, sum_d, gl_t, norm_t, dgate, dvalues, db, dyn, dscores, dlog, dstep, skip_sum = scratch

    def lower(at):
        gl[at, :] = grad[at, :].astype(BF)

    norm_t[...] = jnp.transpose(normed[...])
    gl = normed
    by_rows(lower)
    gl_t[...] = jnp.transpose(gl[...])
    for ref in (small, sum_u, sum_d, dscores, dlog, dstep, skip_sum):
        ref[...] = jnp.zeros_like(ref)

    def first(c, carry):
        first_backward(c, gl, wq, rows, gate, mixed, dyn, sum_u, sum_d)
        return carry

    lax.fori_loop(0, 6, first, 0)
    then("first")
    if not ready:
        first_terms(rb, heads, rows, cols, seg_row, scan, then)
    norm_pull(sum_u, sum_d)

    def chunk(j, carry):
        backward_chunk(j, rows, skip, gate, values, masks, padded, scores, step3, log3, log_t, mixed, dyn, sum_u, sum_d,
                       gl_t, norm_t, gq, small, dgate, dvalues, dscores, dlog, dstep, skip_sum, work)
        then.at_chunk(j)
        return carry

    lax.fori_loop(0, 6, chunk, 0)
    then("chunks")
    dact = work[0]
    scores_backward(act, cols, seg_row, dscores, dact)
    steps_backward(rb[:, STEP:USED], heads, dlog, dstep, db, small, skip_sum)
    then("steps")
    for n in range(2):
        here = slice(128 * n, 128 * (n + 1))
        conv_backward(rb, here, rows, slice(INNER + 128 * n, INNER + 128 * (n + 1)), masks, dact, slope, here, small, db, padded)
    put_product(gb, pl.ds(0, USED), norm_t, db[...])
    gb[:, :, :, USED:] = jnp.zeros((4, 4, 48, 128), BF)
    then("b_grad")
    normed_backward(dgate, dvalues, db, wq, wb, dyn)
    then("normed_back")
    stream_backward(dyn, stream, rows[6:7, 0:D], grad, small, finish)
    then("done")


def whole_kernel(shard_b, shard_q, tokens, cotangent, a_log, dt_bias, head_skip, segments, counts,
                 output, tokens_grad, ob0, oq0, s0, ob1, oq1, s1, far_rb, far_values, far_gate, far_mixed,
                 wb0, wq0, wb1, wq1, gb1, gq1,
                 second, grad, rb, values, gate, mixed, rows0, rows1, skip0, skip1, small0, small1, normed, square, local_sem, heads, cols, seg_row, *scratch):
    places = iter(scratch)
    take = lambda n: [next(places) for _ in range(n)]
    scan, backward = take(17), take(12)
    dgate, dyn = backward[4], backward[7]
    forward = (normed, dyn, square, dgate)
    wide = [take(3) for _ in range(4)]
    narrow = [take(3) for _ in range(4)]
    sums_by_axis = take(4)
    semaphores = Semaphores(*take(2))
    at = Place()
    greet([at.at(dx=d) for d in STEPS] + [at.at(dy=d) for d in STEPS] + [at.at(dz=dz, dc=dc) for dz, dc in GROUP])

    parts = range(3)
    ab, *aq = groups = [GatherGroup(at, s, t, semaphores) for s, t in [(shard_b, wide[3][0])] + [(shard_q.at[n], wide[n][0]) for n in parts]]
    b0, x0, y0, z0, b1, x1, y1, z1 = planes = [
        GatherPlane(at, w, semaphores) for wb, wq in ((wb0, wq0), (wb1, wq1)) for w in [wb] + [wq.at[n] for n in parts]
    ]
    def sums_of(gb, gq, ob, oq):
        pairs = [(gq.at[n], oq.at[n]) for n in parts] + [(gb, ob)]
        return [Reduce(at, g, o, wide[n] + narrow[n], semaphores) for n, (g, o) in enumerate(pairs)]

    X1, Y1, Z1, B1 = sums1 = sums_of(gb1, gq1, ob1, oq1)
    X0, Y0, Z0, B0 = sums0 = sums_of(wb1, wq1, ob0, oq0)
    S1, S0 = [SmallReduce(at, *v, semaphores) for v in ((small1, s1, sums_by_axis), (small0, s0, sums_by_axis))]

    def two(step):
        return [partial(step, 0), partial(step, 1)]

    away, back = [], []
    for n, (near, far) in enumerate(((rb, far_rb), (values, far_values), (gate, far_gate), (mixed, far_mixed))):
        away.append(pltpu.make_async_copy(near, far, local_sem.at[n]))
        back.append(pltpu.make_async_copy(far, near, local_sem.at[4 + n]))

    steps = {
        "f0.rows": [y0.begin],
        "f0.normed": [z0.begin],
        "f0.scores": [away[0].start, x0.far, y0.near, x0.end],
        "f0.chunk0": [b1.begin, x1.begin, z0.near],
        "f0.chunk1": [y0.far, b1.near, y0.end],
        "f0.chunk2": [y1.begin, x1.near, b1.far],
        "f0.chunk3": [z0.far, z1.begin, z0.end],
        "f0.chunk4": [b1.end, y1.near],
        "f0.chunk5": [x1.far],
        "f0.yn": [each.start for each in away[1:]] + [z1.near],
        "f1.begin": [away[0].wait],
        "f1.rows": [y1.far],
        "f1.scores": [each.wait for each in away[1:]] + [x1.end, y1.end],
        "f1.chunk1": [z1.far],
        "f1.chunk3": [z1.end],
        "b1.first": [each.copies.finish for each in groups + planes],
        "b1.chunk1": [X1.begin],
        "b1.chunk2": two(X1.pair),
        "b1.chunk3": [Y1.begin],
        "b1.chunk4": two(X1.near) + two(Y1.pair),
        "b1.chunk5": [Z1.begin] + two(X1.far),
        "b1.chunks": [each.start for each in back[1:]],
        "b1.b_grad": [back[0].start, B1.begin],
        "b1.normed_back": two(Y1.near) + two(Z1.pair) + [X1.along_z],
        "b1.done": [each.wait for each in back] + two(Y1.far) + [X1.along_core, S1.begin],
        "b0.first": two(Z1.near) + [S1.along_y] + two(B1.pair) + [Y1.along_z, X1.end],
        "b0.chunk0": two(Z1.far) + two(B1.near) + [Y1.along_core, S1.along_z],
        "b0.chunk1": [X0.begin] + two(B1.far) + [Z1.along_z, Y1.end, S1.along_core],
        "b0.chunk2": two(X0.pair) + [Z1.along_core, B1.along_z, S1.end],
        "b0.chunk3": [Y0.begin, Z1.end, B1.along_core],
        "b0.chunk4": two(X0.near) + two(Y0.pair) + [B1.end],
        "b0.chunk5": [Z0.begin] + two(X0.far) + two(Y0.near) + [X0.along_z],
        "b0.b_grad": [B0.begin] + two(Z0.pair) + two(Y0.far),
        "b0.normed_back": two(B0.pair) + [Y0.along_z, X0.along_core],
        "b0.done": [S0.begin]
        + two(Z0.near)
        + two(B0.near)
        + [Y0.along_core, S0.along_y, X0.end]
        + two(Z0.far)
        + [Z0.along_z]
        + two(B0.far)
        + [B0.along_z, S0.along_z, Z0.along_core, B0.along_core, S0.along_core, Y0.end, Z0.end, B0.end, S0.end],
    }

    ab.begin()
    for each in aq:
        each.begin()
    heads[...] = jnp.zeros_like(heads)
    for l in range(2):
        for n, source in enumerate((a_log, dt_bias, head_skip)):
            heads[l, n : n + 1, 0:HEADS] = source[l : l + 1, :]
    slot_columns(segments, counts, cols, seg_row)
    conv_masks(cols, scan[4])
    scan[5][T:, :] = jnp.zeros((8, 128), F32)
    ab.end(wb0, wb1)
    b0.begin()
    aq[0].end(wq0.at[0], wq1.at[0])
    x0.begin()
    b0.near()
    x0.near()
    b0.far()
    for n in (1, 2):
        aq[n].end(wq0.at[n], wq1.at[n])
    b0.end()

    head0, head1 = heads.at[0], heads.at[1]
    run_forward(tokens, wq0, wb0, head0, cols, seg_row, rows0, skip0, rb, values, gate, mixed, second, scan, forward, Plan("f0.", steps))
    Plan("f1.", steps)("begin")
    run_forward(second, wq1, wb1, head1, cols, seg_row, rows1, skip1, rb, values, gate, mixed, grad, scan, forward, Plan("f1.", steps))

    def turn(at):
        live = cols[at, 7:8]
        output[at, :] = (grad[at, :] * live).astype(BF)
        grad[at, :] = cotangent[at, :].astype(F32) * live

    by_rows(turn)

    def keep(at, value):
        grad[at, :] = value

    run_backward(grad, second, normed, wq1, wb1, head1, cols, seg_row, rows1, skip1, rb, values, gate, mixed,
                 gq1, gb1, small1, keep, scan, backward, True, Plan("b1.", steps))
    rms_normed(tokens, rows0[6:7, 0:D], normed)

    def give(at, value):
        tokens_grad[at, :] = value.astype(BF)

    run_backward(grad, tokens, normed, wq0, wb0, head0, cols, seg_row, rows0, skip0, rb, values, gate, mixed,
                 wq1, wb1, small0, give, scan, backward, False, Plan("b0.", steps))
    for each in sums1 + sums0 + [S1, S0]:
        each.copies.finish()


SENDS = 4 * 7 + 8 * GatherPlane.SENDS + 8 * Reduce.SENDS + 2 * SmallReduce.SENDS


def two_blocks(shards, *rest):
    outs = (shape(8, B), shape(3, 8, Q), shape(8, 128))
    wb, wq = pltpu.VMEM((4, 4, 48, B), BF), pltpu.VMEM((3, 4, 4, 48, Q), BF)
    buffers = []
    for width in WIDTHS:
        buffers += wide_scratch(width)
    for width in WIDTHS:
        buffers += narrow_scratch(width)
    return pl.pallas_call(
        whole_kernel,
        out_shape=(shape(T, D, dtype=BF), shape(T, D, dtype=BF)) + outs + outs + (shape(T, USED),) + (shape(T, INNER),) * 3,
        in_specs=vm(9),
        out_specs=tuple(vm(8)) + (pl.BlockSpec(memory_space=pl.ANY),) * 4,
        scratch_shapes=[wb, wq] * 3
        + [pltpu.VMEM((T, D), F32)] * 2
        + [pltpu.VMEM((T, USED), F32)]
        + [pltpu.VMEM((T, INNER), F32)] * 3
        + [pltpu.VMEM((8, CONV), F32)] * 2
        + [pltpu.VMEM((8, INNER), F32)] * 2
        + [pltpu.VMEM((8, CONV), F32)] * 2
        + [pltpu.VMEM((T, D), BF), pltpu.VMEM((T, 128), F32), pltpu.SemaphoreType.DMA((8,))]
        + [pltpu.VMEM((2, 8, 128), F32), pltpu.VMEM((T, 128), F32), pltpu.VMEM((8, T), F32)]
        + scan_scratch()
        + backward_scratch()
        + buffers
        + small_scratch()
        + dma_pair(SENDS),
        compiler_params=pltpu.CompilerParams(collective_id=0, has_side_effects=True, vmem_limit_bytes=LIMIT),
        name="two_blocks",
    )(*shards, *rest)


def shards_of(norm_gain, in_weight, conv_weight, conv_bias, gate_gain, out_weight):
    taps = jnp.transpose(conv_weight, (0, 2, 1)).reshape(2, 56)
    small = jnp.concatenate([conv_bias, taps, gate_gain, norm_gain, jnp.zeros((2, 40), BF)], axis=1)
    tile = jnp.concatenate([small[:, None, :], jnp.zeros((2, 5, 128), BF)], axis=1)
    wide = jnp.concatenate([in_weight[:, :, INNER + INNER :], jnp.zeros((2, 6, SMALL - STEP - HEADS), BF), tile], axis=2)
    kinds = [jnp.transpose(out_weight, (0, 2, 1)), in_weight[:, :, :INNER], in_weight[:, :, INNER : 2 * INNER]]
    q = jnp.stack([v.reshape(12, 3, PART) for v in kinds], axis=2).reshape(12, 3, Q).transpose(1, 0, 2)
    return jnp.pad(wide.reshape(12, B), ((0, 4), (0, 0))), jnp.pad(q, ((0, 0), (0, 4), (0, 0)))


def local(tokens, cotangent, segments, counts, norm_gain, in_weight, conv_weight, conv_bias, a_log, dt_bias, skip, gate_gain, out_weight):
    shards = shards_of(norm_gain, in_weight, conv_weight, conv_bias, gate_gain, out_weight)
    output, tokens_grad, ob0, oq0, s0, ob1, oq1, s1, *_ = two_blocks(
        shards, tokens, cotangent, a_log, dt_bias, skip, segments.reshape(1, T), counts.reshape(1, 1)
    )
    small = jnp.stack([s0, s1])
    sums = jnp.stack([oq0, oq1])[:, :, 0:6].reshape(2, 3, 6, 3, PART).transpose(3, 0, 2, 1, 4).reshape(3, 2, 6, INNER)
    return (
        output,
        tokens_grad,
        small[:, 6, 0:6],
        jnp.concatenate([sums[1], sums[2], jnp.stack([ob0, ob1])[:, 0:6, 0 : STEP + HEADS]], axis=2),
        jnp.transpose(small[:, 1:5, 0:14], (0, 2, 1)),
        small[:, 0, 0:14],
        small[:, 7, 0:24],
        small[:, 7, 32:56],
        small[:, 7, 64:88],
        small[:, 5, 0:12],
        jnp.transpose(sums[0], (0, 2, 1)),
    )


def solution(mesh):
    axis = P("fsdp")
    rows, second, third = P("fsdp", None), P(None, "fsdp"), P(None, None, "fsdp")
    middle = P(None, "fsdp", None)
    return jax.shard_map(
        local,
        mesh=mesh,
        in_specs=(rows, rows, axis, axis, second, middle, middle, second, P(), P(), P(), second, third),
        out_specs=(rows, rows, second, middle, middle, second, P(), P(), P(), second, third),
        check_vma=False,
    )
```

```python
from functools import partial

import jax
import jax.numpy as jnp
from jax import lax
from jax.experimental import pallas as pl
from jax.experimental.pallas import tpu as pltpu
from jax.sharding import PartitionSpec as P

D = 768
HEADS = 24
STATE = 128
INNER = 1536
CONV = 1792
T = 384
PART = 512
Q = 1536
STEP = 256
USED = 384
SMALL = 384
B = 512
EPS = 1e-05
F32 = jnp.float32
BF = jnp.bfloat16
HIGHEST = lax.Precision.HIGHEST
MESH = pl.DeviceIdType.MESH


def nn(a, b):
    return lax.dot_general(a, b, (((1,), (0,)), ((), ())), preferred_element_type=F32)


def nt(a, b):
    return lax.dot_general(a, b, (((1,), (1,)), ((), ())), preferred_element_type=F32)


def tn(a, b):
    return lax.dot_general(a, b, (((0,), (0,)), ((), ())), preferred_element_type=F32)


def exact(a, b):
    return lax.dot_general(a, b, (((1,), (0,)), ((), ())), precision=HIGHEST, preferred_element_type=F32)


def iota(shape, dim):
    return lax.broadcasted_iota(jnp.int32, shape, dim)


def ones_where(cond):
    return jnp.where(cond, 1.0, 0.0)


def tiles(start, width):
    if isinstance(start, int):
        return pl.ds(start, width)
    return pl.ds(pl.multiple_of(start, 128), width)


def sigmoid(v):
    return 1.0 / (1.0 + jnp.exp(-v))


def weight(w, cols):
    v = w[:, :, :, cols]
    return v.reshape(D, v.shape[-1])


def part_of(j, kind):
    return lax.div(j, 2), tiles(PART * kind + 256 * lax.rem(j, 2), 256)


def weight_chunk(wq, j, kind):
    n, cols = part_of(j, kind)
    return wq[n, :, :, :, cols].reshape(D, 256)


def put_product(g, cols, left, right):
    for n in range(2):
        v = nn(left[T * n : T * (n + 1), :], right)
        g[2 * n : 2 * n + 2, :, :, cols] = v.astype(BF).reshape(2, 4, 48, v.shape[-1])


def put_chunk(gq, j, kind, left, right):
    n, cols = part_of(j, kind)
    put_product(gq.at[n], cols, left, right)


def pack3(v):
    hi = v.astype(BF).astype(F32)
    rest = v - hi
    mid = rest.astype(BF).astype(F32)
    low = rest - mid
    return (hi + pltpu.roll(mid, 32, 1) + pltpu.roll(low, 64, 1)).astype(BF)


def unpack3(v):
    return v + pltpu.roll(v, 96, 1) + pltpu.roll(v, 64, 1)


def head_mask(shape=(T, 128)):
    return iota(shape, 1) < HEADS


def spread_matrix(j, width, shift):
    return ones_where((iota((128, width), 0) & 31) == 4 * j + (iota((128, width), 1) >> shift)).astype(BF)


UNITS = ((14, 4682), (12, 5462), (6, 10923))


def small_rows(wb, heads, rows, skip):
    pick = ones_where(iota((128, D), 1) == 6 * iota((128, D), 0)).astype(BF)
    held = nn(pick, weight(wb, tiles(SMALL, 128))).astype(BF)

    kinds = [UNITS[0] + (14 * n,) for n in range(5)] + [UNITS[1] + (70,), UNITS[2] + (82,)]

    def body(c, carry):
        channel = iota((128, 128), 1) + 128 * c
        units = [(channel * magic) >> 16 for _, magic in UNITS]
        spreads = []
        for n, (entries, _, offset) in enumerate(kinds):
            unit = units[max(n - 4, 0)]
            spreads.append(ones_where(iota((128, 128), 0) == offset + channel - unit * entries).astype(BF))
        got = nn(held, jnp.concatenate(spreads, axis=1))
        for n in range(7):
            mine = jnp.where(units[max(n - 4, 0)] == iota((128, 128), 0), got[:, 128 * n : 128 * (n + 1)], 0.0)
            rows[n : n + 1, tiles(128 * c, 128)] = jnp.sum(mine, axis=0, keepdims=True)
        return carry

    lax.fori_loop(0, 14, body, 0, unroll=2)
    which = ones_where((iota((128, INNER), 1) >> 6) == iota((128, INNER), 0))
    skip[...] = exact(heads[...], which)


def by_rows(body, count=12):
    size = T // count

    def step(n, carry):
        body(pl.ds(pl.multiple_of(n * size, size), size))
        return carry

    lax.fori_loop(0, count, step, 0, unroll=3)


def rms_normed(stream, gain, normed):
    def body(at):
        v = stream[at, :].astype(F32)
        r = lax.rsqrt(jnp.mean(v * v, axis=-1, keepdims=True) + EPS)
        normed[at, :] = (v * r * gain).astype(BF)

    by_rows(body)


def step_terms(raw, heads):
    mask = head_mask()
    rate = -jnp.exp(heads[0:1, :])
    x = jnp.where(mask, raw + heads[1:2, :], 0.0)
    step = jnp.where(mask, jnp.maximum(x, 0.0) + jnp.log1p(jnp.exp(-jnp.abs(x))), 0.0)
    return rate, x, step


def prepare_scan(raw, heads, step3, log3, log_t):
    rate, x, step = step_terms(raw, heads)
    lower = ones_where(iota((T, T), 0) >= iota((T, T), 1)).astype(BF)
    total = unpack3(nn(lower, pack3(jnp.where(head_mask(), step * rate, 0.0))))
    total = jnp.where(head_mask(), total, 0.0)
    step3[...] = pack3(step)
    log3[...] = pack3(total)
    flipped = jnp.transpose(total)
    for h in range(HEADS):
        log_t[h] = flipped[h : h + 1]


def slot_columns(segments, counts, cols, seg_row):
    seg = jnp.broadcast_to(segments[...].astype(F32), (8, T))
    slot, row = iota((8, T), 1), iota((8, T), 0)
    seg_row[...] = seg
    lines = seg
    for k in range(1, 4):
        lines = jnp.where(row == k, jnp.where(slot >= k, pltpu.roll(seg, k, 1), -1.0), lines)
        lines = jnp.where(row == k + 3, jnp.where(slot < T - k, pltpu.roll(seg, T - k, 1), -1.0), lines)
    lines = jnp.where(row == 7, ones_where(slot < counts[...]), lines)
    cols[...] = jnp.transpose(jnp.concatenate([lines, jnp.zeros((120, T), F32)], axis=0))


def conv_masks(cols, masks):
    for k in range(1, 7):
        masks[k - 1] = jnp.broadcast_to(ones_where(cols[:, k : k + 1] == cols[:, 0:1]), (T, 128))


def taken(src, masks, i, here):
    at = block_rows(i)
    if i == 0:
        ci = src[at, here]
        return [ci] + [pltpu.roll(ci, k, 0) * masks[k - 1, at, :] for k in range(1, 4)]
    slab = src[128 * i - 8 : 128 * (i + 1), here]
    return [slab[8:]] + [pltpu.roll(slab, k, 0)[8:] * masks[k - 1, at, :] for k in range(1, 4)]


def conv_forward(src, here, rows, channels, masks, out, there, slope=None):
    for i in range(3):
        ci = taken(src, masks, i, here)
        total = rows[0:1, channels] + ci[0] * rows[4:5, channels]
        for k in range(1, 4):
            total = total + ci[k] * rows[4 - k : 5 - k, channels]
        sg = sigmoid(total)
        out[block_rows(i), there] = total * sg
        if slope is not None:
            slope[block_rows(i), there] = sg * (1.0 + total * (1.0 - sg))


def conv_backward(src, here, rows, channels, masks, dact, slope, there, small, out, padded):
    sums = [0.0] * 5
    for i in range(3):
        ci = taken(src, masks, i, here)
        dc = dact[block_rows(i), there] * slope[block_rows(i), there]
        padded[block_rows(i), :] = dc
        for n, v in enumerate([dc] + [dc * ci[3 - m] for m in range(4)]):
            sums[n] = sums[n] + jnp.sum(v.reshape(16, 8, 128), axis=0)
    for n in range(5):
        small[n : n + 1, channels] = jnp.sum(sums[n], axis=0, keepdims=True)
    for i in range(3):
        at = block_rows(i)
        slab = padded[128 * i : 128 * (i + 1) + 8, :]
        dci = slab[:128] * rows[4:5, channels]
        for k in range(1, 4):
            dci = dci + pltpu.roll(slab, 136 - k, 0)[:128] * masks[k + 2, at, :] * rows[4 - k : 5 - k, channels]
        out[at, here] = dci.astype(BF)


def linked_pairs(cols, seg_row):
    return (cols[:, 0:1] == seg_row[0:1, :]) & (iota((T, T), 0) >= iota((T, T), 1))


def score_pass(act, cols, seg_row, scores):
    b = act[:, 0:STATE]
    c = act[:, STATE:]
    s = lax.dot_general(c, b, (((1,), (1,)), ((), ())), precision=HIGHEST, preferred_element_type=F32)
    s = jnp.where(linked_pairs(cols, seg_row), s, 0.0)
    scores[...] = s


def lane_heads(q):
    return (iota((128, 256), 1) >> 6) == q


def block_rows(i):
    return slice(128 * i, 128 * (i + 1))


def decays(at, j, log3, log_t):
    wide = nn(log3[at, :], spread_matrix(j, 512, 7))
    out = []
    for q in range(4):
        out.append(jnp.exp(jnp.minimum(wide[:, 128 * q : 128 * (q + 1)] - log_t[4 * j + q, :, at], 0.0)))
    return out


def by_head(part):
    return jnp.concatenate([jnp.where(lane_heads(q), part, 0) for q in range(4)], axis=0)


def halves(v):
    return v[:, :128] + v[:, 128:]


def dynamic_block(i):
    return pl.ds(pl.multiple_of(128 * i, 128), 128)


def value_chunk(j, values, rows, masks, x, slope=None):
    for n in range(2):
        here = tiles(j * 256 + 128 * n, 128)
        conv_forward(values, here, rows, here, masks, x, slice(128 * n, 128 * (n + 1)), slope)


def forward_chunk(j, rows, skip, gate_ref, scores, step3, log3, log_t, mixed_ref, gated, square, work):
    here = tiles(j * 256, 256)
    log_e, xd_ref, xd_low, y_ref, act = work[0], work[5], work[3], work[2], work[7]

    def inside(i, carry):
        at = dynamic_block(i)
        spread = spread_matrix(j, 256, 6)
        log_e[at, :] = nn(log3[at, :], spread)
        xd = act[at, :] * nn(step3[at, :], spread)
        xd_ref[at, :] = xd
        sc = scores[at, at]
        left = jnp.concatenate([(sc * e).astype(BF) for e in decays(at, j, log3, log_t)], axis=1)
        y_ref[at, :] = nn(left, by_head(xd.astype(BF)))
        return carry

    lax.fori_loop(0, 3, inside, 0, unroll=True)
    for i in range(1, 3):
        at, before = block_rows(i), slice(0, 128 * i)
        edge = log_e[128 * i - 1 : 128 * i, :]
        for k in range(i):
            part = block_rows(k)
            xd_low[part, :] = (xd_ref[part, :] * jnp.exp(jnp.minimum(edge - log_e[part, :], 0.0))).astype(BF)
        y_ref[at, :] += jnp.exp(jnp.minimum(log_e[at, :] - edge, 0.0)) * nn(scores[at, before].astype(BF), xd_low[before, :])

    def gating(i, carry):
        at = dynamic_block(i)
        mixed = y_ref[at, :] + skip[2:3, here] * act[at, :]
        mixed_ref[at, here] = mixed
        gate = gate_ref[at, here]
        u = mixed * (gate * sigmoid(gate))
        gated[at, here] = u
        square[at, :] += halves(u * u)
        return carry

    lax.fori_loop(0, 3, gating, 0, unroll=True)


def gate_norm(rows, gated, square, yn):
    r = lax.rsqrt(jnp.sum(square[...], axis=-1, keepdims=True) * (1.0 / INNER) + EPS)

    def gain(c, carry):
        here = tiles(c * 256, 256)
        yn[:, here] = (gated[:, here] * r * rows[5:6, here]).astype(BF)
        return carry

    lax.fori_loop(0, 6, gain, 0)


def first_backward(c, gl, wq, rows, gate_ref, mixed_ref, dyn, sum_u, sum_d):
    here = tiles(c * 256, 256)
    dyn[:, here] = nn(gl[...], weight_chunk(wq, c, 0))

    def body(i, carry):
        at = dynamic_block(i)
        gate = gate_ref[at, here]
        u = mixed_ref[at, here] * (gate * sigmoid(gate))
        sum_u[at, :] += halves(u * u)
        sum_d[at, :] += halves(u * dyn[at, here] * rows[5:6, here])
        return carry

    lax.fori_loop(0, 3, body, 0, unroll=True)


def norm_pull(sum_u, sum_d):
    r = lax.rsqrt(jnp.sum(sum_u[...], axis=-1, keepdims=True) * (1.0 / INNER) + EPS)
    pull = r * r * r * (jnp.sum(sum_d[...], axis=-1, keepdims=True) * (1.0 / INNER))
    sum_u[...] = jnp.broadcast_to(r, (T, 128))
    sum_d[...] = jnp.broadcast_to(pull, (T, 128))


def backward_chunk(j, rows, skip, gate_ref, values, masks, padded, scores, step3, log3, log_t, mixed_ref, dyn, sum_u, sum_d,
                   gl_t, norm_t, gq, small, dgate, dvalues, dscores, dlog, dstep, skip_sum, work):
    here = tiles(j * 256, 256)
    log_e, dm_ref, v_ref, low, dxd_ref, step_e, yn, act, slope = work
    value_chunk(j, values, rows, masks, act, slope)
    skips = skip_sum.at[0:8, 0:256]
    skips[...] = jnp.zeros((8, 256), F32)
    small[5:6, here] = jnp.zeros((1, 256), F32)

    def inside(i, carry):
        at = dynamic_block(i)
        spread = spread_matrix(j, 256, 6)
        log_e[at, :] = nn(log3[at, :], spread)
        step_e[at, :] = nn(step3[at, :], spread)
        x = act[at, :]
        xd = x * step_e[at, :]
        r, pull = sum_u[at, 0:1], sum_d[at, 0:1]
        dy = dyn[at, here]
        gate = gate_ref[at, here]
        mixed = mixed_ref[at, here]
        sg = sigmoid(gate)
        silu = gate * sg
        gain = rows[5:6, here]
        u = mixed * silu
        ur = u * r
        small[5:6, here] += jnp.sum(dy * ur, axis=0, keepdims=True)
        yn[at, :] = (ur * gain).astype(BF)
        du = r * (gain * dy) - u * pull
        dgate[at, here] = (du * mixed * (sg * (1.0 + gate * (1.0 - sg)))).astype(BF)
        dm = du * silu
        dm_ref[at, :] = dm
        skips[...] += jnp.sum((dm * x).reshape(16, 8, 256), axis=0)
        sc = scores[at, at]
        es = decays(at, j, log3, log_t)
        ws = [(sc * e).astype(BF) for e in es]
        part, dpart = xd.astype(BF), dm.astype(BF)
        dright = by_head(dpart)
        y = nn(jnp.concatenate(ws, axis=1), by_head(part))
        dxd = tn(jnp.concatenate(ws, axis=0), dright)
        g = nt(dright, part)
        ds = g[0:128] * es[0]
        for q in range(1, 4):
            ds = ds + g[128 * q : 128 * (q + 1)] * es[q]
        dscores[at, at] += ds
        v_ref[at, :] = dpart.astype(F32) * y - part.astype(F32) * dxd
        dxd_ref[at, :] = dxd
        return carry

    lax.fori_loop(0, 3, inside, 0, unroll=True)
    put_chunk(gq, j, 0, gl_t, yn[...])
    put_chunk(gq, j, 1, norm_t, dgate[:, here])
    for i in range(1, 3):
        at, before = block_rows(i), slice(0, 128 * i)
        edge = log_e[128 * i - 1 : 128 * i, :]
        for k in range(i):
            part = block_rows(k)
            low[part, :] = (act[part, :] * step_e[part, :] * jnp.exp(jnp.minimum(edge - log_e[part, :], 0.0))).astype(BF)
        de = (dm_ref[at, :] * jnp.exp(jnp.minimum(log_e[at, :] - edge, 0.0))).astype(BF)
        linked = scores[at, before].astype(BF)
        z = nn(linked, low[before, :])
        dscores[at, before] += nt(de, low[before, :])
        v_ref[at, :] += de.astype(F32) * z
        for k in range(i):
            part = block_rows(k)
            dz = tn(linked[:, part], de)
            v_ref[part, :] -= low[part, :].astype(F32) * dz
            dxd_ref[part, :] += jnp.exp(jnp.minimum(edge - log_e[part, :], 0.0)) * dz

    def outside(i, carry):
        at = dynamic_block(i)
        dxd = dxd_ref[at, :]
        gather = ones_where(4 * j + ((iota((512, 128), 0) & 255) >> 6) == iota((512, 128), 1)).astype(BF)

        def head_sums(a):
            hi = a.astype(BF)
            return nn(jnp.concatenate([hi, (a - hi.astype(F32)).astype(BF)], axis=1), gather)

        dlog[at, :] += head_sums(v_ref[at, :])
        dstep[at, :] += head_sums(act[at, :] * dxd)
        dxd_ref[at, :] = step_e[at, :] * dxd + skip[2:3, here] * dm_ref[at, :]
        return carry

    lax.fori_loop(0, 3, outside, 0, unroll=True)
    which = ones_where(4 * j + (iota((256, 128), 0) >> 6) == iota((256, 128), 1))
    skip_sum[8:16, 0:128] += exact(skips[...], which)
    for n in range(2):
        there = tiles(j * 256 + 128 * n, 128)
        conv_backward(values, there, rows, there, masks, dxd_ref, slope, slice(128 * n, 128 * (n + 1)), small, dvalues, padded)
    put_chunk(gq, j, 2, norm_t, dvalues[:, here])


def scores_backward(act, cols, seg_row, dscores, dact):
    ds = jnp.where(linked_pairs(cols, seg_row), dscores[...], 0.0).astype(BF)
    b = act[:, 0:STATE].astype(BF)
    c = act[:, STATE:].astype(BF)
    dact[:, 0:STATE] = tn(ds, c)
    dact[:, STATE:] = nn(ds, b)


def steps_backward(raw, heads, dlog, dstep, drest, small, skip_sum):
    rate, x, step = step_terms(raw, heads)
    upper = ones_where(iota((T, T), 0) <= iota((T, T), 1)).astype(BF)
    dsum = unpack3(nn(upper, pack3(dlog[...])))
    dsum = jnp.where(head_mask(), dsum, 0.0)
    dx = jnp.where(head_mask(), (dstep[...] + rate * dsum) * sigmoid(x), 0.0)
    drest[:, STEP:USED] = dx.astype(BF)
    rates = jnp.sum(dsum * step, axis=0, keepdims=True) * jnp.where(head_mask((1, 128)), rate, 0.0)
    biases = jnp.sum(dx, axis=0, keepdims=True)
    skips = jnp.sum(skip_sum[8:16, 0:128], axis=0, keepdims=True)
    small[7:8, 0:128] = rates + pltpu.roll(biases, 32, 1) + pltpu.roll(skips, 64, 1)


def normed_backward(dgate, dvalues, db, wq, wb, dn):
    for n in range(2):
        half = slice(2 * n, 2 * n + 2)
        total = nt(db[...], wb[half, :, :, 0:USED].reshape(T, USED))
        for s in range(3):
            cols = slice(PART * s, PART * (s + 1))
            total += nt(dgate[:, cols], wq[s, half, :, :, PART : 2 * PART].reshape(T, PART))
            total += nt(dvalues[:, cols], wq[s, half, :, :, 2 * PART :].reshape(T, PART))
        dn[:, T * n : T * (n + 1)] = total


def stream_backward(dn, stream, gain, grad, small, give):
    small[6:7, 0:D] = jnp.zeros((1, D), F32)

    def body(at):
        v, d = stream[at, :].astype(F32), dn[at, 0:D]
        r = lax.rsqrt(jnp.mean(v * v, axis=-1, keepdims=True) + EPS)
        small[6:7, 0:D] += jnp.sum(d * v * r, axis=0, keepdims=True)
        gd = gain * d
        give(at, grad[at, :] + r * gd - v * (r * r * r * jnp.mean(v * gd, axis=-1, keepdims=True)))

    by_rows(body)


class Place:
    def __init__(self):
        me = lax.axis_index("fsdp")
        self.me = me
        self.x = lax.div(me, 32)
        self.y = lax.rem(lax.div(me, 8), 4)
        self.z = lax.rem(lax.div(me, 2), 4)
        self.c = lax.rem(me, 2)

    def at(self, dx=0, dy=0, dz=0, dc=0):
        x = lax.rem(self.x + dx, 4)
        y = lax.rem(self.y + dy, 4)
        z = lax.rem(self.z + dz, 4)
        c = lax.rem(self.c + dc, 2)
        return ((x * 4 + y) * 4 + z) * 2 + c

    def along(self, axis, step):
        return self.at(dx=step) if axis == 0 else self.at(dy=step)

    def half(self, core, size, color=0, colors=1):
        return pl.ds(pl.multiple_of(core * size + color * (size // 2), 128), size // colors)


def greet(places):
    barrier = pltpu.get_barrier_semaphore()
    for place in places:
        pl.semaphore_signal(barrier, inc=1, device_id=(place,), device_id_type=MESH)
    pl.semaphore_wait(barrier, len(places))


class Semaphores:
    def __init__(self, send, recv):
        self.send, self.recv, self.count = send, recv, 0

    def next(self):
        self.count += 1
        return self.send.at[self.count - 1], self.recv.at[self.count - 1]


class Copies:
    def __init__(self, semaphores):
        self.semaphores, self.made, self.over = semaphores, {}, set()

    def make(self, name, src, dst, device):
        send, recv = self.semaphores.next()
        self.made[name] = pltpu.make_async_remote_copy(
            src_ref=src, dst_ref=dst, send_sem=send, recv_sem=recv, device_id=(device,), device_id_type=MESH
        )

    def start(self, *name):
        self.made[name].start()

    def got(self, *name):
        self.made[name].wait_recv()

    def sent(self, *name):
        self.made[name].wait_send()
        self.over.add(name)

    def finish(self):
        for name in self.made:
            if name not in self.over:
                self.sent(*name)


STEPS = (1, 3, 2)
OFFSETS = (0, 3, 1, 2)
GROUP = [(dz, dc) for dz in (1, 3, 2, 0) for dc in (0, 1) if (dz, dc) != (0, 0)]


class GatherGroup:
    def __init__(self, at, shard, room, semaphores):
        self.at, self.shard, self.size = at, shard, room.shape[3]
        self.slots = room.at[0:2, :, 0:16, :]
        self.mine = (lax.div(at.z, 2), lax.rem(at.z, 2) * 2 + at.c)
        self.copies = Copies(semaphores)
        for dz, dc in GROUP:
            core = lax.rem(at.c + dc, 2)
            self.copies.make((dz, dc), shard.at[:, at.half(core, self.size)], self.slots.at[self.mine], at.at(dz=dz, dc=dc))

    def begin(self):
        for name in GROUP:
            self.copies.start(*name)
        self.slots[self.mine] = self.shard[:, self.at.half(self.at.c, self.size)]

    def end(self, first, second):
        for name in GROUP:
            self.copies.got(*name)
        row, k = iota((96, 128), 0), iota((96, 128), 1)
        within = k & 15
        block = jnp.where(within >= 6, 1, 0)
        aim = block * 48 + (k >> 4) * 6 + within - 6 * block
        select = ones_where((row == aim) & (within < 12)).astype(BF)
        got = nn(select, self.slots[...].reshape(128, self.size)).astype(BF)
        at = self.at
        first[at.x, at.y, :, at.half(at.c, self.size)] = got[:48]
        second[at.x, at.y, :, at.half(at.c, self.size)] = got[48:]


class GatherPlane:
    SENDS = 20

    def __init__(self, at, w, semaphores):
        self.copies = c = Copies(semaphores)
        size = w.shape[3] // 2
        for color in range(2):
            cols = at.half(at.c, size, color, 2)
            own = w.at[at.x, at.y, :, cols]
            for step in STEPS:
                c.make(("a", color, step), own, own, at.along(color, step))
            for o in OFFSETS:
                line = w.at[:, lax.rem(at.y + o, 4), :, cols] if color == 0 else w.at[lax.rem(at.x + o, 4), :, :, cols]
                if o == 0:
                    for step in STEPS:
                        c.make(("c", color, step), line, line, at.along(1 - color, step))
                c.make(("p", color, o), line, line, at.at(dc=1))

    def begin(self):
        for step in STEPS:
            for color in range(2):
                self.copies.start("a", color, step)

    def near(self):
        for color in range(2):
            for step in STEPS:
                self.copies.got("a", color, step)
            for step in STEPS:
                self.copies.start("c", color, step)
            self.copies.start("p", color, 0)

    def far(self):
        for step in STEPS:
            for color in range(2):
                self.copies.got("c", color, step)
                self.copies.start("p", color, 4 - step)

    def end(self):
        for o in OFFSETS:
            for color in range(2):
                self.copies.got("p", color, o)


def plus(a, b):
    return a.astype(F32) + b.astype(F32)


class Reduce:
    SENDS = 18

    def __init__(self, at, g, out, scratch, semaphores):
        self.h, self.rb, self.rb1, self.zs, self.zr, self.xs = scratch
        self.at, self.g, self.out = at, g, out
        self.size = g.shape[3] // 2
        self.copies = c = Copies(semaphores)
        other = lax.rem(at.c + 1, 2)
        for color in range(2):
            cols = self.here(color)
            c.make(("p", color), g.at[:, :, :, at.half(other, self.size, color, 2)], self.h.at[:, :, :, cols], at.at(dc=1))
            for step in STEPS:
                c.make(("a", color, step), self.rows(color, step), self.rb.at[color, step - 1], at.along(color, step))
                c.make(("d", color, step), self.block(color, step), self.rb1.at[color, step - 1], at.along(1 - color, step))
        for dz in STEPS:
            c.make(("z", dz), self.zs.at[lax.rem(at.z + dz, 4)], self.zr.at[at.z], at.at(dz=dz))
        c.make(("x",), self.xs, out.at[:, at.half(at.c, self.size)], at.at(dc=1))

    def here(self, color):
        return pl.ds(color * (self.size // 2), self.size // 2)

    def rows(self, color, o):
        if color == 0:
            return self.h.at[lax.rem(self.at.x + o, 4), :, :, self.here(color)]
        return self.h.at[:, lax.rem(self.at.y + o, 4), :, self.here(color)]

    def block(self, color, o):
        dx, dy = (0, o) if color == 0 else (o, 0)
        return self.h.at[lax.rem(self.at.x + dx, 4), lax.rem(self.at.y + dy, 4), :, self.here(color)]

    def begin(self):
        for color in range(2):
            self.copies.start("p", color)

    def pair(self, color):
        at = self.at
        self.copies.got("p", color)
        cols = self.here(color)

        def add(x, carry):
            self.h[x, :, :, cols] += self.g[x, :, :, at.half(at.c, self.size, color, 2)]
            return carry

        lax.fori_loop(0, 4, add, 0, unroll=True)
        for step in STEPS:
            self.copies.start("a", color, step)

    def near(self, color):
        for step in STEPS:
            self.copies.got("a", color, step)
        cols = self.here(color)

        def add(n, carry):
            x, y = (self.at.x, n) if color == 0 else (n, self.at.y)
            there = (x, y, slice(None), cols)
            self.h[there] = (plus(self.h[there], self.rb[color, 0, n]) + plus(self.rb[color, 1, n], self.rb[color, 2, n])).astype(BF)
            return carry

        lax.fori_loop(0, 4, add, 0, unroll=True)
        for step in STEPS:
            self.copies.start("d", color, step)

    def far(self, color):
        for step in STEPS:
            self.copies.got("d", color, step)
        there = self.block(color, 0)
        there[...] = (plus(there[...], self.rb1[color, 0]) + plus(self.rb1[color, 1], self.rb1[color, 2])).astype(BF)

    def along_z(self):
        at = self.at
        row, k = iota((64, 48), 0), iota((64, 48), 1)
        select = ones_where(((row & 15) < 12) & (k == 12 * (row >> 4) + (row & 15))).astype(BF)
        self.zs[...] = nn(select, self.h[at.x, at.y]).astype(BF).reshape(4, 16, self.size)
        for dz in STEPS:
            self.copies.start("z", dz)
        self.zr[at.z] = self.zs[at.z]

    def along_core(self):
        at = self.at
        for dz in STEPS:
            self.copies.got("z", dz)
        total = plus(self.zr[0], self.zr[1]) + plus(self.zr[2], self.zr[3])
        low, high = total[0:8], jnp.concatenate([total[6:12], total[0:2]], axis=0)
        core = jnp.broadcast_to(at.c, (8, self.size))
        self.xs[...] = jnp.where(core == 0, high, low)
        for color in range(2):
            for step in STEPS:
                self.copies.sent("a", color, step)
                self.copies.sent("d", color, step)
        for dz in STEPS:
            self.copies.sent("z", dz)
        self.copies.start("x")
        self.out[:, at.half(at.c, self.size)] = jnp.where(core == 0, low, high)

    def end(self):
        self.copies.got("x")
        self.copies.sent("x")


class SmallReduce:
    SENDS = 10

    def __init__(self, at, small, out, scratch, semaphores):
        self.at, self.small, self.out = at, small, out
        self.sx, self.sy, self.sz, self.sc = scratch
        self.copies = c = Copies(semaphores)
        for d in STEPS:
            c.make(("sx", d), self.sx.at[at.x], self.sx.at[at.x], at.at(dx=d))
            c.make(("sy", d), self.sy.at[at.y], self.sy.at[at.y], at.at(dy=d))
            c.make(("sz", d), self.sz.at[at.z], self.sz.at[at.z], at.at(dz=d))
        c.make(("sc",), self.sc.at[at.c], self.sc.at[at.c], at.at(dc=1))

    def begin(self):
        self.sx[self.at.x] = self.small[...]
        for d in STEPS:
            self.copies.start("sx", d)

    def step(self, name, here, following, index):
        for d in STEPS:
            self.copies.got(name, d)
        following[index] = (here[0] + here[1]) + (here[2] + here[3])

    def along_y(self):
        self.step("sx", self.sx, self.sy, self.at.y)
        for d in STEPS:
            self.copies.start("sy", d)

    def along_z(self):
        self.step("sy", self.sy, self.sz, self.at.z)
        for d in STEPS:
            self.copies.start("sz", d)

    def along_core(self):
        self.step("sz", self.sz, self.sc, self.at.c)
        self.copies.start("sc")

    def end(self):
        self.copies.got("sc")
        for name in list(self.copies.made):
            self.copies.sent(*name)
        total = self.sc[0] + self.sc[1]

        self.sc[0] = total

        def own(entries, width):
            def part(n, sums):
                pick = (iota((128, 128), 0) + 128 * n == entries * self.at.me + iota((128, 128), 1)) & (iota((128, 128), 1) < entries)
                return sums + exact(self.sc[0, :, tiles(128 * n, 128)], ones_where(pick))

            return lax.fori_loop(0, width // 128, part, jnp.zeros((8, 128), F32))

        self.out[0:5, :] = own(14, CONV)[0:5]
        self.out[5:6, :] = own(12, INNER)[5:6]
        self.out[6:7, :] = own(6, D)[6:7]
        self.out[7:8, :] = total[7:8, 0:128]


def dma_pair(count):
    return [pltpu.SemaphoreType.DMA((count,)), pltpu.SemaphoreType.DMA((count,))]


def wide_scratch(width):
    size = width // 2
    return [
        pltpu.VMEM((4, 4, 48, size), BF),
        pltpu.VMEM((2, 3, 4, 48, size // 2), BF),
        pltpu.VMEM((2, 3, 48, size // 2), BF),
    ]


def narrow_scratch(width):
    size = width // 2
    return [
        pltpu.VMEM((4, 16, size), BF),
        pltpu.VMEM((4, 16, size), BF),
        pltpu.VMEM((8, size), F32),
    ]


def small_scratch():
    return [pltpu.VMEM((4, 8, CONV), F32)] * 3 + [pltpu.VMEM((2, 8, CONV), F32)]


WIDTHS = (Q, Q, Q, B)


def vm(count):
    return [pl.BlockSpec(memory_space=pltpu.VMEM)] * count


def shape(*dims, dtype=F32):
    return jax.ShapeDtypeStruct(dims, dtype)


def whole(width):
    return shape(4, 4, 48, width, dtype=BF)


LIMIT = 63 * 1024 * 1024


def scan_scratch():
    return [
        pltpu.VMEM((T, T), F32),
        pltpu.VMEM((T, 128), BF),
        pltpu.VMEM((T, 128), BF),
        pltpu.VMEM((HEADS, 1, T), F32),
        pltpu.VMEM((6, T, 128), F32),
        pltpu.VMEM((T + 8, 128), F32),
        pltpu.VMEM((T, 256), F32),
        pltpu.VMEM((T, 256), F32),
    ] + [pltpu.VMEM((T, 256), dtype) for dtype in (F32, F32, F32, BF, F32, F32, BF, F32, F32)]


def backward_scratch():
    return [
        pltpu.VMEM((T, 128), F32),
        pltpu.VMEM((T, 128), F32),
        pltpu.VMEM((D, T), BF),
        pltpu.VMEM((D, T), BF),
        pltpu.VMEM((T, INNER), BF),
        pltpu.VMEM((T, INNER), BF),
        pltpu.VMEM((T, USED), BF),
        pltpu.VMEM((T, INNER), F32),
        pltpu.VMEM((T, T), F32),
        pltpu.VMEM((T, 128), F32),
        pltpu.VMEM((T, 128), F32),
        pltpu.VMEM((16, 256), F32),
    ]


class Plan:
    def __init__(self, prefix, steps):
        self.prefix, self.steps = prefix, steps

    def __call__(self, name):
        for step in self.steps.get(self.prefix + name, ()):
            step()

    def at_chunk(self, j):
        for n in range(6):
            if self.prefix + "chunk%d" % n in self.steps:
                pl.when(j == n)(partial(self, "chunk%d" % n))


def first_terms(rb, heads, rows, cols, seg_row, scan, then):
    scores, step3, log3, log_t, masks, padded, act, slope, *work = scan
    prepare_scan(rb[:, STEP:USED], heads, step3, log3, log_t)
    for n in range(2):
        here = slice(128 * n, 128 * (n + 1))
        conv_forward(rb, here, rows, slice(INNER + 128 * n, INNER + 128 * (n + 1)), masks, act, here, slope)
    score_pass(act, cols, seg_row, scores)
    then("scores")


def run_forward(stream, wq, wb, heads, cols, seg_row, rows, skip, rb, values, gate, mixed, following, scan, scratch, then):
    scores, step3, log3, log_t, masks, padded, act, slope, *work = scan
    normed, gated, square, yn = scratch
    small_rows(wb, heads, rows, skip)
    then("rows")
    rms_normed(stream, rows[6:7, 0:D], normed)
    rb[...] = nn(normed[...], weight(wb, pl.ds(0, USED)))
    then("normed")
    first_terms(rb, heads, rows, cols, seg_row, scan, then)
    square[...] = jnp.zeros_like(square)

    def chunk(j, carry):
        here = tiles(j * 256, 256)
        values[:, here] = nn(normed[...], weight_chunk(wq, j, 2))
        gate[:, here] = nn(normed[...], weight_chunk(wq, j, 1))
        value_chunk(j, values, rows, masks, work[7])
        forward_chunk(j, rows, skip, gate, scores, step3, log3, log_t, mixed, gated, square, work)
        then.at_chunk(j)
        return carry

    lax.fori_loop(0, 6, chunk, 0)
    gate_norm(rows, gated, square, yn)
    then("yn")
    for n in range(2):
        there = slice(T * n, T * (n + 1))
        total = stream[:, there].astype(F32)
        for s in range(3):
            total += nt(yn[:, PART * s : PART * (s + 1)], wq[s, 2 * n : 2 * n + 2, :, :, 0:PART].reshape(T, PART))
        following[:, there] = total


def run_backward(grad, stream, normed, wq, wb, heads, cols, seg_row, rows, skip, rb, values, gate, mixed, gq, gb, small, finish, scan, scratch, ready, then):
    scores, step3, log3, log_t, masks, padded, act, slope, *work = scan
    sum_u, sum_d, gl_t, norm_t, dgate, dvalues, db, dyn, dscores, dlog, dstep, skip_sum = scratch

    def lower(at):
        gl[at, :] = grad[at, :].astype(BF)

    norm_t[...] = jnp.transpose(normed[...])
    gl = normed
    by_rows(lower)
    gl_t[...] = jnp.transpose(gl[...])
    for ref in (small, sum_u, sum_d, dscores, dlog, dstep, skip_sum):
        ref[...] = jnp.zeros_like(ref)

    def first(c, carry):
        first_backward(c, gl, wq, rows, gate, mixed, dyn, sum_u, sum_d)
        return carry

    lax.fori_loop(0, 6, first, 0)
    then("first")
    if not ready:
        first_terms(rb, heads, rows, cols, seg_row, scan, then)
    norm_pull(sum_u, sum_d)

    def chunk(j, carry):
        backward_chunk(j, rows, skip, gate, values, masks, padded, scores, step3, log3, log_t, mixed, dyn, sum_u, sum_d,
                       gl_t, norm_t, gq, small, dgate, dvalues, dscores, dlog, dstep, skip_sum, work)
        then.at_chunk(j)
        return carry

    lax.fori_loop(0, 6, chunk, 0)
    then("chunks")
    dact = work[0]
    scores_backward(act, cols, seg_row, dscores, dact)
    steps_backward(rb[:, STEP:USED], heads, dlog, dstep, db, small, skip_sum)
    then("steps")
    for n in range(2):
        here = slice(128 * n, 128 * (n + 1))
        conv_backward(rb, here, rows, slice(INNER + 128 * n, INNER + 128 * (n + 1)), masks, dact, slope, here, small, db, padded)
    put_product(gb, pl.ds(0, USED), norm_t, db[...])
    gb[:, :, :, USED:] = jnp.zeros((4, 4, 48, 128), BF)
    then("b_grad")
    normed_backward(dgate, dvalues, db, wq, wb, dyn)
    then("normed_back")
    stream_backward(dyn, stream, rows[6:7, 0:D], grad, small, finish)
    then("done")


def whole_kernel(shard_b, shard_q, tokens, cotangent, a_log, dt_bias, head_skip, segments, counts,
                 output, tokens_grad, in_grad, ob0, oq0, s0, ob1, oq1, s1, far_rb, far_values, far_gate, far_mixed,
                 wb0, wq0, wb1, wq1, gb1, gq1,
                 second, grad, rb, values, gate, mixed, rows0, rows1, skip0, skip1, small, normed, square, local_sem, heads, cols, seg_row, *scratch):
    places = iter(scratch)
    take = lambda n: [next(places) for _ in range(n)]
    scan, backward = take(17), take(12)
    dgate, dyn = backward[4], backward[7]
    forward = (normed, dyn, square, dgate)
    wide = [take(3) for _ in range(4)]
    narrow = [take(3) for _ in range(4)]
    sums_by_axis = take(4)
    semaphores = Semaphores(*take(2))
    at = Place()
    greet([at.at(dx=d) for d in STEPS] + [at.at(dy=d) for d in STEPS] + [at.at(dz=dz, dc=dc) for dz, dc in GROUP])

    parts = range(3)
    ab, *aq = groups = [GatherGroup(at, s, t, semaphores) for s, t in [(shard_b, wide[3][0])] + [(shard_q.at[n], wide[n][0]) for n in parts]]
    b0, x0, y0, z0, b1, x1, y1, z1 = planes = [
        GatherPlane(at, w, semaphores) for wb, wq in ((wb0, wq0), (wb1, wq1)) for w in [wb] + [wq.at[n] for n in parts]
    ]
    def sums_of(gb, gq, ob, oq):
        pairs = [(gq.at[n], oq.at[n]) for n in parts] + [(gb, ob)]
        return [Reduce(at, g, o, wide[n] + narrow[n], semaphores) for n, (g, o) in enumerate(pairs)]

    X1, Y1, Z1, B1 = sums1 = sums_of(gb1, gq1, ob1, oq1)
    X0, Y0, Z0, B0 = sums0 = sums_of(wb1, wq1, ob0, oq0)
    S1, S0 = [SmallReduce(at, *v, semaphores) for v in ((small, s1, sums_by_axis), (small, s0, sums_by_axis))]

    def two(step):
        return [partial(step, 0), partial(step, 1)]

    away, back = [], []
    for n, (near, far) in enumerate(((rb, far_rb), (values, far_values), (gate, far_gate), (mixed, far_mixed))):
        away.append(pltpu.make_async_copy(near, far, local_sem.at[n]))
        back.append(pltpu.make_async_copy(far, near, local_sem.at[4 + n]))

    steps = {
        "f0.rows": [y0.begin],
        "f0.normed": [z0.begin],
        "f0.scores": [away[0].start, x0.far, y0.near, x0.end],
        "f0.chunk0": [b1.begin, x1.begin, z0.near],
        "f0.chunk1": [y0.far, b1.near, y0.end],
        "f0.chunk2": [y1.begin, x1.near, b1.far],
        "f0.chunk3": [z0.far, z1.begin, z0.end],
        "f0.chunk4": [b1.end, y1.near],
        "f0.chunk5": [x1.far],
        "f0.yn": [each.start for each in away[1:]] + [z1.near],
        "f1.begin": [away[0].wait],
        "f1.rows": [y1.far],
        "f1.scores": [each.wait for each in away[1:]] + [x1.end, y1.end],
        "f1.chunk1": [z1.far],
        "f1.chunk3": [z1.end],
        "b1.first": [each.copies.finish for each in groups + planes],
        "b1.chunk1": [X1.begin],
        "b1.chunk2": two(X1.pair),
        "b1.chunk3": [Y1.begin],
        "b1.chunk4": two(X1.near) + two(Y1.pair),
        "b1.chunk5": [Z1.begin] + two(X1.far),
        "b1.chunks": [each.start for each in back[1:]],
        "b1.b_grad": [back[0].start, B1.begin],
        "b1.normed_back": two(Y1.near) + two(Z1.pair) + [X1.along_z],
        "b1.done": [each.wait for each in back] + two(Y1.far) + [X1.along_core, S1.begin],
        "b0.first": two(Z1.near) + [S1.along_y] + two(B1.pair) + [Y1.along_z, X1.end],
        "b0.chunk0": two(Z1.far) + two(B1.near) + [Y1.along_core, S1.along_z],
        "b0.chunk1": [X0.begin] + two(B1.far) + [Z1.along_z, Y1.end, S1.along_core],
        "b0.chunk2": two(X0.pair) + [Z1.along_core, B1.along_z, S1.end],
        "b0.chunk3": [Y0.begin, Z1.end, B1.along_core],
        "b0.chunk4": two(X0.near) + two(Y0.pair) + [B1.end],
        "b0.chunk5": [Z0.begin] + two(X0.far) + two(Y0.near) + [X0.along_z],
        "b0.b_grad": [B0.begin] + two(Z0.pair) + two(Y0.far),
        "b0.normed_back": two(B0.pair) + [Y0.along_z, X0.along_core],
        "b0.done": [S0.begin]
        + two(Z0.near)
        + two(B0.near)
        + [Y0.along_core, S0.along_y, X0.end]
        + two(Z0.far)
        + [Z0.along_z]
        + two(B0.far)
        + [B0.along_z, S0.along_z, Z0.along_core, B0.along_core, S0.along_core, Y0.end, Z0.end, B0.end, S0.end],
    }

    ab.begin()
    for each in aq:
        each.begin()
    heads[...] = jnp.zeros_like(heads)
    for l in range(2):
        for n, source in enumerate((a_log, dt_bias, head_skip)):
            heads[l, n : n + 1, 0:HEADS] = source[l : l + 1, :]
    slot_columns(segments, counts, cols, seg_row)
    conv_masks(cols, scan[4])
    scan[5][T:, :] = jnp.zeros((8, 128), F32)
    ab.end(wb0, wb1)
    b0.begin()
    aq[0].end(wq0.at[0], wq1.at[0])
    x0.begin()
    b0.near()
    x0.near()
    b0.far()
    for n in (1, 2):
        aq[n].end(wq0.at[n], wq1.at[n])
    b0.end()

    head0, head1 = heads.at[0], heads.at[1]
    run_forward(tokens, wq0, wb0, head0, cols, seg_row, rows0, skip0, rb, values, gate, mixed, second, scan, forward, Plan("f0.", steps))
    Plan("f1.", steps)("begin")
    run_forward(second, wq1, wb1, head1, cols, seg_row, rows1, skip1, rb, values, gate, mixed, grad, scan, forward, Plan("f1.", steps))

    def turn(at):
        live = cols[at, 7:8]
        output[at, :] = (grad[at, :] * live).astype(BF)
        grad[at, :] = cotangent[at, :].astype(F32) * live

    by_rows(turn)

    def keep(at, value):
        grad[at, :] = value

    run_backward(grad, second, normed, wq1, wb1, head1, cols, seg_row, rows1, skip1, rb, values, gate, mixed,
                 gq1, gb1, small, keep, scan, backward, True, Plan("b1.", steps))
    rms_normed(tokens, rows0[6:7, 0:D], normed)

    def give(at, value):
        tokens_grad[at, :] = value.astype(BF)

    run_backward(grad, tokens, normed, wq0, wb0, head0, cols, seg_row, rows0, skip0, rb, values, gate, mixed,
                 wq1, wb1, small, give, scan, backward, False, Plan("b0.", steps))
    for each in sums1 + sums0 + [S1, S0]:
        each.copies.finish()
    for l, (ob, oq) in enumerate(((ob0, oq0), (ob1, oq1))):
        for n in parts:
            for kind in (1, 2):
                start = INNER * (kind - 1) + PART * n
                in_grad[l, :, start : start + PART] = oq[n, 0:6, PART * kind : PART * (kind + 1)]
        in_grad[l, :, 2 * INNER :] = ob[0:6, 0 : STEP + HEADS]


SENDS = 4 * 7 + 8 * GatherPlane.SENDS + 8 * Reduce.SENDS + 2 * SmallReduce.SENDS


def two_blocks(shards, *rest):
    outs = (shape(8, B), shape(3, 8, Q), shape(8, 128))
    wb, wq = pltpu.VMEM((4, 4, 48, B), BF), pltpu.VMEM((3, 4, 4, 48, Q), BF)
    buffers = []
    for width in WIDTHS:
        buffers += wide_scratch(width)
    for width in WIDTHS:
        buffers += narrow_scratch(width)
    return pl.pallas_call(
        whole_kernel,
        out_shape=(shape(T, D, dtype=BF), shape(T, D, dtype=BF), shape(2, 6, 2 * INNER + STEP + HEADS)) + outs + outs + (shape(T, USED),) + (shape(T, INNER),) * 3,
        in_specs=vm(9),
        out_specs=tuple(vm(9)) + (pl.BlockSpec(memory_space=pl.ANY),) * 4,
        scratch_shapes=[wb, wq] * 3
        + [pltpu.VMEM((T, D), F32)] * 2
        + [pltpu.VMEM((T, USED), F32)]
        + [pltpu.VMEM((T, INNER), F32)] * 3
        + [pltpu.VMEM((8, CONV), F32)] * 2
        + [pltpu.VMEM((8, INNER), F32)] * 2
        + [pltpu.VMEM((8, CONV), F32)]
        + [pltpu.VMEM((T, D), BF), pltpu.VMEM((T, 128), F32), pltpu.SemaphoreType.DMA((8,))]
        + [pltpu.VMEM((2, 8, 128), F32), pltpu.VMEM((T, 128), F32), pltpu.VMEM((8, T), F32)]
        + scan_scratch()
        + backward_scratch()
        + buffers
        + small_scratch()
        + dma_pair(SENDS),
        compiler_params=pltpu.CompilerParams(collective_id=0, has_side_effects=True, vmem_limit_bytes=LIMIT),
        name="two_blocks",
    )(*shards, *rest)


def shards_of(norm_gain, in_weight, conv_weight, conv_bias, gate_gain, out_weight):
    taps = jnp.transpose(conv_weight, (0, 2, 1)).reshape(2, 56)
    small = jnp.concatenate([conv_bias, taps, gate_gain, norm_gain, jnp.zeros((2, 40), BF)], axis=1)
    tile = jnp.concatenate([small[:, None, :], jnp.zeros((2, 5, 128), BF)], axis=1)
    wide = jnp.concatenate([in_weight[:, :, INNER + INNER :], jnp.zeros((2, 6, SMALL - STEP - HEADS), BF), tile], axis=2)
    kinds = [jnp.transpose(out_weight, (0, 2, 1)), in_weight[:, :, :INNER], in_weight[:, :, INNER : 2 * INNER]]
    q = jnp.stack([v.reshape(12, 3, PART) for v in kinds], axis=2).reshape(12, 3, Q).transpose(1, 0, 2)
    return jnp.pad(wide.reshape(12, B), ((0, 4), (0, 0))), jnp.pad(q, ((0, 0), (0, 4), (0, 0)))


def local(tokens, cotangent, segments, counts, norm_gain, in_weight, conv_weight, conv_bias, a_log, dt_bias, skip, gate_gain, out_weight):
    shards = shards_of(norm_gain, in_weight, conv_weight, conv_bias, gate_gain, out_weight)
    output, tokens_grad, in_grad, _, oq0, s0, _, oq1, s1, *_ = two_blocks(
        shards, tokens, cotangent, a_log, dt_bias, skip, segments.reshape(1, T), counts.reshape(1, 1)
    )
    small = jnp.stack([s0, s1])
    outs = jnp.stack([oq0, oq1])[:, :, 0:6, 0:PART]
    return (
        output,
        tokens_grad,
        small[:, 6, 0:6],
        in_grad,
        jnp.transpose(small[:, 1:5, 0:14], (0, 2, 1)),
        small[:, 0, 0:14],
        small[:, 7, 0:24],
        small[:, 7, 32:56],
        small[:, 7, 64:88],
        small[:, 5, 0:12],
        jnp.transpose(outs.transpose(0, 2, 1, 3).reshape(2, 6, INNER), (0, 2, 1)),
    )


def solution(mesh):
    axis = P("fsdp")
    rows, second, third = P("fsdp", None), P(None, "fsdp"), P(None, None, "fsdp")
    middle = P(None, "fsdp", None)
    return jax.shard_map(
        local,
        mesh=mesh,
        in_specs=(rows, rows, axis, axis, second, middle, middle, second, P(), P(), P(), second, third),
        out_specs=(rows, rows, second, middle, middle, second, P(), P(), P(), second, third),
        check_vma=False,
    )
```
